32 devices in a mesh: dp: 8 (over z, x), mp: 4 (over y, core).
Axes of the slice: x: 2, y: 2, z: 4, core: 2. Of those that a mesh axis runs over, the one named last changes fastest.
Arguments:
- tokens: bfloat16 [8, 2048, 1024], P('dp', 'mp'), may hold values from -6 to 6
- cotangent: bfloat16 [8, 2048, 1024], P('dp', 'mp'), may hold values from -6 to 6
- w_qkv: float32 [3, 1024, 1024], P(None, 'dp', 'mp'), may hold values from -0.1875 to 0.1875
- w_out: float32 [1024, 1024], P('mp', 'dp'), may hold values from -3 to 3
- w_up: float32 [1024, 4096], P('dp', 'mp'), may hold values from -0.1875 to 0.1875
- w_down: float32 [4096, 1024], P('mp', 'dp'), may hold values from -0.09375 to 0.09375
- gain_attn: float32 [1024], replicated, may hold values from 0.5 to 1.5
- shift_attn: float32 [1024], replicated, may hold values from -1.5 to 1.5
- gain_ffn: float32 [1024], replicated, may hold values from 0.5 to 1.5
- shift_ffn: float32 [1024], replicated, may hold values from -1.5 to 1.5
- bias_up: float32 [4096], P('mp'), may hold values from -1.5 to 1.5
- bias_down: float32 [1024], replicated, may hold values from -1.5 to 1.5
- random_blocks: int32 [8, 16, 30, 3], P('dp', 'mp'), may hold values from 1 to 30
Outputs:
- out_tokens: bfloat16 [8, 2048, 1024], P('dp', 'mp')
- grad_tokens: float32 [8, 2048, 1024], P('dp', 'mp')
- new_qkv: float32 [3, 1024, 1024], P(None, 'dp', 'mp')
- qkv_rows: float32 [3, 1024], P(None, 'dp')
- qkv_cols: float32 [3, 1024], P(None, 'mp')
- new_out: float32 [1024, 1024], P('mp', 'dp')
- out_rows: float32 [1024], P('mp')
- out_cols: float32 [1024], P('dp')
- new_up: float32 [1024, 4096], P('dp', 'mp')
- up_rows: float32 [1024], P('dp')
- up_cols: float32 [4096], P('mp')
- new_down: float32 [4096, 1024], P('mp', 'dp')
- down_rows: float32 [4096], P('mp')
- down_cols: float32 [1024], P('dp')
- grad_gain_attn: float32 [1024], replicated
- grad_shift_attn: float32 [1024], replicated
- grad_gain_ffn: float32 [1024], replicated
- grad_shift_ffn: float32 [1024], replicated
- grad_bias_up: float32 [4096], P('mp')
- grad_bias_down: float32 [1024], replicated
The draws below stay inside these ranges and needn't reach their ends.
Inputs may be any that keep to these rules, and one draw needn't show every extreme that they name: `random_blocks`: every entry names a block of the same document other than its first and last; entries may repeat and may equal window blocks.
All inputs are finite; a program needn't handle non-finite values.
Results may differ from the reference program's by a relative error of at most 0.04.
Values may be sent and summed in bfloat16 or wider, within the bound.
No kernel may reach another device: no remote copies, remote signals or barrier semaphores. Data moves between devices by JAX's collectives and lax.ppermute only.
A program may use at most 192 MiB of HBM per device.

```python
import jax
import jax.numpy as jnp
from jax import lax

D = 1024
HEADS = 16
HD = 64
FF = 4096
BLOCK = 64
RAND_BLOCKS = 3
SEQ = 2048
DOCS = 8
NB = 32


def place_ends(entries, rng, low, top_value):
    longest = entries.shape.index(max(entries.shape))
    spots = []
    for shift in (0, 1):
        where = [jax.random.randint(jax.random.fold_in(rng, axis), (), 0, length) for axis, length in enumerate(entries.shape)]
        where[longest] = (where[longest] + shift) % entries.shape[longest]
        spots.append(tuple(where))
    return entries.at[spots[0]].set(low).at[spots[1]].set(top_value)


def levels(key, dims, split, low, high):
    loudness, own = 1.0, jax.random.fold_in(key, 6)
    for axis_at, shards_of in split:
        steps = jnp.exp(jax.random.uniform(jax.random.fold_in(own, axis_at), (shards_of,), jnp.float32, low / len(split), high / len(split)))
        loudness = loudness * jnp.repeat(steps, dims[axis_at] // shards_of).reshape([-1 if axis == axis_at else 1 for axis in range(len(dims))])
    return loudness


def centred(own_key, dims, scale, most, cuts=(), kind=jnp.bfloat16):
    gain = levels(own_key, dims, cuts, -0.22, 0.18) if cuts else 1.0
    drawn = jax.random.normal(own_key, dims, jnp.float32) * scale * gain
    return jnp.minimum(jnp.maximum(drawn, -most), most).astype(kind)


def setup_inputs(seed: int = 0) -> dict:
    splits = jax.random.split(jax.random.key(seed), 14)
    return {
        "tokens": centred(splits[0], (DOCS, SEQ, D), 1.0, 6.0, ((0, 8), (1, 4))),
        "cotangent": centred(splits[1], (DOCS, SEQ, D), 1.0, 6.0, ((0, 8), (1, 4))),
        "w_qkv": centred(splits[2], (3, D, D), D ** -0.5, 0.1875, ((1, 8), (2, 4)), jnp.float32),
        "w_out": centred(splits[3], (D, D), 4 ** -0.5, 3.0, ((0, 4), (1, 8)), jnp.float32),
        "w_up": centred(splits[4], (D, FF), D ** -0.5, 0.1875, ((0, 8), (1, 4)), jnp.float32),
        "w_down": centred(splits[5], (FF, D), FF ** -0.5, 0.09375, ((0, 4), (1, 8)), jnp.float32),
        "gain_attn": jnp.clip(1.0 + 0.1 * jax.random.normal(splits[6], (D,), jnp.float32), 0.5, 1.5),
        "shift_attn": centred(splits[7], (D,), 0.3, 1.5, (), jnp.float32),
        "gain_ffn": jnp.clip(1.0 + 0.1 * jax.random.normal(splits[8], (D,), jnp.float32), 0.5, 1.5),
        "shift_ffn": centred(splits[9], (D,), 0.3, 1.5, (), jnp.float32),
        "bias_up": centred(splits[10], (FF,), 0.3, 1.5, ((0, 4),), jnp.float32),
        "bias_down": centred(splits[11], (D,), 0.3, 1.5, (), jnp.float32),
        "random_blocks": place_ends(jax.random.randint(splits[12], (DOCS, HEADS, NB - 2, RAND_BLOCKS), 1, SEQ // BLOCK - 1), jax.random.fold_in(splits[12], 1), 1, (SEQ // BLOCK - 1) - 1).astype(jnp.int32),
    }


EPS_NORM = 1e-05
EPS_FACTOR = 1e-30
LEARN_RATE = 0.1
GELU_SCALE = 0.7978845608028654
PRECISE = lax.Precision.HIGHEST

@jax.custom_vjp
def low(v):
    return lax.optimization_barrier(v.astype(jnp.bfloat16)).astype(jnp.float32)

@jax.custom_vjp
def low_back(v):
    return v

def low_keep(v):
    return (low(v), None)

def low_pass(kept, grad):
    return (grad,)

def back_keep(v):
    return (v, None)

def back_low(kept, grad):
    return (low(grad),)
low.defvjp(low_keep, low_pass)
low_back.defvjp(back_keep, back_low)

def gelu_tanh(values):
    return 0.5 * values * (1.0 + jnp.tanh(GELU_SCALE * (values + 0.044715 * values * values * values)))

def block_table(random_rows, blocks_all):
    middle = jnp.arange(1, blocks_all - 1, dtype=jnp.int32)[:, None]
    fixed = jnp.concatenate([jnp.zeros_like(middle), middle - 1, middle, middle + 1, jnp.zeros_like(middle) + (blocks_all - 1)], axis=1)
    return jnp.concatenate([fixed, random_rows.astype(jnp.int32)], axis=1)

def layer_norm(values, norm_gain, norm_shift):
    center = lax.optimization_barrier(jnp.mean(values, axis=-1, keepdims=True))
    spread = values - center
    variance = lax.optimization_barrier(jnp.mean(spread * spread, axis=-1, keepdims=True))
    return spread * lax.rsqrt(variance + EPS_NORM) * norm_gain + norm_shift

def soft_rows(scores):
    highest = lax.optimization_barrier(jnp.max(scores, axis=-1, keepdims=True))
    expanded = jnp.exp(scores - highest)
    return expanded / lax.optimization_barrier(jnp.sum(expanded, axis=-1, keepdims=True))

def head_attention(queries, key_rows, value_rows, key_table):
    blocks_all = queries.shape[0] // BLOCK
    scaling = HD ** (-0.5)
    query_blocks = queries.reshape(blocks_all, BLOCK, HD)
    key_near = jnp.take(key_rows.reshape(blocks_all, BLOCK, HD), key_table, axis=0).reshape(blocks_all - 2, -1, HD)
    value_near = jnp.take(value_rows.reshape(blocks_all, BLOCK, HD), key_table, axis=0).reshape(blocks_all - 2, -1, HD)
    score_mid = low_back(jnp.einsum('nqe,nke->nqk', query_blocks[1:-1], key_near, precision=PRECISE) * scaling)
    prob_mid = low(soft_rows(score_mid))
    out_mid = jnp.einsum('nqk,nke->nqe', prob_mid, value_near, precision=PRECISE)
    query_ends = jnp.concatenate([query_blocks[0], query_blocks[-1]], axis=0)
    score_ends = low_back(jnp.einsum('qe,ke->qk', query_ends, key_rows, precision=PRECISE) * scaling)
    prob_ends = low(soft_rows(score_ends))
    out_ends = jnp.einsum('qk,ke->qe', prob_ends, value_rows, precision=PRECISE)
    joined = jnp.concatenate([out_ends[:BLOCK][None], out_mid, out_ends[BLOCK:][None]], axis=0)
    return joined.reshape(-1, HD)

def layer(inputs, w_qkv, w_out, w_up, w_down, gain_attn, shift_attn, gain_ffn, shift_ffn, bias_up, bias_down, tables):
    seq_rows = inputs.shape[0]
    normed = low(layer_norm(inputs, gain_attn, shift_attn))
    project = low_back(low(jnp.einsum('ld,cde->cle', normed, low(w_qkv), precision=PRECISE)))
    heads_split = project.reshape(3, seq_rows, HEADS, HD).transpose(0, 2, 1, 3)
    attend = jax.checkpoint(head_attention)
    attended = lax.map(lambda members: attend(*members), (heads_split[0], heads_split[1], heads_split[2], tables))
    heads_out = low_back(low(attended.transpose(1, 0, 2).reshape(seq_rows, HEADS * HD)))
    branch = low_back(jnp.dot(heads_out, low(w_out), precision=PRECISE))
    middle = inputs + branch
    normed_two = low(layer_norm(middle, gain_ffn, shift_ffn))
    hidden = low_back(jnp.dot(normed_two, low(w_up), precision=PRECISE) + bias_up)
    active = low(gelu_tanh(hidden))
    return middle + jnp.dot(active, low(w_down), precision=PRECISE) + bias_down

def adafactor(weight, gradient):
    squared = gradient * gradient
    row_mean = lax.optimization_barrier(jnp.mean(squared, axis=-1)) + EPS_FACTOR
    col_mean = lax.optimization_barrier(jnp.mean(squared, axis=-2)) + EPS_FACTOR
    whole = lax.optimization_barrier(jnp.mean(squared, axis=(-2, -1))) + EPS_FACTOR
    row_factor = row_mean / whole[..., None]
    col_factor = col_mean / whole[..., None]
    update = gradient * lax.rsqrt(row_factor[..., :, None] * col_factor[..., None, :] * whole[..., None, None])
    return (weight - LEARN_RATE * update, row_factor, col_factor)

def reference(tokens, cotangent, w_qkv, w_out, w_up, w_down, gain_attn, shift_attn, gain_ffn, shift_ffn, bias_up, bias_down, random_blocks):
    blocks_all = SEQ // BLOCK
    params = (w_qkv, w_out, w_up, w_down, gain_attn, shift_attn, gain_ffn, shift_ffn, bias_up, bias_down)

    def one_document(summed, members):
        doc_tokens, doc_cotangent, doc_random = members
        tables = jax.vmap(lambda random_rows: block_table(random_rows, blocks_all))(doc_random)

        def forward(inputs, *weights):
            return layer(inputs, *weights, tables)
        result, pullback = jax.vjp(forward, doc_tokens.astype(jnp.float32), *params)
        gradients = pullback(doc_cotangent.astype(jnp.float32))
        summed = tuple((earlier + latest for earlier, latest in zip(summed, gradients[1:])))
        return (summed, (result.astype(jnp.bfloat16), gradients[0]))
    initial = tuple((jnp.zeros_like(member) for member in params))
    summed, outputs = lax.scan(one_document, initial, (tokens, cotangent, random_blocks))
    new_qkv, qkv_rows, qkv_cols = adafactor(w_qkv, summed[0])
    new_out, out_rows, out_cols = adafactor(w_out, summed[1])
    new_up, up_rows, up_cols = adafactor(w_up, summed[2])
    new_down, down_rows, down_cols = adafactor(w_down, summed[3])
    return (outputs[0], outputs[1], new_qkv, qkv_rows, qkv_cols, new_out, out_rows, out_cols, new_up, up_rows, up_cols, new_down, down_rows, down_cols, summed[4], summed[5], summed[6], summed[7], summed[8], summed[9])
```

```python
import functools

import jax
import jax.numpy as jnp
from jax import lax
from jax.experimental import pallas as pl
from jax.experimental.pallas import tpu as pltpu
from jax.sharding import PartitionSpec as P

BLOCK = 64
EPS_NORM = 1e-05
EPS_FACTOR = 1e-30
LEARN_RATE = 0.1
GELU_SCALE = 0.7978845608028654
GELU_CUBE = 0.044715
F32 = jnp.float32
BF16 = jnp.bfloat16
NN = (((1,), (0,)), ((), ()))
NT = (((1,), (1,)), ((), ()))
TN = (((0,), (0,)), ((), ()))
VMEM_LIMIT = 40 << 20
CHUNKS = 1


def dot(left, right, form):
    return lax.dot_general(left, right, form, preferred_element_type=F32)


def swap(value, bit, size, axis="mp"):
    return lax.ppermute(value, axis, [(i, i ^ bit) for i in range(size)])


def gather_pieces(piece, size):
    if size != 4:
        whole = lax.all_gather(piece, "mp", axis=0, tiled=True)
        return [whole]
    near = swap(piece, 1, size)
    far = swap(piece, 2, size)
    return [piece, near, far, swap(far, 1, size)]


def scatter_sum(partial, size):
    low = partial.astype(BF16)
    rows = low.shape[0] // size
    if size != 4:
        return lax.psum_scatter(low, "mp", scatter_dimension=0, tiled=True).astype(F32)
    part = [low[n * rows : (n + 1) * rows] for n in range(4)]
    got = swap(jnp.concatenate([part[1], part[3]], axis=0), 1, size)
    own = partial[:rows] + got[:rows].astype(F32)
    other = (partial[2 * rows : 3 * rows] + got[rows:].astype(F32)).astype(BF16)
    return own + swap(other, 2, size).astype(F32)


def butterfly(value, axis, size):
    bit = 1
    while bit < size:
        value = value + swap(value, bit, size, axis)
        bit *= 2
    return value


def stack_heads(block, heads, head_dim):
    if heads == 1:
        return block
    owner = lax.broadcasted_iota(jnp.int32, block.shape, 1) // head_dim
    zero = jnp.zeros_like(block)
    return jnp.concatenate([jnp.where(owner == h, block, zero) for h in range(heads)], axis=0)


def unstack_heads(stacked, heads, head_dim):
    if heads == 1:
        return stacked
    rows = stacked.shape[0] // heads
    owner = lax.broadcasted_iota(jnp.int32, (rows, stacked.shape[1]), 1) // head_dim
    result = stacked[:rows]
    for h in range(1, heads):
        result = jnp.where(owner >= h, stacked[h * rows : (h + 1) * rows], result)
    return result


def block_rows(place):
    return pl.ds(pl.multiple_of(place * BLOCK, BLOCK), BLOCK)


def near_rows(ref, fixed, drawn, heads, head_dim):
    parts = [ref[block_rows(place), :] for place in fixed]
    for places in drawn:
        block = ref[block_rows(places[0]), :]
        if heads > 1:
            owner = lax.broadcasted_iota(jnp.int32, block.shape, 1) // head_dim
            for h in range(1, heads):
                block = jnp.where(owner >= h, ref[block_rows(places[h]), :], block)
        parts.append(block)
    return jnp.concatenate(parts, axis=0)


def probabilities(keys, queries):
    scores = dot(keys, queries, NT)
    expanded = jnp.exp(scores - jnp.max(scores, axis=0, keepdims=True))
    return expanded * (1.0 / jnp.sum(expanded, axis=0, keepdims=True))


def scale_low(block, scaling):
    return (block.astype(F32) * scaling).astype(BF16)


def table_of(random_ref, place, step, heads, draws):
    group = pl.program_id(0)
    fixed = [place(0), place(step), place(step + 1), place(step + 2), place(-1)]
    drawn = [
        [place(random_ref[group * heads + h, step * draws + j]) for h in range(heads)]
        for j in range(draws)
    ]
    return fixed, drawn


def placer(index_ref, blocks_all, pieces):
    per_piece = blocks_all // pieces

    def place(block):
        if isinstance(block, int):
            block = jnp.int32(block % blocks_all)
        if pieces == 1:
            return block
        return ((block // per_piece) ^ index_ref[0]) * per_piece + block % per_piece

    return place


def forward_kernel(heads, head_dim, draws, pieces, unroll, random_ref, index_ref, q_ref, k_ref, v_ref, o_ref):
    blocks_all = q_ref.shape[0] // BLOCK
    scaling = head_dim**-0.5
    place = placer(index_ref, blocks_all, pieces)

    def attend(queries, keys, values):
        stacked = stack_heads(scale_low(queries, scaling), heads, head_dim)
        probs = probabilities(keys, stacked).astype(BF16)
        return unstack_heads(dot(probs, values, TN), heads, head_dim).astype(BF16)

    def middle(step, carry):
        fixed, drawn = table_of(random_ref, place, step, heads, draws)
        keys = near_rows(k_ref, fixed, drawn, heads, head_dim)
        values = near_rows(v_ref, fixed, drawn, heads, head_dim)
        at = block_rows(fixed[2])
        o_ref[at, :] = attend(q_ref[at, :], keys, values)
        return carry

    lax.fori_loop(0, blocks_all - 2, middle, 0, unroll=unroll)
    for end in (0, -1):
        at = block_rows(place(end))
        o_ref[at, :] = attend(q_ref[at, :], k_ref[...], v_ref[...])


def backward_kernel(
    heads,
    head_dim,
    draws,
    pieces,
    unroll,
    random_ref,
    index_ref,
    q_ref,
    k_ref,
    v_ref,
    g_ref,
    dq_ref,
    dk_ref,
    dv_ref,
    k_near,
    v_near,
    k_drawn,
    v_drawn,
    k_ends,
    v_ends,
):
    blocks_all = q_ref.shape[0] // BLOCK
    scaling = head_dim**-0.5
    place = placer(index_ref, blocks_all, pieces)
    owner = lax.broadcasted_iota(jnp.int32, (BLOCK, q_ref.shape[1]), 1) // head_dim
    for ref in (k_drawn, v_drawn, k_ends, v_ends):
        ref[...] = jnp.zeros_like(ref)

    def back(queries, grads, keys, values):
        q_stack = stack_heads(scale_low(queries, scaling), heads, head_dim)
        g_stack = stack_heads(grads, heads, head_dim)
        probs = probabilities(keys, q_stack)
        grad_probs = dot(values, g_stack, NT)
        center = jnp.sum(probs * grad_probs, axis=0, keepdims=True)
        grad_scores = (probs * (grad_probs - center)).astype(BF16)
        grad_keys = dot(grad_scores, q_stack, NN)
        grad_values = dot(probs.astype(BF16), g_stack, NN)
        grad_queries = unstack_heads(dot(grad_scores, keys, TN), heads, head_dim) * scaling
        return grad_queries.astype(BF16), grad_keys, grad_values

    for number, end in enumerate((0, -1)):
        at = block_rows(place(end))
        dq, dk, dv = back(q_ref[at, :], g_ref[at, :], k_ref[...], v_ref[...])
        dq_ref[at, :] = dq
        if number == 0:
            k_near[...] = dk
            v_near[...] = dv
        else:
            k_near[...] += dk
            v_near[...] += dv

    def middle(step, carry):
        fixed, drawn = table_of(random_ref, place, step, heads, draws)
        keys = near_rows(k_ref, fixed, drawn, heads, head_dim)
        values = near_rows(v_ref, fixed, drawn, heads, head_dim)
        at = block_rows(fixed[2])
        dq, dk, dv = back(q_ref[at, :], g_ref[at, :], keys, values)
        dq_ref[at, :] = dq
        for part, near, far, ends in ((dk, k_near, k_drawn, k_ends), (dv, v_near, v_drawn, v_ends)):
            ends[0:BLOCK, :] += part[0:BLOCK]
            ends[BLOCK:, :] += part[4 * BLOCK : 5 * BLOCK]
            if pieces == 1:
                window = pl.ds(pl.multiple_of(step * BLOCK, BLOCK), 3 * BLOCK)
                near[window, :] += part[BLOCK : 4 * BLOCK]
            else:
                for n in range(1, 4):
                    near[block_rows(fixed[n]), :] += part[n * BLOCK : (n + 1) * BLOCK]
            for j in range(draws):
                block = part[(5 + j) * BLOCK : (6 + j) * BLOCK]
                for h in range(heads):
                    kept = block if heads == 1 else jnp.where(owner == h, block, 0.0)
                    far[block_rows(drawn[j][h]), :] += kept
        return carry

    lax.fori_loop(0, blocks_all - 2, middle, 0, unroll=unroll)
    for near, far, ends, out in ((k_near, k_drawn, k_ends, dk_ref), (v_near, v_drawn, v_ends, dv_ref)):
        near[block_rows(place(0)), :] += ends[0:BLOCK, :]
        near[block_rows(place(-1)), :] += ends[BLOCK:, :]
        out[...] = (near[...] + far[...]).astype(BF16)


def attention_call(kernel, unroll, project, grads, random_rows, index, pieces):
    seq_rows = project.shape[0]
    columns = project.shape[1] // 3
    local_heads, _, draws = random_rows.shape
    head_dim = columns // local_heads
    width = min(128, columns)
    groups = columns // width

    narrow = width < 128
    if narrow:
        operands = [project[:, n * columns : (n + 1) * columns] for n in range(3)]
    else:
        operands = [project] * 3

    def spec(part):
        first = 0 if narrow else part * groups
        return pl.BlockSpec((seq_rows, width), lambda g, *refs: (0, first + g))

    result = jax.ShapeDtypeStruct((seq_rows, columns), BF16)
    backward = grads is not None
    total = pltpu.VMEM((seq_rows, width), F32)
    ends = pltpu.VMEM((2 * BLOCK, width), F32)
    return pl.pallas_call(
        functools.partial(kernel, width // head_dim, head_dim, draws, pieces, unroll),
        grid_spec=pltpu.PrefetchScalarGridSpec(
            num_scalar_prefetch=2,
            grid=(groups,),
            in_specs=[spec(0), spec(1), spec(2)] + [spec(0)] * backward,
            out_specs=[spec(0)] * (3 if backward else 1),
            scratch_shapes=[total] * 4 + [ends] * 2 if backward else [],
        ),
        out_shape=[result] * (3 if backward else 1),
        compiler_params=pltpu.CompilerParams(vmem_limit_bytes=VMEM_LIMIT),
    )(
        random_rows.reshape(local_heads, -1),
        index,
        *operands,
        *([grads] if backward else []),
    )


def norm_forward(values, norm_gain, norm_shift):
    center = jnp.mean(values, axis=1, keepdims=True)
    spread = values - center
    variance = jnp.mean(spread * spread, axis=1, keepdims=True)
    inverse = lax.rsqrt(variance + EPS_NORM)
    normal = spread * inverse
    return ((normal * norm_gain + norm_shift).astype(BF16), normal, inverse)


def norm_backward(grad_norm, norm_gain, normal, inverse):
    scaled = grad_norm * norm_gain
    mean_plain = jnp.mean(scaled, axis=1, keepdims=True)
    mean_normal = jnp.mean(scaled * normal, axis=1, keepdims=True)
    grad_values = inverse * (scaled - mean_plain - normal * mean_normal)
    return (grad_values, jnp.sum(grad_norm * normal, axis=0), jnp.sum(grad_norm, axis=0))


def gelu_parts(values):
    square = values * values
    curve = jnp.tanh(GELU_SCALE * values * (1.0 + GELU_CUBE * square))
    half = 0.5 * (1.0 + curve)
    slope = half + 0.5 * values * (1.0 - curve * curve) * (
        GELU_SCALE * (1.0 + 3.0 * GELU_CUBE * square)
    )
    return values * half, slope


def rows_of(arrays, first, count):
    return jnp.concatenate([a[first : first + count] for a in arrays], axis=0)


def body(
    dp_size,
    mp_size,
    tokens,
    cotangent,
    w_qkv,
    w_out,
    w_up,
    w_down,
    gain_attn,
    shift_attn,
    gain_ffn,
    shift_ffn,
    bias_up,
    bias_down,
    random_blocks,
):
    paired = mp_size == 4
    outer = mp_size // 2
    index = lax.axis_index("mp").astype(jnp.int32).reshape(1)
    model = w_qkv.shape[1] * dp_size
    shard = w_qkv.shape[1]
    hidden = w_up.shape[1]
    attn = w_out.shape[0]
    lines = [[core + 2 * n for n in range(outer)] for core in range(2)]

    def to_low(value):
        return value.astype(BF16)

    qkv_low = lax.all_gather(
        to_low(w_qkv).transpose(1, 0, 2).reshape(shard, 3 * attn), "dp", axis=0, tiled=True
    )
    rest_low = lax.all_gather(
        jnp.concatenate([to_low(w_up), to_low(w_out).T, to_low(w_down).T], axis=1),
        "dp",
        axis=0,
        tiled=True,
    )
    up_low = rest_low[:, :hidden]
    out_low = rest_low[:, hidden : hidden + attn]
    down_low = rest_low[:, hidden + attn :]

    inputs = tokens[0].astype(F32)
    own_rows = inputs.shape[0]
    normed_low, normal_one, inverse_one = norm_forward(inputs, gain_attn, shift_attn)
    normed_full = jnp.concatenate(gather_pieces(normed_low, mp_size), axis=0)
    seq_rows = normed_full.shape[0]
    pieces = mp_size if paired else 1
    project = dot(normed_full, qkv_low, NN).astype(BF16)
    [heads_out] = attention_call(
        forward_kernel, 5, project, None, random_blocks[0], index, pieces
    )

    if paired:
        near_rows_count = seq_rows // 2
        outs = [heads_out[:near_rows_count], swap(heads_out[near_rows_count:], 2, mp_size)]
        out_parts = [out_low, swap(out_low, 2, mp_size)]
    else:
        moved = lax.all_to_all(
            heads_out, "mp", 0, 1, axis_index_groups=lines, tiled=True
        )
        outs = [moved]
        out_parts = [lax.all_gather(out_low, "mp", axis=1, axis_index_groups=lines, tiled=True)]
        core = lax.axis_index("mp") % 2

    def pair_order(value):
        if paired:
            return value
        half = value.shape[0] // 2
        return jnp.where(core == 0, value, jnp.roll(value, half, axis=0))

    outs = [pair_order(o) for o in outs]
    branch_pair = sum(dot(o, w, NT) for o, w in zip(outs, out_parts))
    branch = branch_pair[:own_rows] + swap(
        branch_pair[own_rows:].astype(BF16), 1, mp_size
    ).astype(F32)
    middle = inputs + branch
    second_low, normal_two, inverse_two = norm_forward(middle, gain_ffn, shift_ffn)
    second_full = jnp.concatenate(gather_pieces(second_low, mp_size), axis=0)
    grad_top = cotangent[0]
    grad_top_full = jnp.concatenate(gather_pieces(grad_top, mp_size), axis=0)
    active, slope = gelu_parts(dot(second_full, up_low, NN) + bias_up)
    active_low = active.astype(BF16)
    grad_hidden = (dot(grad_top_full, down_low, NN) * slope).astype(BF16)
    grad_second = scatter_sum(dot(grad_hidden, up_low, NT), mp_size)
    grad_bias_up = jnp.sum(grad_hidden.astype(F32), axis=0)
    grad_up_w = dot(second_full, grad_hidden, TN)
    grad_down_w = dot(grad_top_full, active_low, TN)

    grad_middle_norm, grad_gain_ffn, grad_shift_ffn = norm_backward(
        grad_second, gain_ffn, normal_two, inverse_two
    )
    grad_top_float = grad_top.astype(F32)
    grad_middle = grad_top_float + grad_middle_norm
    grad_bias_down = jnp.sum(grad_top_float, axis=0)
    grad_branch = grad_middle.astype(BF16)
    grad_pair = jnp.concatenate([grad_branch, swap(grad_branch, 1, mp_size)], axis=0)
    if paired:
        grad_heads = jnp.concatenate(
            [
                dot(grad_pair, out_parts[0], NN).astype(BF16),
                swap(dot(grad_pair, out_parts[1], NN).astype(BF16), 2, mp_size),
            ],
            axis=0,
        )
    else:
        moved = pair_order(dot(grad_pair, out_parts[0], NN).astype(BF16))
        grad_heads = lax.all_to_all(moved, "mp", 1, 0, axis_index_groups=lines, tiled=True)
    dq, dk, dv = attention_call(
        backward_kernel, 3, project, grad_heads, random_blocks[0], index, pieces
    )
    grad_project = jnp.concatenate([dq, dk, dv], axis=1)
    grad_qkv_w = dot(normed_full, grad_project, TN)
    grad_out_parts = [dot(grad_pair, o, TN).astype(BF16) for o in outs]
    if paired:
        grad_out_w = (
            grad_out_parts[0].astype(F32) + swap(grad_out_parts[1], 2, mp_size).astype(F32)
        ).astype(BF16)
    else:
        grad_out_w = lax.psum_scatter(
            grad_out_parts[0], "mp", scatter_dimension=1, axis_index_groups=lines, tiled=True
        )

    ffn_out = scatter_sum(dot(active_low, down_low, NT), mp_size)
    out_tokens = (middle + ffn_out + bias_down).astype(BF16)

    grad_normed = scatter_sum(dot(grad_project, qkv_low, NT), mp_size)
    grad_input_norm, grad_gain_attn, grad_shift_attn = norm_backward(
        grad_normed, gain_attn, normal_one, inverse_one
    )
    grad_tokens = (grad_middle + grad_input_norm)[None]

    def shard_sum(value):
        return lax.psum_scatter(
            value.astype(BF16), "dp", scatter_dimension=0, tiled=True
        ).astype(F32)

    ffn_shard = shard_sum(jnp.concatenate([grad_up_w.astype(BF16), grad_down_w.astype(BF16)], axis=1))
    attn_shard = shard_sum(jnp.concatenate([grad_qkv_w.astype(BF16), grad_out_w], axis=1))
    shards = [attn_shard[:, n * attn : (n + 1) * attn] for n in range(4)] + [
        ffn_shard[:, :hidden],
        ffn_shard[:, hidden:],
    ]
    squares = [g * g for g in shards]
    token_grads = [grad_gain_attn, grad_shift_attn, grad_gain_ffn, grad_shift_ffn, grad_bias_down]
    mp_sums = butterfly(
        jnp.concatenate([jnp.sum(s, axis=1) for s in squares] + token_grads), "mp", mp_size
    )
    model_sums = [mp_sums[n * shard : (n + 1) * shard] for n in range(6)]
    totals = jnp.stack([jnp.sum(s) for s in model_sums])
    local_sums = [jnp.sum(s, axis=0) for s in squares]
    dp_sums = butterfly(
        jnp.concatenate(
            local_sums
            + [mp_sums[6 * shard :], grad_bias_up, jnp.pad(totals, (0, 128 - totals.shape[0]))]
        ),
        "dp",
        dp_size,
    )
    cuts = []
    start = 0
    for length in [attn] * 4 + [hidden] * 2 + [model] * 5 + [hidden, 6]:
        cuts.append(dp_sums[start : start + length])
        start += length
    totals = cuts[12]

    def factored(gradient, model_sum, other_sum, whole_sum, other_total):
        model_mean = model_sum / other_total + EPS_FACTOR
        other_mean = other_sum / model + EPS_FACTOR
        whole = whole_sum / (model * other_total) + EPS_FACTOR
        model_factor = model_mean / whole
        other_factor = other_mean / whole
        update = gradient * lax.rsqrt(model_factor[:, None] * other_factor[None, :] * whole)
        return (LEARN_RATE * update, model_factor, other_factor)

    attn_total = attn * mp_size
    hidden_total = hidden * mp_size
    wide = [attn_total] * 4 + [hidden_total] * 2
    steps = [
        factored(shards[n], model_sums[n], cuts[n], totals[n], wide[n]) for n in range(6)
    ]
    new_qkv = w_qkv - jnp.stack([steps[n][0] for n in range(3)])
    return (
        out_tokens[None],
        grad_tokens,
        new_qkv,
        jnp.stack([steps[n][1] for n in range(3)]),
        jnp.stack([steps[n][2] for n in range(3)]),
        w_out - steps[3][0].T,
        steps[3][2],
        steps[3][1],
        w_up - steps[4][0],
        steps[4][1],
        steps[4][2],
        w_down - steps[5][0].T,
        steps[5][2],
        steps[5][1],
        cuts[6],
        cuts[7],
        cuts[8],
        cuts[9],
        cuts[11],
        cuts[10],
    )


def solution(mesh):
    placed = (
        P("dp", "mp", None),
        P("dp", "mp", None),
        P(None, "dp", "mp"),
        P("mp", "dp"),
        P("dp", "mp"),
        P("mp", "dp"),
        P(),
        P(),
        P(),
        P(),
        P("mp"),
        P(),
        P("dp", "mp", None, None),
    )
    return jax.shard_map(
        functools.partial(body, mesh.shape["dp"], mesh.shape["mp"]),
        mesh=mesh,
        in_specs=placed,
        out_specs=(
            P("dp", "mp", None),
            P("dp", "mp", None),
            P(None, "dp", "mp"),
            P(None, "dp"),
            P(None, "mp"),
            P("mp", "dp"),
            P("mp"),
            P("dp"),
            P("dp", "mp"),
            P("dp"),
            P("mp"),
            P("mp", "dp"),
            P("mp"),
            P("dp"),
            P(),
            P(),
            P(),
            P(),
            P("mp"),
            P(),
        ),
        check_vma=False,
    )
```

```python
import functools

import jax
import jax.numpy as jnp
from jax import lax
from jax.experimental import pallas as pl
from jax.experimental.pallas import tpu as pltpu
from jax.sharding import PartitionSpec as P

BLOCK = 64
EPS_NORM = 1e-05
EPS_FACTOR = 1e-30
LEARN_RATE = 0.1
GELU_SCALE = 0.7978845608028654
GELU_CUBE = 0.044715
F32 = jnp.float32
BF16 = jnp.bfloat16
NN = (((1,), (0,)), ((), ()))
NT = (((1,), (1,)), ((), ()))
TN = (((0,), (0,)), ((), ()))
VMEM_LIMIT = 24 << 20


def cost(microseconds):
    return pl.CostEstimate(flops=int(microseconds * 1.15e9), bytes_accessed=1 << 10, transcendentals=0)


CHEAP = cost(0.01)


def dot(left, right, form):
    return lax.dot_general(left, right, form, preferred_element_type=F32)


def swap(value, bit, size, axis="mp"):
    return lax.ppermute(value, axis, [(i, i ^ bit) for i in range(size)])


def after(value, *others):
    return lax.optimization_barrier((value, *others))[0]


def shifted(value, by, size):
    return lax.ppermute(value, "dp", [(i, (i + by) % size) for i in range(size)])


def scatter_model(partial, size):
    if size != 8:
        return lax.psum_scatter(partial, "dp", scatter_dimension=0, tiled=True).astype(F32)
    kept, sent = scatter_model_split(partial, size)
    return sum(p.astype(F32) for p in scatter_model_end(kept, swap(sent, 1, size, "dp"), size))


def scatter_model_split(partial, size):
    mine = lax.axis_index("dp")
    rows = partial.shape[0] // size
    columns = partial.shape[1]
    side = mine % 2
    split = partial.reshape(4, 2, rows, columns)

    def of_side(which):
        return lax.dynamic_slice(split, (0, which, 0, 0), (4, 1, rows, columns)).reshape(
            4, rows, columns
        )

    return of_side(side), of_side(1 - side)


def scatter_model_end(kept, got, size):
    level = lax.axis_index("dp") // 2
    rows, columns = kept.shape[1:]
    pair = (kept.astype(F32) + got.astype(F32)).astype(BF16)

    def of_level(which):
        return lax.dynamic_slice(pair, (which, 0, 0), (1, rows, columns))[0]

    parts = [shifted(of_level((level + n) % 4), 2 * n, size) for n in (1, 3, 2)]
    return [of_level(level)] + parts


def assemble_kernel(count, place_ref, *refs):
    rows = refs[0].shape[0]
    for n in range(count):
        at = pl.ds(pl.multiple_of(place_ref[n] * rows, rows), rows)
        refs[count][at, :] = refs[n][...]


def assemble(parts, places):
    count = len(parts)
    rows, columns = parts[0].shape
    tile = min(512, columns)
    return pl.pallas_call(
        functools.partial(assemble_kernel, count),
        grid=(columns // tile,),
        in_specs=[pl.BlockSpec(memory_space=pltpu.SMEM)]
        + [pl.BlockSpec((rows, tile), lambda i: (0, i))] * count,
        out_specs=pl.BlockSpec((count * rows, tile), lambda i: (0, i)),
        out_shape=jax.ShapeDtypeStruct((count * rows, columns), parts[0].dtype),
        compiler_params=pltpu.CompilerParams(vmem_limit_bytes=VMEM_LIMIT),
        cost_estimate=CHEAP,
    )(jnp.stack(places).astype(jnp.int32), *parts)


def butterfly(value, axis, size):
    bit = 1
    while bit < size:
        value = value + swap(value, bit, size, axis)
        bit *= 2
    return value


def stack_heads(block, heads, head_dim):
    if heads == 1:
        return block
    owner = lax.broadcasted_iota(jnp.int32, block.shape, 1) // head_dim
    zero = jnp.zeros_like(block)
    return jnp.concatenate([jnp.where(owner == h, block, zero) for h in range(heads)], axis=0)


def unstack_heads(stacked, heads, head_dim):
    if heads == 1:
        return stacked
    rows = stacked.shape[0] // heads
    owner = lax.broadcasted_iota(jnp.int32, (rows, stacked.shape[1]), 1) // head_dim
    result = stacked[:rows]
    for h in range(1, heads):
        result = jnp.where(owner >= h, stacked[h * rows : (h + 1) * rows], result)
    return result


def block_rows(place):
    return pl.ds(pl.multiple_of(place * BLOCK, BLOCK), BLOCK)


def near_rows(ref, fixed, drawn, heads, head_dim):
    parts = [ref[block_rows(place), :] for place in fixed]
    for places in drawn:
        block = ref[block_rows(places[0]), :]
        if heads > 1:
            owner = lax.broadcasted_iota(jnp.int32, block.shape, 1) // head_dim
            for h in range(1, heads):
                block = jnp.where(owner >= h, ref[block_rows(places[h]), :], block)
        parts.append(block)
    return jnp.concatenate(parts, axis=0)


def probabilities(keys, queries):
    scores = dot(keys, queries, NT)
    expanded = jnp.exp(scores - jnp.max(scores, axis=0, keepdims=True))
    return expanded * (1.0 / jnp.sum(expanded, axis=0, keepdims=True))


def scale_low(block, scaling):
    return (block.astype(F32) * scaling).astype(BF16)


def table_of(random_ref, place, step, first, heads, draws):
    fixed = [place(0), place(step), place(step + 1), place(step + 2), place(-1)]
    drawn = [
        [place(random_ref[first + h, step * draws + j]) for h in range(heads)]
        for j in range(draws)
    ]
    return fixed, drawn


def placer(index_ref, blocks_all, pieces):
    per_piece = blocks_all // pieces

    def place(block):
        if isinstance(block, int):
            block = jnp.int32(block % blocks_all)
        if pieces == 1:
            return block
        return ((block // per_piece) ^ index_ref[0]) * per_piece + block % per_piece

    return place


def forward_kernel(first, heads, head_dim, draws, pieces, unroll, random_ref, index_ref, q_ref, k_ref, v_ref, o_ref):
    blocks_all = q_ref.shape[0] // BLOCK
    scaling = head_dim**-0.5
    place = placer(index_ref, blocks_all, pieces)

    def attend(queries, keys, values):
        stacked = stack_heads(scale_low(queries, scaling), heads, head_dim)
        probs = probabilities(keys, stacked).astype(BF16)
        return unstack_heads(dot(probs, values, TN), heads, head_dim).astype(BF16)

    def middle(step, carry):
        fixed, drawn = table_of(random_ref, place, step, first, heads, draws)
        keys = near_rows(k_ref, fixed, drawn, heads, head_dim)
        values = near_rows(v_ref, fixed, drawn, heads, head_dim)
        at = block_rows(fixed[2])
        o_ref[at, :] = attend(q_ref[at, :], keys, values)
        return carry

    lax.fori_loop(0, blocks_all - 2, middle, 0, unroll=unroll)
    for end in (0, -1):
        at = block_rows(place(end))
        o_ref[at, :] = attend(q_ref[at, :], k_ref[...], v_ref[...])


def backward_kernel(
    first,
    heads,
    head_dim,
    draws,
    pieces,
    unroll,
    random_ref,
    index_ref,
    q_ref,
    k_ref,
    v_ref,
    *refs,
):
    parts = len(refs) - 8
    grad_refs, out_ref = refs[:parts], refs[parts]
    g_ref, k_near, v_near, k_drawn, v_drawn, k_ends, v_ends = refs[parts + 1 :]
    width = q_ref.shape[1]
    rows = g_ref.shape[0] // parts
    for n, ref in enumerate(grad_refs):
        g_ref[n * rows : (n + 1) * rows, :] = ref[...]
    blocks_all = q_ref.shape[0] // BLOCK
    scaling = head_dim**-0.5
    place = placer(index_ref, blocks_all, pieces)
    owner = lax.broadcasted_iota(jnp.int32, (BLOCK, q_ref.shape[1]), 1) // head_dim
    for ref in (k_drawn, v_drawn, k_ends, v_ends):
        ref[...] = jnp.zeros_like(ref)

    def back(queries, grads, keys, values):
        q_stack = stack_heads(scale_low(queries, scaling), heads, head_dim)
        g_stack = stack_heads(grads, heads, head_dim)
        probs = probabilities(keys, q_stack)
        grad_probs = dot(values, g_stack, NT)
        center = jnp.sum(probs * grad_probs, axis=0, keepdims=True)
        grad_scores = (probs * (grad_probs - center)).astype(BF16)
        grad_keys = dot(grad_scores, q_stack, NN)
        grad_values = dot(probs.astype(BF16), g_stack, NN)
        grad_queries = unstack_heads(dot(grad_scores, keys, TN), heads, head_dim) * scaling
        return grad_queries.astype(BF16), grad_keys, grad_values

    for number, end in enumerate((0, -1)):
        at = block_rows(place(end))
        dq, dk, dv = back(q_ref[at, :], g_ref[at, :], k_ref[...], v_ref[...])
        out_ref[at, 0:width] = dq
        if number == 0:
            k_near[...] = dk
            v_near[...] = dv
        else:
            k_near[...] += dk
            v_near[...] += dv

    def middle(step, carry):
        fixed, drawn = table_of(random_ref, place, step, first, heads, draws)
        keys = near_rows(k_ref, fixed, drawn, heads, head_dim)
        values = near_rows(v_ref, fixed, drawn, heads, head_dim)
        at = block_rows(fixed[2])
        dq, dk, dv = back(q_ref[at, :], g_ref[at, :], keys, values)
        out_ref[at, 0:width] = dq
        for part, near, far, ends in ((dk, k_near, k_drawn, k_ends), (dv, v_near, v_drawn, v_ends)):
            ends[0:BLOCK, :] += part[0:BLOCK]
            ends[BLOCK:, :] += part[4 * BLOCK : 5 * BLOCK]
            if pieces == 1:
                window = pl.ds(pl.multiple_of(step * BLOCK, BLOCK), 3 * BLOCK)
                near[window, :] += part[BLOCK : 4 * BLOCK]
            else:
                for n in range(1, 4):
                    near[block_rows(fixed[n]), :] += part[n * BLOCK : (n + 1) * BLOCK]
            for j in range(draws):
                block = part[(5 + j) * BLOCK : (6 + j) * BLOCK]
                for h in range(heads):
                    kept = block if heads == 1 else jnp.where(owner == h, block, 0.0)
                    far[block_rows(drawn[j][h]), :] += kept
        return carry

    lax.fori_loop(0, blocks_all - 2, middle, 0, unroll=unroll)
    for n, near, far, ends in ((1, k_near, k_drawn, k_ends), (2, v_near, v_drawn, v_ends)):
        near[block_rows(place(0)), :] += ends[0:BLOCK, :]
        near[block_rows(place(-1)), :] += ends[BLOCK:, :]
        out_ref[:, n * width : (n + 1) * width] = (near[...] + far[...]).astype(BF16)


def attention_call(kernel, unroll, project, group, groups, grads, table, index, pieces):
    seq_rows = project.shape[0]
    width = project.shape[1] // (3 * groups)
    heads = table.shape[0] // groups
    draws = table.shape[1] // (seq_rows // BLOCK - 2)
    head_dim = width // heads
    narrow = width % 128 != 0
    first = 3 * group * width
    if narrow:
        operands = [project[:, first + n * width : first + (n + 1) * width] for n in range(3)]
    else:
        operands = [project] * 3

    def spec(part):
        column = 0 if narrow else part
        return pl.BlockSpec((seq_rows, width), lambda g, *refs: (0, column))

    columns = width * (3 if grads else 1)
    total = pltpu.VMEM((seq_rows, width), F32)
    ends = pltpu.VMEM((2 * BLOCK, width), F32)
    return pl.pallas_call(
        functools.partial(kernel, group * heads, heads, head_dim, draws, pieces, unroll),
        grid_spec=pltpu.PrefetchScalarGridSpec(
            num_scalar_prefetch=2,
            grid=(1,),
            in_specs=[spec(3 * group), spec(3 * group + 1), spec(3 * group + 2)]
            + [pl.BlockSpec(g.shape, lambda g, *refs: (0, 0)) for g in grads],
            out_specs=pl.BlockSpec((seq_rows, columns), lambda g, *refs: (0, 0)),
            scratch_shapes=[pltpu.VMEM((seq_rows, width), BF16)] + [total] * 4 + [ends] * 2
            if grads
            else [],
        ),
        out_shape=jax.ShapeDtypeStruct((seq_rows, columns), BF16),
        compiler_params=pltpu.CompilerParams(vmem_limit_bytes=VMEM_LIMIT),
        cost_estimate=cost(20) if grads else CHEAP,
    )(
        table,
        index,
        *operands,
        *grads,
    )


def call(kernel, grid, in_specs, out_specs, out_shape, operands, estimate=CHEAP, limit=16):
    return pl.pallas_call(
        kernel,
        grid=grid,
        in_specs=in_specs,
        out_specs=out_specs,
        out_shape=out_shape,
        compiler_params=pltpu.CompilerParams(vmem_limit_bytes=limit << 20),
        cost_estimate=estimate,
    )(*operands)


def whole(array):
    shape = array if isinstance(array, tuple) else array.shape
    return pl.BlockSpec(shape, lambda i: (0,) * len(shape))


def row_tiles(tile, columns, column=0):
    return pl.BlockSpec((tile, columns), lambda i: (i, column))


def piece_tiles(number, tiles, tile, columns):
    return pl.BlockSpec((tile, columns), lambda i: (jnp.clip(i - number * tiles, 0, tiles - 1), 0))


def chosen(refs, tiles):
    which = pl.program_id(0) // tiles
    value = refs[0][...]
    for n in range(1, len(refs)):
        value = jnp.where(which == n, refs[n][...], value)
    return value


def store_chosen(refs, tiles, value):
    for n, ref in enumerate(refs):

        @pl.when(pl.program_id(0) // tiles == n)
        def _(ref=ref):
            ref[...] = value.astype(ref.dtype)


def folded(value):
    rows, columns = value.shape
    return jnp.sum(value.reshape(rows // 8, 8, columns), axis=0)


def normalize(values):
    center = jnp.mean(values, axis=1, keepdims=True)
    spread = values - center
    variance = jnp.mean(spread * spread, axis=1, keepdims=True)
    inverse = lax.rsqrt(variance + EPS_NORM)
    return spread * inverse, inverse


def norm_kernel(x_ref, gain_ref, shift_ref, h_ref):
    normal, _ = normalize(x_ref[...].astype(F32))
    h_ref[...] = (normal * gain_ref[...] + shift_ref[...]).astype(BF16)


def norm_call(values, gain, shift):
    rows, model = values.shape
    tile = min(128, rows)
    return call(
        norm_kernel,
        (rows // tile,),
        [row_tiles(tile, model), whole((1, model)), whole((1, model))],
        row_tiles(tile, model),
        jax.ShapeDtypeStruct((rows, model), BF16),
        (values, gain.reshape(1, model), shift.reshape(1, model)),
    )


def residual_norm_kernel(own_ref, got_ref, gain_ref, shift_ref, r_ref, h_ref):
    values = own_ref[...] + got_ref[...].astype(F32)
    r_ref[...] = values
    normal, _ = normalize(values)
    h_ref[...] = (normal * gain_ref[...] + shift_ref[...]).astype(BF16)


def residual_norm_call(own, got, gain, shift):
    rows, model = own.shape
    tile = min(128, rows)
    tiles = row_tiles(tile, model)
    return call(
        residual_norm_kernel,
        (rows // tile,),
        [tiles, tiles, whole((1, model)), whole((1, model))],
        [tiles, tiles],
        [jax.ShapeDtypeStruct((rows, model), F32), jax.ShapeDtypeStruct((rows, model), BF16)],
        (own, got, gain.reshape(1, model), shift.reshape(1, model)),
    )


def norm_back_kernel(count, x_ref, base_ref, gain_ref, *refs):
    grad_ref, gain_sum, shift_sum = refs[count : count + 3]
    more = refs[count + 3 :]

    @pl.when(pl.program_id(0) == 0)
    def _():
        for ref in (gain_sum, shift_sum, *more[:1]):
            ref[...] = jnp.zeros_like(ref)

    grad_norm = refs[0][...].astype(F32)
    for ref in refs[1:count]:
        grad_norm = grad_norm + ref[...].astype(F32)
    normal, inverse = normalize(x_ref[...].astype(F32))
    base = base_ref[...].astype(F32)
    scaled = grad_norm * gain_ref[...]
    mean_plain = jnp.mean(scaled, axis=1, keepdims=True)
    mean_normal = jnp.mean(scaled * normal, axis=1, keepdims=True)
    grad = base + inverse * (scaled - mean_plain - normal * mean_normal)
    grad_ref[...] = grad
    gain_sum[...] += folded(grad_norm * normal)
    shift_sum[...] += folded(grad_norm)
    if more:
        more[0][...] += folded(base)
        more[1][...] = grad.astype(BF16)


def norm_back_call(values, base, gain, grads, more=False):
    rows, model = values.shape
    tile = min(128, rows)
    tiles = row_tiles(tile, model)
    sums = jax.ShapeDtypeStruct((8, model), F32)
    result = jax.ShapeDtypeStruct((rows, model), F32)
    low = jax.ShapeDtypeStruct((rows, model), BF16)
    return call(
        functools.partial(norm_back_kernel, len(grads)),
        (rows // tile,),
        [tiles, tiles, whole((1, model))] + [tiles] * len(grads),
        [tiles] + [whole((8, model))] * 2 + ([whole((8, model)), tiles] if more else []),
        [result, sums, sums] + ([sums, low] if more else []),
        (values, base, gain.reshape(1, model), *grads),
    )


def pack_kernel(groups, width, qkv_ref, out_ref, up_ref, down_ref, attn_ref, ffn_ref):
    attn = groups * width
    for g in range(groups):
        for c in range(3):
            at = (3 * g + c) * width
            attn_ref[:, at : at + width] = qkv_ref[c, :, g * width : (g + 1) * width].astype(BF16)
    attn_ref[:, 3 * attn :] = out_ref[...].T.astype(BF16)
    hidden = up_ref.shape[1]
    ffn_ref[:, :hidden] = up_ref[...].astype(BF16)
    ffn_ref[:, hidden:] = down_ref[...].T.astype(BF16)


def pack(weights, groups, width):
    w_qkv, w_out, w_up, w_down = weights
    _, shard, attn = w_qkv.shape
    hidden = w_up.shape[1]
    if width % 128 or shard % 128 or hidden % 128:
        qkv = w_qkv.astype(BF16).reshape(3, shard, groups, width).transpose(1, 2, 0, 3)
        return (
            jnp.concatenate([qkv.reshape(shard, 3 * attn), w_out.astype(BF16).T], axis=1),
            jnp.concatenate([w_up.astype(BF16), w_down.astype(BF16).T], axis=1),
        )
    outs = [
        jax.ShapeDtypeStruct((shard, 4 * attn), BF16),
        jax.ShapeDtypeStruct((shard, 2 * hidden), BF16),
    ]
    return call(
        functools.partial(pack_kernel, groups, width),
        (1,),
        [whole(w) for w in weights],
        [whole(o.shape) for o in outs],
        outs,
        weights,
    )


def qkv_kernel(tiles, *refs):
    w_ref, o_ref = refs[-2:]
    o_ref[...] = dot(chosen(refs[:-2], tiles), w_ref[...], NN).astype(BF16)


def qkv_call(pieces, weights, columns):
    rows, model = pieces[0].shape
    tile = min(256, rows)
    tiles = rows // tile
    count = len(pieces)
    return call(
        functools.partial(qkv_kernel, tiles),
        (count * tiles,),
        [piece_tiles(n, tiles, tile, model) for n in range(count)] + [whole((model, columns))],
        row_tiles(tile, columns),
        jax.ShapeDtypeStruct((count * rows, columns), BF16),
        (*pieces, weights),
    )


def branch_kernel(tiles, groups, x_ref, *refs):
    outs, gots = refs[:groups], refs[groups : 2 * groups]
    near_ref, far_ref, own_ref, other_ref = refs[2 * groups :]

    def joined(parts):
        return jnp.concatenate([p[...] for p in parts], axis=1) if groups > 1 else parts[0][...]

    value = dot(joined(outs), near_ref[...], NT) + dot(joined(gots), far_ref[...], NT)
    step = pl.program_id(0)

    @pl.when(step < tiles)
    def _():
        own_ref[...] = value + x_ref[...].astype(F32)

    @pl.when(step >= tiles)
    def _():
        other_ref[...] = value.astype(BF16)


def branch_call(tokens, outs, gots, attn_low, out_far):
    rows, model = tokens.shape
    attn = out_far.shape[1]
    groups = len(outs)
    width = attn // groups
    tile = min(256, rows)
    tiles = rows // tile
    return call(
        functools.partial(branch_kernel, tiles, groups),
        (2 * tiles,),
        [piece_tiles(0, tiles, tile, model)]
        + [row_tiles(tile, width)] * (2 * groups)
        + [pl.BlockSpec((model, attn), lambda i: (0, 3)), whole(out_far)],
        [piece_tiles(0, tiles, tile, model), piece_tiles(1, tiles, tile, model)],
        [jax.ShapeDtypeStruct((rows, model), F32), jax.ShapeDtypeStruct((rows, model), BF16)],
        (tokens, *outs, *gots, attn_low, out_far),
    )


def gelu_parts(values):
    square = values * values
    curve = jnp.tanh(values * (GELU_SCALE + (GELU_SCALE * GELU_CUBE) * square))
    half = 0.5 + 0.5 * curve
    slope = half + (0.5 * values) * (1.0 - curve * curve) * (
        GELU_SCALE + (3.0 * GELU_SCALE * GELU_CUBE) * square
    )
    return values * half, slope


def ffn_kernel(tiles, count, *refs):
    h_refs, g_refs = refs[:count], refs[count : 2 * count]
    up_ref, down_ref, bias_ref, both_ref, sum_ref = refs[2 * count : 2 * count + 5]
    dh_refs = refs[2 * count + 5 :]
    hidden = up_ref.shape[1]

    @pl.when(pl.program_id(0) == 0)
    def _():
        sum_ref[...] = jnp.zeros_like(sum_ref)

    hidden_pre = dot(chosen(h_refs, tiles), up_ref[...], NN) + bias_ref[...]
    grad_active = dot(chosen(g_refs, tiles), down_ref[...], NN)
    active, slope = gelu_parts(hidden_pre)
    grad_hidden = (grad_active * slope).astype(BF16)
    both_ref[:, :hidden] = grad_hidden
    both_ref[:, hidden:] = active.astype(BF16)
    sum_ref[...] += folded(grad_hidden.astype(F32))
    store_chosen(dh_refs, tiles, dot(grad_hidden, up_ref[...], NT))


def ffn_call(normed, grads, ffn_low, bias):
    count = len(normed)
    rows, model = normed[0].shape
    hidden = ffn_low.shape[1] // 2
    tile = min(256, rows)
    tiles = rows // tile
    pieces = [piece_tiles(n, tiles, tile, model) for n in range(count)]
    both = jax.ShapeDtypeStruct((count * rows, 2 * hidden), BF16)
    return call(
        functools.partial(ffn_kernel, tiles, count),
        (count * tiles,),
        pieces
        + pieces
        + [
            pl.BlockSpec((model, hidden), lambda i: (0, 0)),
            pl.BlockSpec((model, hidden), lambda i: (0, 1)),
            whole((1, hidden)),
        ],
        [row_tiles(tile, 2 * hidden), whole((8, hidden))] + pieces,
        [both, jax.ShapeDtypeStruct((8, hidden), F32)]
        + [jax.ShapeDtypeStruct((rows, model), BF16)] * count,
        (*normed, *grads, ffn_low, ffn_low, bias.reshape(1, hidden)),
        limit=24,
    )


def row_piece(number, rows, columns):
    return pl.BlockSpec((rows, columns), lambda i: (number, 0))


def outer_kernel(count, rights_count, extras, *refs):
    lefts = refs[:count]
    at = count
    o_ref = refs[-1]
    column = 0
    for _ in range(rights_count):
        total = dot(lefts[0][...], refs[at][...], TN)
        for n in range(1, count):
            total = total + dot(lefts[n][...], refs[at + n][...], TN)
        at += count
        o_ref[:, column : column + total.shape[1]] = total.astype(BF16)
        column += total.shape[1]
    if extras:
        total = refs[at][...].astype(F32)
        for n in range(1, extras):
            total = total + refs[at + n][...].astype(F32)
        o_ref[:, column:] = total.astype(BF16)


def outer_sum(lefts, rights, extras=()):
    count = len(lefts)
    rows, model = lefts[0].shape
    tile = min(512, model)
    columns = sum(r.shape[1] for r in rights) + (extras[0].shape[1] if extras else 0)
    specs = [pl.BlockSpec((rows, tile), lambda i: (0, i))] * count
    operands = list(lefts)
    for right in rights:
        specs += [row_piece(n, rows, right.shape[1]) for n in range(count)]
        operands += [right] * count
    specs += [row_tiles(tile, e.shape[1]) for e in extras]
    return call(
        functools.partial(outer_kernel, count, len(rights), len(extras)),
        (model // tile,),
        specs,
        row_tiles(tile, columns),
        jax.ShapeDtypeStruct((model, columns), BF16),
        (*operands, *extras),
    )


def double_outer_kernel(count, steps, *refs):
    rights, o_ref = refs[2 * count : 3 * count], refs[3 * count]
    first = pl.program_id(0) < steps
    total = None
    for n in range(count):
        left = jnp.where(first, refs[n][...], refs[count + n][...])
        part = dot(left, rights[n][...], TN)
        total = part if total is None else total + part
    o_ref[...] = total.astype(BF16)


def double_outer_sum(lefts, other_lefts, rights):
    count = len(lefts)
    rows, model = lefts[0].shape
    columns = rights[0][0].shape[1] // 2
    tile = min(512, model)
    steps = model // tile

    def left_spec(which):
        return pl.BlockSpec(
            (rows, tile), lambda i: (0, jnp.clip(i - which * steps, 0, steps - 1))
        )

    def right_spec(block):
        return pl.BlockSpec((rows, columns), lambda i: (block, i // steps))

    return call(
        functools.partial(double_outer_kernel, count, steps),
        (2 * steps,),
        [left_spec(0)] * count + [left_spec(1)] * count + [right_spec(n) for _, n in rights],
        pl.BlockSpec((tile, columns), lambda i: (i % steps, i // steps)),
        jax.ShapeDtypeStruct((model, 2 * columns), BF16),
        (*lefts, *other_lefts, *(a for a, _ in rights)),
        limit=24,
    )


def head_grads_kernel(tiles, count, width, *refs):
    w_ref, outs = refs[count], refs[count + 1 :]
    value = dot(chosen(refs[:count], tiles), w_ref[...], NN).astype(BF16)
    for n, out in enumerate(outs):
        out[...] = value[:, n * width : (n + 1) * width]


def head_grads_call(pieces, weights, column, attn, groups):
    count = len(pieces)
    rows, model = pieces[0].shape
    width = attn // groups
    tile = min(256, rows)
    tiles = rows // tile
    return call(
        functools.partial(head_grads_kernel, tiles, count, width),
        (count * tiles,),
        [piece_tiles(n, tiles, tile, model) for n in range(count)]
        + [pl.BlockSpec((model, attn), lambda i: (0, column))],
        [row_tiles(tile, width)] * groups,
        [jax.ShapeDtypeStruct((count * rows, width), BF16)] * groups,
        (*pieces, weights),
    )


def back_project_kernel(groups, tiles, *refs):
    w_ref, outs = refs[groups], refs[groups + 1 :]
    parts = [refs[n][...] for n in range(groups)]
    grads = jnp.concatenate(parts, axis=1) if groups > 1 else parts[0]
    store_chosen(outs, tiles, dot(grads, w_ref[...], NT))


def back_project(grads, weights, first, count, rows):
    groups = len(grads)
    columns = grads[0].shape[1]
    model = weights.shape[0]
    tile = min(256, rows)
    tiles = rows // tile
    return call(
        functools.partial(back_project_kernel, groups, tiles),
        (count * tiles,),
        [pl.BlockSpec((tile, columns), lambda i: (first * tiles + i, 0))] * groups
        + [whole((model, groups * columns))],
        [piece_tiles(n, tiles, tile, model) for n in range(count)],
        [jax.ShapeDtypeStruct((rows, model), BF16)] * count,
        (*grads, weights),
    )


def down_kernel(tiles, z_ref, w_ref, *outs):
    store_chosen(outs, tiles, dot(z_ref[...], w_ref[...], NT))


def down_call(both, ffn_low, count):
    model = ffn_low.shape[0]
    hidden = ffn_low.shape[1] // 2
    rows = both.shape[0] // count
    tile = min(256, rows)
    tiles = rows // tile
    return call(
        functools.partial(down_kernel, tiles),
        (count * tiles,),
        [
            pl.BlockSpec((tile, hidden), lambda i: (i, 1)),
            pl.BlockSpec((model, hidden), lambda i: (0, 1)),
        ],
        [piece_tiles(n, tiles, tile, model) for n in range(count)],
        [jax.ShapeDtypeStruct((rows, model), BF16)] * count,
        (both, ffn_low),
    )


def columns_of(refs, cuts):
    for matrix, (which, first, blocks) in enumerate(cuts):
        for n, at in enumerate(first if isinstance(first, tuple) else range(first, first + blocks)):
            yield matrix, n, refs[which][:, at * 128 : (at + 1) * 128].astype(F32)


def sums_kernel(cuts, grads_count, token_count, *refs):
    grads = refs[:grads_count]
    token_refs = refs[grads_count : grads_count + token_count]
    bias_refs = refs[grads_count + token_count : -2]
    across_ref, along_ref = refs[-2:]
    across_ref[...] = jnp.zeros_like(across_ref)
    totals = [None] * len(cuts)
    row = 0
    for matrix, _, value in columns_of(grads, cuts):
        square = value * value
        totals[matrix] = square if totals[matrix] is None else totals[matrix] + square
        along_ref[row : row + 1, :] = jnp.sum(square, axis=0, keepdims=True)
        row += 1
    for matrix, total in enumerate(totals):
        across_ref[matrix : matrix + 1, :] = jnp.sum(total.T, axis=0, keepdims=True)

    def store_rows(ref, row, value):
        for n in range(value.shape[1] // 128):
            ref[row + n : row + n + 1, :] = value[:, n * 128 : (n + 1) * 128]

    bias = bias_refs[0][...]
    for ref in bias_refs[1:]:
        bias = bias + ref[...]
    store_rows(along_ref, row, jnp.sum(bias, axis=0, keepdims=True))
    row = 8
    for ref in token_refs:
        value = jnp.sum(ref[...], axis=0, keepdims=True)
        store_rows(across_ref, row, value)
        row += value.shape[1] // 128


def join_kernel(matrices, across_ref, along_ref, o_ref):
    along_rows = along_ref.shape[0]
    token_rows = across_ref.shape[0] - 8
    o_ref[0:along_rows, :] = along_ref[...]
    o_ref[along_rows : along_rows + token_rows, :] = across_ref[8:, :]
    o_ref[along_rows + token_rows :, :] = jnp.broadcast_to(
        jnp.sum(across_ref[0:8, :], axis=1, keepdims=True), (8, 128)
    )


def step_kernel(cuts, grads_count, model, wide, *refs):
    grads = refs[:grads_count]
    across_ref, sums_ref, qkv_ref, out_ref, up_ref, down_ref = refs[grads_count : grads_count + 6]
    n_qkv, n_out, n_up, n_down, qkv_rows, qkv_cols = refs[grads_count + 6 : grads_count + 12]
    singles = refs[grads_count + 12 : grads_count + 18]
    copies = refs[grads_count + 18 :]
    totals_at = sums_ref.shape[0] - 8
    scales = []
    for matrix in range(len(cuts)):
        whole_mean = sums_ref[totals_at + matrix : totals_at + matrix + 1, :] / (
            model * wide[matrix]
        ) + EPS_FACTOR
        model_factor = (across_ref[matrix : matrix + 1, :] / wide[matrix] + EPS_FACTOR) / whole_mean
        if matrix < 3:
            qkv_rows[matrix : matrix + 1, :] = model_factor
        else:
            singles[matrix - 3][...] = model_factor
        scales.append((whole_mean, jnp.broadcast_to(model_factor, (128, 128)).T))
    row = 0
    for matrix, n, value in columns_of(grads, cuts):
        whole_mean, model_factor = scales[matrix]
        other_factor = (sums_ref[row : row + 1, :] / model + EPS_FACTOR) / whole_mean
        row += 1
        update = LEARN_RATE * (value * lax.rsqrt(model_factor * other_factor * whole_mean))
        at = slice(n * 128, (n + 1) * 128)
        if matrix < 3:
            n_qkv[matrix, :, at] = qkv_ref[matrix, :, at] - update
            qkv_cols[matrix : matrix + 1, at] = other_factor
            continue
        singles[matrix][n : n + 1, :] = other_factor
        if matrix == 3:
            n_out[at, :] = out_ref[at, :] - update.T
        elif matrix == 4:
            n_up[:, at] = up_ref[:, at] - update
        else:
            n_down[at, :] = down_ref[at, :] - update.T
    for ref in copies:
        count = ref.shape[0]
        ref[...] = sums_ref[row : row + count, :]
        row += count


def step_tail(dp_size, mp_size, attn_grads, ffn_grads, weights, token_sums, bias_sums, groups):
    w_qkv, w_out, w_up, w_down = weights
    shard, attn = w_qkv.shape[1:]
    hidden = w_up.shape[1]
    model = shard * dp_size
    per_group = attn // groups // 128
    attn_blocks, hidden_blocks = attn // 128, hidden // 128
    grads = [*attn_grads, ffn_grads]
    joined = jnp.concatenate([g[:, : 3 * attn // groups] for g in attn_grads], axis=1)
    grads = [joined, attn_grads[0], ffn_grads]
    cuts = [
        (
            0,
            tuple(
                (3 * g + c) * per_group + n for g in range(groups) for n in range(per_group)
            ),
            0,
        )
        for c in range(3)
    ]
    cuts += [
        (1, 3 * per_group, attn_blocks),
        (2, 0, hidden_blocks),
        (2, hidden_blocks, hidden_blocks),
    ]
    rows = 4 * attn_blocks + 2 * hidden_blocks
    bias_rows = hidden_blocks
    token_rows = len(token_sums) * model // 128

    def square(count):
        return jax.ShapeDtypeStruct((count, 128), F32)

    operands = (*grads, *token_sums, *bias_sums)
    across, along = call(
        functools.partial(sums_kernel, cuts, len(grads), len(token_sums)),
        (1,),
        [whole(a) for a in operands],
        [whole((8 + token_rows, 128)), whole((rows + bias_rows, 128))],
        [square(8 + token_rows), square(rows + bias_rows)],
        operands,
    )
    across = butterfly(across, "mp", mp_size)
    count = rows + bias_rows + token_rows + 8
    sums = call(
        functools.partial(join_kernel, len(cuts)),
        (1,),
        [whole(across), whole(along)],
        whole((count, 128)),
        square(count),
        (across, along),
    )
    sums = butterfly(sums, "dp", dp_size)
    wide = [attn * mp_size] * 4 + [hidden * mp_size] * 2
    operands = (*grads, across, sums, *weights)
    outs = [jax.ShapeDtypeStruct(w.shape, F32) for w in weights]
    outs += [jax.ShapeDtypeStruct((3, shard), F32), jax.ShapeDtypeStruct((3, attn), F32)]
    outs += [square(1)] * 3 + [square(attn_blocks), square(hidden_blocks), square(hidden_blocks)]
    outs += [square(bias_rows)] + [square(model // 128)] * len(token_sums)
    new_qkv, new_out, new_up, new_down, qkv_rows, qkv_cols, *rest = call(
        functools.partial(step_kernel, cuts, len(grads), model, wide),
        (1,),
        [whole(a) for a in operands],
        [whole(o.shape) for o in outs],
        outs,
        operands,
    )
    rest = [r.reshape(-1) for r in rest]
    return (
        (new_qkv, qkv_rows, qkv_cols),
        (new_out, rest[3], rest[0]),
        (new_up, rest[1], rest[4]),
        (new_down, rest[5], rest[2]),
        rest[7:],
        rest[6],
    )


def step_plain(dp_size, mp_size, attn_grads, ffn_grads, weights, token_sums, bias_sums, groups):
    w_qkv, w_out, w_up, w_down = weights
    shard, attn = w_qkv.shape[1:]
    hidden = w_up.shape[1]
    model = shard * dp_size
    width = attn // groups
    qkv = jnp.stack([g[:, : 3 * width].reshape(shard, 3, width) for g in attn_grads], axis=1)
    shards = [qkv[:, :, n].reshape(shard, attn) for n in range(3)] + [
        attn_grads[0][:, 3 * width :],
        ffn_grads[:, :hidden].astype(F32),
        ffn_grads[:, hidden:].astype(F32),
    ]
    squares = [g * g for g in shards]
    across = butterfly(
        jnp.concatenate(
            [jnp.sum(s, axis=1) for s in squares] + [jnp.sum(t, axis=0) for t in token_sums]
        ),
        "mp",
        mp_size,
    )
    model_sums = [across[n * shard : (n + 1) * shard] for n in range(6)]
    totals = jnp.stack([jnp.sum(s) for s in model_sums])
    sums = butterfly(
        jnp.concatenate(
            [jnp.sum(s, axis=0) for s in squares]
            + [across[6 * shard :], jnp.sum(sum(bias_sums), axis=0), totals]
        ),
        "dp",
        dp_size,
    )
    cuts = []
    start = 0
    for length in [attn] * 4 + [hidden] * 2 + [model] * len(token_sums) + [hidden, 6]:
        cuts.append(sums[start : start + length])
        start += length
    steps = []
    for n in range(6):
        wide = (attn if n < 4 else hidden) * mp_size
        whole_mean = cuts[-1][n] / (model * wide) + EPS_FACTOR
        model_factor = (model_sums[n] / wide + EPS_FACTOR) / whole_mean
        other_factor = (cuts[n] / model + EPS_FACTOR) / whole_mean
        update = shards[n] * lax.rsqrt(model_factor[:, None] * other_factor[None, :] * whole_mean)
        steps.append((LEARN_RATE * update, model_factor, other_factor))
    return (
        (
            w_qkv - jnp.stack([steps[n][0] for n in range(3)]),
            jnp.stack([steps[n][1] for n in range(3)]),
            jnp.stack([steps[n][2] for n in range(3)]),
        ),
        (w_out - steps[3][0].T, steps[3][2], steps[3][1]),
        (w_up - steps[4][0], steps[4][1], steps[4][2]),
        (w_down - steps[5][0].T, steps[5][2], steps[5][1]),
        cuts[6 : 6 + len(token_sums)],
        cuts[-2],
    )


def results(out_tokens, grad_tokens, step):
    qkv, out, up, down, token_sums, bias_sum = step
    return (
        out_tokens[None],
        grad_tokens[None],
        *qkv,
        *out,
        *up,
        *down,
        *token_sums[:4],
        bias_sum,
        token_sums[4],
    )


def body(
    dp_size,
    mp_size,
    tokens,
    cotangent,
    w_qkv,
    w_out,
    w_up,
    w_down,
    gain_attn,
    shift_attn,
    gain_ffn,
    shift_ffn,
    bias_up,
    bias_down,
    random_blocks,
):
    weights = (w_qkv, w_out, w_up, w_down)
    own_tokens, grad_top = tokens[0], cotangent[0]
    random_rows = random_blocks[0].reshape(random_blocks.shape[1], -1)
    index = lax.axis_index("mp").astype(jnp.int32).reshape(1)
    shard, attn = w_qkv.shape[1:]
    own_rows, model = own_tokens.shape
    width = min(128, attn)
    groups = attn // width
    low_attn, low_ffn = pack(weights, groups, width)
    if mp_size == 4 and dp_size == 8 and width == 128:
        arrange = paired_layer
    else:
        arrange = plain_layer
    out_tokens, grad_tokens, attn_grads, ffn_grads, token_sums, bias_sums = arrange(
        dp_size,
        mp_size,
        own_tokens,
        grad_top,
        random_rows,
        index,
        low_attn,
        low_ffn,
        (gain_attn, shift_attn, gain_ffn, shift_ffn),
        bias_up,
        bias_down,
        groups,
        width,
    )
    aligned = width == 128 and shard == 128 and w_up.shape[1] % 128 == 0
    step = (step_tail if aligned else step_plain)(
        dp_size, mp_size, attn_grads, ffn_grads, weights, token_sums, bias_sums, groups
    )
    return results(out_tokens, grad_tokens, step)


def paired_layer(
    dp_size,
    mp_size,
    tokens,
    grad_top,
    random_rows,
    index,
    low_attn,
    low_ffn,
    norms,
    bias_up,
    bias_down,
    groups,
    width,
):
    gain_attn, shift_attn, gain_ffn, shift_ffn = norms
    rows, model = tokens.shape
    attn = groups * width
    mine = lax.axis_index("dp")
    index_rows = gain_attn.reshape(8, -1)

    def other_core(value):
        return swap(value, 1, mp_size)

    def other_chip(value):
        return swap(value, 2, mp_size)

    offsets = (0, 1, 3, 2)
    places = [(mine + 2 * n) % dp_size for n in offsets]
    places += [p ^ 1 for p in places]

    def levels_of(low):
        return [low] + [shifted(low, -2 * n, dp_size) for n in offsets[1:]]

    def between_x(value):
        return swap(value, 1, dp_size, "dp")

    def fence(value, *others):
        return after(value, other_core(after(index_rows, *others)))

    normed = norm_call(tokens, gain_attn, shift_attn)
    normed = norm_call(tokens, gain_attn, shift_attn)
    normed_near = other_core(normed)
    far = other_chip(normed)
    attn_levels = levels_of(after(low_attn, normed))
    attn_swapped = [between_x(level) for level in attn_levels[:3]]
    attn_swapped.append(between_x(after(attn_levels[3], far, *attn_swapped)))
    ffn_low = lax.all_gather(
        after(low_ffn, far, attn_levels[3], *attn_swapped[:3]), "dp", axis=0, tiled=True
    )

    normed_pieces = [normed, normed_near, far, other_core(far)]
    top_far = other_chip(after(grad_top, far))
    top_near = other_core(grad_top)
    attn_low = assemble(attn_levels + attn_swapped, places)
    project = qkv_call(normed_pieces, after(attn_low, random_rows), 3 * attn)
    out_far = other_chip(after(attn_low[:, 3 * attn :], far))

    heads_out, heads_got = [], []
    for group in range(groups):
        if group == groups - 1:
            project = after(project, top_far)
        heads_out.append(
            attention_call(
                forward_kernel, 5, project, group, groups, (), random_rows, index, mp_size
            )
        )
        heads_got.append(other_chip(heads_out[-1][2 * rows :]))
    own, other = branch_call(
        tokens, heads_out, heads_got, attn_low, out_far
    )
    middle, second = residual_norm_call(own, other_core(other), gain_ffn, shift_ffn)

    second_far = other_chip(second)
    second_near = other_core(second)
    both_near, bias_near, back_own, back_near = ffn_call(
        [second, second_near], [grad_top, top_near], ffn_low, bias_up
    )
    second_far = after(second_far, back_own)
    second_last = other_core(second_far)
    top_last = other_core(top_far)
    both_far, bias_far, back_far, back_last = ffn_call(
        [second_far, second_last], [top_far, top_last], ffn_low, bias_up
    )
    crossing = (back_far.astype(F32) + other_core(back_last).astype(F32)).astype(BF16)
    crossed = other_chip(crossing)
    back_got = other_core(back_near)
    ffn_grads = double_outer_sum(
        [after(second, crossing), second_near, second_far, second_last],
        [grad_top, top_near, top_far, top_last],
        [(both_near, 0), (both_near, 1), (both_far, 0), (both_far, 1)],
    )
    down_far, down_last = down_call(after(both_far, ffn_grads), ffn_low, 2)
    crossed = after(crossed, ffn_grads, down_far)
    ffn_shard = lax.psum_scatter(
        after(ffn_grads, crossed), "dp", scatter_dimension=0, tiled=True
    )
    grad_middle, gain_two, shift_two, top_sum, grad_branch = norm_back_call(
        middle, grad_top, gain_ffn, [back_own, back_got, crossed], True
    )

    branch_pieces = [grad_branch, other_core(grad_branch)]
    away = head_grads_call(branch_pieces, out_far, 0, attn, groups)
    came = [other_chip(a) for a in away]
    stay = list(head_grads_call(branch_pieces, attn_low, 3, attn, groups))
    out_away = other_chip(
        outer_sum([after(grad_branch, *away, *stay), branch_pieces[1]], heads_got)
    )
    out_stay = outer_sum(branch_pieces, [h[: 2 * rows] for h in heads_out])
    down_crossing = (
        down_far.astype(F32) + other_core(after(down_last, *away)).astype(F32)
    ).astype(BF16)
    down_crossed = other_chip(after(down_crossing, came[0]))

    grad_projects = []
    project = after(project, down_crossing, out_stay)
    for group in range(groups):
        grad_projects.append(
            attention_call(
                backward_kernel,
                3,
                project,
                group,
                groups,
                (stay[group], came[group]),
                random_rows,
                index,
                mp_size,
            )
        )
        if group == 0:
            first_sum = outer_sum(normed_pieces, grad_projects[:1], (out_stay, out_away))
            kept, sent = scatter_model_split(first_sum, dp_size)
            project, kept, sent = lax.optimization_barrier((project, kept, sent))
            sums = [(kept, between_x(sent))]
    grad_projects[-1] = after(grad_projects[-1], sums[0][1], down_crossed)

    [back_last] = back_project(grad_projects, attn_low, 3, 1, rows)
    came_last = other_core(back_last)
    [back_far] = back_project(
        [after(grad_projects[0], back_last)] + grad_projects[1:], attn_low, 2, 1, rows
    )
    crossing = (back_far.astype(F32) + came_last.astype(F32)).astype(BF16)
    crossed = other_chip(crossing)
    late = [fence(g, crossing) for g in grad_projects]
    for group in range(1, groups):
        kept, sent = scatter_model_split(
            outer_sum(normed_pieces, late[group : group + 1]), dp_size
        )
        sums.append((kept, between_x(sent)))
    sums[0] = (after(sums[0][0], crossing), sums[0][1])
    attn_parts = [scatter_model_end(*s, dp_size) for s in sums]
    back_own, back_near = back_project(late, attn_low, 0, 2, rows)
    back_got = other_core(back_near)
    down_own, down_near = down_call(after(both_near, back_own), ffn_low, 2)
    out_tokens = (
        middle
        + down_own.astype(F32)
        + other_core(down_near).astype(F32)
        + down_crossed.astype(F32)
        + bias_down
    ).astype(BF16)
    grad_tokens, gain_one, shift_one = norm_back_call(
        tokens, grad_middle, gain_attn, [back_own, back_got, after(crossed, out_tokens)]
    )
    attn_grads = [sum(after(p, gain_one).astype(F32) for p in parts) for parts in attn_parts]
    token_sums = [gain_one, shift_one, gain_two, shift_two, top_sum]
    return out_tokens, grad_tokens, attn_grads, ffn_shard, token_sums, [bias_near, bias_far]


def plain_layer(
    dp_size,
    mp_size,
    tokens,
    grad_top,
    random_rows,
    index,
    low_attn,
    low_ffn,
    norms,
    bias_up,
    bias_down,
    groups,
    width,
):
    gain_attn, shift_attn, gain_ffn, shift_ffn = norms
    rows, model = tokens.shape
    attn = groups * width
    lines = [[core + 2 * n for n in range(mp_size // 2)] for core in range(2)]
    core = lax.axis_index("mp") % 2

    def gather(value, axis, along=0):
        return lax.all_gather(value, axis, axis=along, tiled=True)

    def other_core(value):
        return swap(value, 1, mp_size)

    def scattered(value):
        return lax.psum_scatter(value, "mp", scatter_dimension=0, tiled=True)

    def own_first(value):
        half = value.shape[0] // 2
        return jnp.where(core == 0, value, jnp.roll(value, half, axis=0))

    attn_low = gather(low_attn, "dp")
    ffn_low = gather(low_ffn, "dp")
    normed = gather(norm_call(tokens, gain_attn, shift_attn), "mp")
    top_full = gather(grad_top, "mp")
    project = qkv_call([normed], attn_low[:, : 3 * attn], 3 * attn)
    out_low = lax.all_gather(
        attn_low[:, 3 * attn :], "mp", axis=1, axis_index_groups=lines, tiled=True
    )
    heads_out = [
        attention_call(forward_kernel, 5, project, g, groups, (), random_rows, index, 1)
        for g in range(groups)
    ]
    moved = own_first(
        lax.all_to_all(
            jnp.concatenate(heads_out, axis=1), "mp", 0, 1, axis_index_groups=lines, tiled=True
        )
    )
    branch = dot(moved, out_low, NT)
    middle, second = residual_norm_call(
        tokens.astype(F32) + branch[:rows],
        other_core(branch[rows:].astype(BF16)),
        gain_ffn,
        shift_ffn,
    )
    second_full = gather(second, "mp")
    both, bias_sum, back = ffn_call([second_full], [top_full], ffn_low, bias_up)
    ffn_grads = double_outer_sum([second_full], [top_full], [(both, 0)])
    ffn_shard = lax.psum_scatter(ffn_grads, "dp", scatter_dimension=0, tiled=True)
    grad_middle, gain_two, shift_two, top_sum, grad_branch = norm_back_call(
        middle, grad_top, gain_ffn, [scattered(back)], True
    )
    branch_pair = jnp.concatenate([grad_branch, other_core(grad_branch)], axis=0)
    away = own_first(dot(branch_pair, out_low, NN).astype(BF16))
    away = lax.all_to_all(away, "mp", 1, 0, axis_index_groups=lines, tiled=True)
    out_grad = lax.psum_scatter(
        dot(branch_pair, moved, TN).astype(BF16),
        "mp",
        scatter_dimension=1,
        axis_index_groups=lines,
        tiled=True,
    )
    grad_projects = [
        attention_call(
            backward_kernel,
            3,
            project,
            g,
            groups,
            (away[:, g * width : (g + 1) * width],),
            random_rows,
            index,
            1,
        )
        for g in range(groups)
    ]
    attn_grads = [
        scatter_model(
            outer_sum([normed], [g], (out_grad,) if n == 0 else ()), dp_size
        )
        for n, g in enumerate(grad_projects)
    ]
    back = sum(
        dot(g, attn_low[:, 3 * n * width : 3 * (n + 1) * width], NT)
        for n, g in enumerate(grad_projects)
    )
    grad_tokens, gain_one, shift_one = norm_back_call(
        tokens, grad_middle, gain_attn, [scattered(back.astype(BF16))]
    )
    down = scattered(down_call(both, ffn_low, 1)[0])
    out_tokens = (middle + down.astype(F32) + bias_down).astype(BF16)
    token_sums = [gain_one, shift_one, gain_two, shift_two, top_sum]
    return out_tokens, grad_tokens, attn_grads, ffn_shard, token_sums, [bias_sum]


def solution(mesh):
    placed = (
        P("dp", "mp", None),
        P("dp", "mp", None),
        P(None, "dp", "mp"),
        P("mp", "dp"),
        P("dp", "mp"),
        P("mp", "dp"),
        P(),
        P(),
        P(),
        P(),
        P("mp"),
        P(),
        P("dp", "mp", None, None),
    )
    return jax.shard_map(
        functools.partial(body, mesh.shape["dp"], mesh.shape["mp"]),
        mesh=mesh,
        in_specs=placed,
        out_specs=(
            P("dp", "mp", None),
            P("dp", "mp", None),
            P(None, "dp", "mp"),
            P(None, "dp"),
            P(None, "mp"),
            P("mp", "dp"),
            P("mp"),
            P("dp"),
            P("dp", "mp"),
            P("dp"),
            P("mp"),
            P("mp", "dp"),
            P("mp"),
            P("dp"),
            P(),
            P(),
            P(),
            P(),
            P("mp"),
            P(),
        ),
        check_vma=False,
    )
```

```python
import functools

import jax
import jax.numpy as jnp
from jax import lax
from jax.experimental import pallas as pl
from jax.experimental.pallas import tpu as pltpu
from jax.sharding import PartitionSpec as P

BLOCK = 64
EPS_NORM = 1e-05
EPS_FACTOR = 1e-30
LEARN_RATE = 0.1
GELU_SCALE = 0.7978845608028654
GELU_CUBE = 0.044715
F32 = jnp.float32
BF16 = jnp.bfloat16
NN = (((1,), (0,)), ((), ()))
NT = (((1,), (1,)), ((), ()))
TN = (((0,), (0,)), ((), ()))
VMEM_LIMIT = 24 << 20


def cost(microseconds):
    return pl.CostEstimate(flops=int(microseconds * 1.15e9), bytes_accessed=1 << 10, transcendentals=0)


CHEAP = cost(0.01)


def dot(left, right, form):
    return lax.dot_general(left, right, form, preferred_element_type=F32)


def swap(value, bit, size, axis="mp"):
    return lax.ppermute(value, axis, [(i, i ^ bit) for i in range(size)])


def after(value, *others):
    return lax.optimization_barrier((value, *others))[0]


def shifted(value, by, size):
    return lax.ppermute(value, "dp", [(i, (i + by) % size) for i in range(size)])


def scatter_model(partial, size):
    if size != 8:
        return lax.psum_scatter(partial, "dp", scatter_dimension=0, tiled=True).astype(F32)
    kept, sent = scatter_model_split(partial, size)
    return sum(p.astype(F32) for p in scatter_model_end(kept, swap(sent, 1, size, "dp"), size))


def scatter_model_split(partial, size):
    mine = lax.axis_index("dp")
    rows = partial.shape[0] // size
    columns = partial.shape[1]
    side = mine % 2
    split = partial.reshape(4, 2, rows, columns)

    def of_side(which):
        return lax.dynamic_slice(split, (0, which, 0, 0), (4, 1, rows, columns)).reshape(
            4, rows, columns
        )

    return of_side(side), of_side(1 - side)


def scatter_model_end(kept, got, size):
    level = lax.axis_index("dp") // 2
    rows, columns = kept.shape[1:]
    pair = (kept.astype(F32) + got.astype(F32)).astype(BF16)

    def of_level(which):
        return lax.dynamic_slice(pair, (which, 0, 0), (1, rows, columns))[0]

    parts = [shifted(of_level((level + n) % 4), 2 * n, size) for n in (1, 3, 2)]
    return [of_level(level)] + parts


def assemble_kernel(count, place_ref, *refs):
    rows = refs[0].shape[0]
    for n in range(count):
        at = pl.ds(pl.multiple_of(place_ref[n] * rows, rows), rows)
        refs[count][at, :] = refs[n][...]


def assemble(parts, places):
    count = len(parts)
    rows, columns = parts[0].shape
    tile = min(512, columns)
    return pl.pallas_call(
        functools.partial(assemble_kernel, count),
        grid=(columns // tile,),
        in_specs=[pl.BlockSpec(memory_space=pltpu.SMEM)]
        + [pl.BlockSpec((rows, tile), lambda i: (0, i))] * count,
        out_specs=pl.BlockSpec((count * rows, tile), lambda i: (0, i)),
        out_shape=jax.ShapeDtypeStruct((count * rows, columns), parts[0].dtype),
        compiler_params=pltpu.CompilerParams(vmem_limit_bytes=VMEM_LIMIT),
        cost_estimate=CHEAP,
    )(jnp.stack(places).astype(jnp.int32), *parts)


def butterfly(value, axis, size):
    bit = 1
    while bit < size:
        value = value + swap(value, bit, size, axis)
        bit *= 2
    return value


def stack_heads(block, heads, head_dim):
    if heads == 1:
        return block
    owner = lax.broadcasted_iota(jnp.int32, block.shape, 1) // head_dim
    zero = jnp.zeros_like(block)
    return jnp.concatenate([jnp.where(owner == h, block, zero) for h in range(heads)], axis=0)


def unstack_heads(stacked, heads, head_dim):
    if heads == 1:
        return stacked
    rows = stacked.shape[0] // heads
    owner = lax.broadcasted_iota(jnp.int32, (rows, stacked.shape[1]), 1) // head_dim
    result = stacked[:rows]
    for h in range(1, heads):
        result = jnp.where(owner >= h, stacked[h * rows : (h + 1) * rows], result)
    return result


def block_rows(place):
    return pl.ds(pl.multiple_of(place * BLOCK, BLOCK), BLOCK)


def near_rows(ref, fixed, drawn, heads, head_dim):
    parts = [ref[block_rows(place), :] for place in fixed]
    for places in drawn:
        block = ref[block_rows(places[0]), :]
        if heads > 1:
            owner = lax.broadcasted_iota(jnp.int32, block.shape, 1) // head_dim
            for h in range(1, heads):
                block = jnp.where(owner >= h, ref[block_rows(places[h]), :], block)
        parts.append(block)
    return jnp.concatenate(parts, axis=0)


def probabilities(keys, queries):
    scores = dot(keys, queries, NT)
    expanded = jnp.exp(scores - jnp.max(scores, axis=0, keepdims=True))
    return expanded * (1.0 / jnp.sum(expanded, axis=0, keepdims=True))


def scale_low(block, scaling):
    return (block.astype(F32) * scaling).astype(BF16)


def table_of(random_ref, place, step, first, heads, draws):
    fixed = [place(0), place(step), place(step + 1), place(step + 2), place(-1)]
    drawn = [
        [place(random_ref[first + h, step * draws + j]) for h in range(heads)]
        for j in range(draws)
    ]
    return fixed, drawn


def placer(index_ref, blocks_all, pieces):
    per_piece = blocks_all // pieces

    def place(block):
        if isinstance(block, int):
            block = jnp.int32(block % blocks_all)
        if pieces == 1:
            return block
        return ((block // per_piece) ^ index_ref[0]) * per_piece + block % per_piece

    return place


def forward_kernel(first, heads, head_dim, draws, pieces, unroll, random_ref, index_ref, q_ref, k_ref, v_ref, o_ref):
    blocks_all = q_ref.shape[0] // BLOCK
    scaling = head_dim**-0.5
    place = placer(index_ref, blocks_all, pieces)

    def attend(queries, keys, values):
        stacked = stack_heads(scale_low(queries, scaling), heads, head_dim)
        probs = probabilities(keys, stacked).astype(BF16)
        return unstack_heads(dot(probs, values, TN), heads, head_dim).astype(BF16)

    def middle(step, carry):
        fixed, drawn = table_of(random_ref, place, step, first, heads, draws)
        keys = near_rows(k_ref, fixed, drawn, heads, head_dim)
        values = near_rows(v_ref, fixed, drawn, heads, head_dim)
        at = block_rows(fixed[2])
        o_ref[at, :] = attend(q_ref[at, :], keys, values)
        return carry

    lax.fori_loop(0, blocks_all - 2, middle, 0, unroll=unroll)
    for end in (0, -1):
        at = block_rows(place(end))
        o_ref[at, :] = attend(q_ref[at, :], k_ref[...], v_ref[...])


def backward_kernel(
    first,
    heads,
    head_dim,
    draws,
    pieces,
    unroll,
    random_ref,
    index_ref,
    q_ref,
    k_ref,
    v_ref,
    *refs,
):
    parts = len(refs) - 8
    grad_refs, out_ref = refs[:parts], refs[parts]
    g_ref, k_near, v_near, k_drawn, v_drawn, k_ends, v_ends = refs[parts + 1 :]
    width = q_ref.shape[1]
    rows = g_ref.shape[0] // parts
    for n, ref in enumerate(grad_refs):
        g_ref[n * rows : (n + 1) * rows, :] = ref[...]
    blocks_all = q_ref.shape[0] // BLOCK
    scaling = head_dim**-0.5
    place = placer(index_ref, blocks_all, pieces)
    owner = lax.broadcasted_iota(jnp.int32, (BLOCK, q_ref.shape[1]), 1) // head_dim
    for ref in (k_drawn, v_drawn, k_ends, v_ends):
        ref[...] = jnp.zeros_like(ref)

    def back(queries, grads, keys, values):
        q_stack = stack_heads(scale_low(queries, scaling), heads, head_dim)
        g_stack = stack_heads(grads, heads, head_dim)
        probs = probabilities(keys, q_stack)
        grad_probs = dot(values, g_stack, NT)
        center = jnp.sum(probs * grad_probs, axis=0, keepdims=True)
        grad_scores = (probs * (grad_probs - center)).astype(BF16)
        grad_keys = dot(grad_scores, q_stack, NN)
        grad_values = dot(probs.astype(BF16), g_stack, NN)
        grad_queries = unstack_heads(dot(grad_scores, keys, TN), heads, head_dim) * scaling
        return grad_queries.astype(BF16), grad_keys, grad_values

    for number, end in enumerate((0, -1)):
        at = block_rows(place(end))
        dq, dk, dv = back(q_ref[at, :], g_ref[at, :], k_ref[...], v_ref[...])
        out_ref[at, 0:width] = dq
        if number == 0:
            k_near[...] = dk
            v_near[...] = dv
        else:
            k_near[...] += dk
            v_near[...] += dv

    def middle(step, carry):
        fixed, drawn = table_of(random_ref, place, step, first, heads, draws)
        keys = near_rows(k_ref, fixed, drawn, heads, head_dim)
        values = near_rows(v_ref, fixed, drawn, heads, head_dim)
        at = block_rows(fixed[2])
        dq, dk, dv = back(q_ref[at, :], g_ref[at, :], keys, values)
        out_ref[at, 0:width] = dq
        for part, near, far, ends in ((dk, k_near, k_drawn, k_ends), (dv, v_near, v_drawn, v_ends)):
            ends[0:BLOCK, :] += part[0:BLOCK]
            ends[BLOCK:, :] += part[4 * BLOCK : 5 * BLOCK]
            if pieces == 1:
                window = pl.ds(pl.multiple_of(step * BLOCK, BLOCK), 3 * BLOCK)
                near[window, :] += part[BLOCK : 4 * BLOCK]
            else:
                for n in range(1, 4):
                    near[block_rows(fixed[n]), :] += part[n * BLOCK : (n + 1) * BLOCK]
            for j in range(draws):
                block = part[(5 + j) * BLOCK : (6 + j) * BLOCK]
                for h in range(heads):
                    kept = block if heads == 1 else jnp.where(owner == h, block, 0.0)
                    far[block_rows(drawn[j][h]), :] += kept
        return carry

    lax.fori_loop(0, blocks_all - 2, middle, 0, unroll=unroll)
    for n, near, far, ends in ((1, k_near, k_drawn, k_ends), (2, v_near, v_drawn, v_ends)):
        near[block_rows(place(0)), :] += ends[0:BLOCK, :]
        near[block_rows(place(-1)), :] += ends[BLOCK:, :]
        out_ref[:, n * width : (n + 1) * width] = (near[...] + far[...]).astype(BF16)


def attention_call(kernel, unroll, project, group, groups, grads, table, index, pieces):
    seq_rows = project.shape[0]
    width = project.shape[1] // (3 * groups)
    heads = table.shape[0] // groups
    draws = table.shape[1] // (seq_rows // BLOCK - 2)
    head_dim = width // heads
    narrow = width % 128 != 0
    first = 3 * group * width
    if narrow:
        operands = [project[:, first + n * width : first + (n + 1) * width] for n in range(3)]
    else:
        operands = [project] * 3

    def spec(part):
        column = 0 if narrow else part
        return pl.BlockSpec((seq_rows, width), lambda g, *refs: (0, column))

    columns = width * (3 if grads else 1)
    total = pltpu.VMEM((seq_rows, width), F32)
    ends = pltpu.VMEM((2 * BLOCK, width), F32)
    return pl.pallas_call(
        functools.partial(kernel, group * heads, heads, head_dim, draws, pieces, unroll),
        grid_spec=pltpu.PrefetchScalarGridSpec(
            num_scalar_prefetch=2,
            grid=(1,),
            in_specs=[spec(3 * group), spec(3 * group + 1), spec(3 * group + 2)]
            + [pl.BlockSpec(g.shape, lambda g, *refs: (0, 0)) for g in grads],
            out_specs=pl.BlockSpec((seq_rows, columns), lambda g, *refs: (0, 0)),
            scratch_shapes=[pltpu.VMEM((seq_rows, width), BF16)] + [total] * 4 + [ends] * 2
            if grads
            else [],
        ),
        out_shape=jax.ShapeDtypeStruct((seq_rows, columns), BF16),
        compiler_params=pltpu.CompilerParams(vmem_limit_bytes=VMEM_LIMIT),
        cost_estimate=cost(5) if grads else CHEAP,
    )(
        table,
        index,
        *operands,
        *grads,
    )


def call(kernel, grid, in_specs, out_specs, out_shape, operands, estimate=CHEAP, limit=16):
    return pl.pallas_call(
        kernel,
        grid=grid,
        in_specs=in_specs,
        out_specs=out_specs,
        out_shape=out_shape,
        compiler_params=pltpu.CompilerParams(vmem_limit_bytes=limit << 20),
        cost_estimate=estimate,
    )(*operands)


def whole(array):
    shape = array if isinstance(array, tuple) else array.shape
    return pl.BlockSpec(shape, lambda i: (0,) * len(shape))


def row_tiles(tile, columns, column=0):
    return pl.BlockSpec((tile, columns), lambda i: (i, column))


def piece_tiles(number, tiles, tile, columns):
    return pl.BlockSpec((tile, columns), lambda i: (jnp.clip(i - number * tiles, 0, tiles - 1), 0))


def chosen(refs, tiles):
    which = pl.program_id(0) // tiles
    value = refs[0][...]
    for n in range(1, len(refs)):
        value = jnp.where(which == n, refs[n][...], value)
    return value


def store_chosen(refs, tiles, value):
    for n, ref in enumerate(refs):

        @pl.when(pl.program_id(0) // tiles == n)
        def _(ref=ref):
            ref[...] = value.astype(ref.dtype)


def folded(value):
    rows, columns = value.shape
    return jnp.sum(value.reshape(rows // 8, 8, columns), axis=0)


def normalize(values):
    center = jnp.mean(values, axis=1, keepdims=True)
    spread = values - center
    variance = jnp.mean(spread * spread, axis=1, keepdims=True)
    inverse = lax.rsqrt(variance + EPS_NORM)
    return spread * inverse, inverse


def norm_kernel(x_ref, gain_ref, shift_ref, h_ref):
    normal, _ = normalize(x_ref[...].astype(F32))
    h_ref[...] = (normal * gain_ref[...] + shift_ref[...]).astype(BF16)


def norm_call(values, gain, shift):
    rows, model = values.shape
    tile = min(128, rows)
    return call(
        norm_kernel,
        (rows // tile,),
        [row_tiles(tile, model), whole((1, model)), whole((1, model))],
        row_tiles(tile, model),
        jax.ShapeDtypeStruct((rows, model), BF16),
        (values, gain.reshape(1, model), shift.reshape(1, model)),
    )


def residual_norm_kernel(own_ref, got_ref, gain_ref, shift_ref, r_ref, h_ref):
    values = own_ref[...] + got_ref[...].astype(F32)
    r_ref[...] = values
    normal, _ = normalize(values)
    h_ref[...] = (normal * gain_ref[...] + shift_ref[...]).astype(BF16)


def residual_norm_call(own, got, gain, shift):
    rows, model = own.shape
    tile = min(128, rows)
    tiles = row_tiles(tile, model)
    return call(
        residual_norm_kernel,
        (rows // tile,),
        [tiles, tiles, whole((1, model)), whole((1, model))],
        [tiles, tiles],
        [jax.ShapeDtypeStruct((rows, model), F32), jax.ShapeDtypeStruct((rows, model), BF16)],
        (own, got, gain.reshape(1, model), shift.reshape(1, model)),
    )


def norm_back_kernel(count, x_ref, base_ref, gain_ref, *refs):
    grad_ref, gain_sum, shift_sum = refs[count : count + 3]
    more = refs[count + 3 :]

    @pl.when(pl.program_id(0) == 0)
    def _():
        for ref in (gain_sum, shift_sum, *more[:1]):
            ref[...] = jnp.zeros_like(ref)

    grad_norm = refs[0][...].astype(F32)
    for ref in refs[1:count]:
        grad_norm = grad_norm + ref[...].astype(F32)
    normal, inverse = normalize(x_ref[...].astype(F32))
    base = base_ref[...].astype(F32)
    scaled = grad_norm * gain_ref[...]
    mean_plain = jnp.mean(scaled, axis=1, keepdims=True)
    mean_normal = jnp.mean(scaled * normal, axis=1, keepdims=True)
    grad = base + inverse * (scaled - mean_plain - normal * mean_normal)
    grad_ref[...] = grad
    gain_sum[...] += folded(grad_norm * normal)
    shift_sum[...] += folded(grad_norm)
    if more:
        more[0][...] += folded(base)
        more[1][...] = grad.astype(BF16)


def norm_back_call(values, base, gain, grads, more=False):
    rows, model = values.shape
    tile = min(128, rows)
    tiles = row_tiles(tile, model)
    sums = jax.ShapeDtypeStruct((8, model), F32)
    result = jax.ShapeDtypeStruct((rows, model), F32)
    low = jax.ShapeDtypeStruct((rows, model), BF16)
    return call(
        functools.partial(norm_back_kernel, len(grads)),
        (rows // tile,),
        [tiles, tiles, whole((1, model))] + [tiles] * len(grads),
        [tiles] + [whole((8, model))] * 2 + ([whole((8, model)), tiles] if more else []),
        [result, sums, sums] + ([sums, low] if more else []),
        (values, base, gain.reshape(1, model), *grads),
    )


def pack_kernel(groups, width, qkv_ref, out_ref, up_ref, down_ref, attn_ref, ffn_ref):
    attn = groups * width
    for g in range(groups):
        for c in range(3):
            at = (3 * g + c) * width
            attn_ref[:, at : at + width] = qkv_ref[c, :, g * width : (g + 1) * width].astype(BF16)
    attn_ref[:, 3 * attn :] = out_ref[...].T.astype(BF16)
    hidden = up_ref.shape[1]
    ffn_ref[:, :hidden] = up_ref[...].astype(BF16)
    ffn_ref[:, hidden:] = down_ref[...].T.astype(BF16)


def pack(weights, groups, width):
    w_qkv, w_out, w_up, w_down = weights
    _, shard, attn = w_qkv.shape
    hidden = w_up.shape[1]
    if width % 128 or shard % 128 or hidden % 128:
        qkv = w_qkv.astype(BF16).reshape(3, shard, groups, width).transpose(1, 2, 0, 3)
        return (
            jnp.concatenate([qkv.reshape(shard, 3 * attn), w_out.astype(BF16).T], axis=1),
            jnp.concatenate([w_up.astype(BF16), w_down.astype(BF16).T], axis=1),
        )
    outs = [
        jax.ShapeDtypeStruct((shard, 4 * attn), BF16),
        jax.ShapeDtypeStruct((shard, 2 * hidden), BF16),
    ]
    return call(
        functools.partial(pack_kernel, groups, width),
        (1,),
        [whole(w) for w in weights],
        [whole(o.shape) for o in outs],
        outs,
        weights,
    )


def qkv_kernel(tiles, *refs):
    w_ref, o_ref = refs[-2:]
    o_ref[...] = dot(chosen(refs[:-2], tiles), w_ref[...], NN).astype(BF16)


def qkv_call(pieces, weights, columns):
    rows, model = pieces[0].shape
    tile = min(256, rows)
    tiles = rows // tile
    count = len(pieces)
    return call(
        functools.partial(qkv_kernel, tiles),
        (count * tiles,),
        [piece_tiles(n, tiles, tile, model) for n in range(count)] + [whole((model, columns))],
        row_tiles(tile, columns),
        jax.ShapeDtypeStruct((count * rows, columns), BF16),
        (*pieces, weights),
    )


def branch_kernel(tiles, groups, x_ref, *refs):
    outs, gots = refs[:groups], refs[groups : 2 * groups]
    near_ref, far_ref, own_ref, other_ref = refs[2 * groups :]

    def joined(parts):
        return jnp.concatenate([p[...] for p in parts], axis=1) if groups > 1 else parts[0][...]

    value = dot(joined(outs), near_ref[...], NT) + dot(joined(gots), far_ref[...], NT)
    step = pl.program_id(0)

    @pl.when(step < tiles)
    def _():
        own_ref[...] = value + x_ref[...].astype(F32)

    @pl.when(step >= tiles)
    def _():
        other_ref[...] = value.astype(BF16)


def branch_call(tokens, outs, gots, attn_low, out_far):
    rows, model = tokens.shape
    attn = out_far.shape[1]
    groups = len(outs)
    width = attn // groups
    tile = min(256, rows)
    tiles = rows // tile
    return call(
        functools.partial(branch_kernel, tiles, groups),
        (2 * tiles,),
        [piece_tiles(0, tiles, tile, model)]
        + [row_tiles(tile, width)] * (2 * groups)
        + [pl.BlockSpec((model, attn), lambda i: (0, 3)), whole(out_far)],
        [piece_tiles(0, tiles, tile, model), piece_tiles(1, tiles, tile, model)],
        [jax.ShapeDtypeStruct((rows, model), F32), jax.ShapeDtypeStruct((rows, model), BF16)],
        (tokens, *outs, *gots, attn_low, out_far),
    )


def gelu_parts(values):
    square = values * values
    curve = jnp.tanh(values * (GELU_SCALE + (GELU_SCALE * GELU_CUBE) * square))
    half = 0.5 + 0.5 * curve
    slope = half + (0.5 * values) * (1.0 - curve * curve) * (
        GELU_SCALE + (3.0 * GELU_SCALE * GELU_CUBE) * square
    )
    return values * half, slope


def ffn_kernel(tiles, count, *refs):
    h_refs, g_refs = refs[:count], refs[count : 2 * count]
    up_ref, down_ref, bias_ref, both_ref, sum_ref = refs[2 * count : 2 * count + 5]
    dh_refs = refs[2 * count + 5 :]
    hidden = up_ref.shape[1]

    @pl.when(pl.program_id(0) == 0)
    def _():
        sum_ref[...] = jnp.zeros_like(sum_ref)

    hidden_pre = dot(chosen(h_refs, tiles), up_ref[...], NN) + bias_ref[...]
    grad_active = dot(chosen(g_refs, tiles), down_ref[...], NN)
    active, slope = gelu_parts(hidden_pre)
    grad_hidden = (grad_active * slope).astype(BF16)
    both_ref[:, :hidden] = grad_hidden
    both_ref[:, hidden:] = active.astype(BF16)
    sum_ref[...] += folded(grad_hidden.astype(F32))
    store_chosen(dh_refs, tiles, dot(grad_hidden, up_ref[...], NT))


def ffn_call(normed, grads, ffn_low, bias):
    count = len(normed)
    rows, model = normed[0].shape
    hidden = ffn_low.shape[1] // 2
    tile = min(256, rows)
    tiles = rows // tile
    pieces = [piece_tiles(n, tiles, tile, model) for n in range(count)]
    both = jax.ShapeDtypeStruct((count * rows, 2 * hidden), BF16)
    return call(
        functools.partial(ffn_kernel, tiles, count),
        (count * tiles,),
        pieces
        + pieces
        + [
            pl.BlockSpec((model, hidden), lambda i: (0, 0)),
            pl.BlockSpec((model, hidden), lambda i: (0, 1)),
            whole((1, hidden)),
        ],
        [row_tiles(tile, 2 * hidden), whole((8, hidden))] + pieces,
        [both, jax.ShapeDtypeStruct((8, hidden), F32)]
        + [jax.ShapeDtypeStruct((rows, model), BF16)] * count,
        (*normed, *grads, ffn_low, ffn_low, bias.reshape(1, hidden)),
        limit=24,
    )


def row_piece(number, rows, columns):
    return pl.BlockSpec((rows, columns), lambda i: (number, 0))


def outer_kernel(count, rights_count, extras, *refs):
    lefts = refs[:count]
    at = count
    o_ref = refs[-1]
    column = 0
    for _ in range(rights_count):
        total = dot(lefts[0][...], refs[at][...], TN)
        for n in range(1, count):
            total = total + dot(lefts[n][...], refs[at + n][...], TN)
        at += count
        o_ref[:, column : column + total.shape[1]] = total.astype(BF16)
        column += total.shape[1]
    if extras:
        total = refs[at][...].astype(F32)
        for n in range(1, extras):
            total = total + refs[at + n][...].astype(F32)
        o_ref[:, column:] = total.astype(BF16)


def outer_sum(lefts, rights, extras=()):
    count = len(lefts)
    rows, model = lefts[0].shape
    tile = min(512, model)
    columns = sum(r.shape[1] for r in rights) + (extras[0].shape[1] if extras else 0)
    specs = [pl.BlockSpec((rows, tile), lambda i: (0, i))] * count
    operands = list(lefts)
    for right in rights:
        specs += [row_piece(n, rows, right.shape[1]) for n in range(count)]
        operands += [right] * count
    specs += [row_tiles(tile, e.shape[1]) for e in extras]
    return call(
        functools.partial(outer_kernel, count, len(rights), len(extras)),
        (model // tile,),
        specs,
        row_tiles(tile, columns),
        jax.ShapeDtypeStruct((model, columns), BF16),
        (*operands, *extras),
    )


def double_outer_kernel(count, steps, *refs):
    rights, o_ref = refs[2 * count : 3 * count], refs[3 * count]
    first = pl.program_id(0) < steps
    total = None
    for n in range(count):
        left = jnp.where(first, refs[n][...], refs[count + n][...])
        part = dot(left, rights[n][...], TN)
        total = part if total is None else total + part
    o_ref[...] = total.astype(BF16)


def double_outer_sum(lefts, other_lefts, rights):
    count = len(lefts)
    rows, model = lefts[0].shape
    columns = rights[0][0].shape[1] // 2
    tile = min(512, model)
    steps = model // tile

    def left_spec(which):
        return pl.BlockSpec(
            (rows, tile), lambda i: (0, jnp.clip(i - which * steps, 0, steps - 1))
        )

    def right_spec(block):
        return pl.BlockSpec((rows, columns), lambda i: (block, i // steps))

    return call(
        functools.partial(double_outer_kernel, count, steps),
        (2 * steps,),
        [left_spec(0)] * count + [left_spec(1)] * count + [right_spec(n) for _, n in rights],
        pl.BlockSpec((tile, columns), lambda i: (i % steps, i // steps)),
        jax.ShapeDtypeStruct((model, 2 * columns), BF16),
        (*lefts, *other_lefts, *(a for a, _ in rights)),
        limit=24,
    )


def head_grads_kernel(tiles, count, width, *refs):
    w_ref, outs = refs[count], refs[count + 1 :]
    value = dot(chosen(refs[:count], tiles), w_ref[...], NN).astype(BF16)
    for n, out in enumerate(outs):
        out[...] = value[:, n * width : (n + 1) * width]


def head_grads_call(pieces, weights, column, attn, groups):
    count = len(pieces)
    rows, model = pieces[0].shape
    width = attn // groups
    tile = min(256, rows)
    tiles = rows // tile
    return call(
        functools.partial(head_grads_kernel, tiles, count, width),
        (count * tiles,),
        [piece_tiles(n, tiles, tile, model) for n in range(count)]
        + [pl.BlockSpec((model, attn), lambda i: (0, column))],
        [row_tiles(tile, width)] * groups,
        [jax.ShapeDtypeStruct((count * rows, width), BF16)] * groups,
        (*pieces, weights),
    )


def back_project_kernel(groups, tiles, *refs):
    w_ref, outs = refs[groups], refs[groups + 1 :]
    parts = [refs[n][...] for n in range(groups)]
    grads = jnp.concatenate(parts, axis=1) if groups > 1 else parts[0]
    store_chosen(outs, tiles, dot(grads, w_ref[...], NT))


def back_project(grads, weights, first, count, rows):
    groups = len(grads)
    columns = grads[0].shape[1]
    model = weights.shape[0]
    tile = min(256, rows)
    tiles = rows // tile
    return call(
        functools.partial(back_project_kernel, groups, tiles),
        (count * tiles,),
        [pl.BlockSpec((tile, columns), lambda i: (first * tiles + i, 0))] * groups
        + [whole((model, groups * columns))],
        [piece_tiles(n, tiles, tile, model) for n in range(count)],
        [jax.ShapeDtypeStruct((rows, model), BF16)] * count,
        (*grads, weights),
    )


def down_kernel(tiles, z_ref, w_ref, *outs):
    store_chosen(outs, tiles, dot(z_ref[...], w_ref[...], NT))


def down_call(both, ffn_low, count):
    model = ffn_low.shape[0]
    hidden = ffn_low.shape[1] // 2
    rows = both.shape[0] // count
    tile = min(256, rows)
    tiles = rows // tile
    return call(
        functools.partial(down_kernel, tiles),
        (count * tiles,),
        [
            pl.BlockSpec((tile, hidden), lambda i: (i, 1)),
            pl.BlockSpec((model, hidden), lambda i: (0, 1)),
        ],
        [piece_tiles(n, tiles, tile, model) for n in range(count)],
        [jax.ShapeDtypeStruct((rows, model), BF16)] * count,
        (both, ffn_low),
    )


def columns_of(refs, cuts):
    for matrix, (which, first, blocks) in enumerate(cuts):
        for n, at in enumerate(first if isinstance(first, tuple) else range(first, first + blocks)):
            yield matrix, n, refs[which][:, at * 128 : (at + 1) * 128].astype(F32)


def sums_kernel(cuts, grads_count, token_count, *refs):
    grads = refs[:grads_count]
    token_refs = refs[grads_count : grads_count + token_count]
    bias_refs = refs[grads_count + token_count : -2]
    across_ref, along_ref = refs[-2:]
    across_ref[...] = jnp.zeros_like(across_ref)
    totals = [None] * len(cuts)
    row = 0
    for matrix, _, value in columns_of(grads, cuts):
        square = value * value
        totals[matrix] = square if totals[matrix] is None else totals[matrix] + square
        along_ref[row : row + 1, :] = jnp.sum(square, axis=0, keepdims=True)
        row += 1
    for matrix, total in enumerate(totals):
        across_ref[matrix : matrix + 1, :] = jnp.sum(total.T, axis=0, keepdims=True)

    def store_rows(ref, row, value):
        for n in range(value.shape[1] // 128):
            ref[row + n : row + n + 1, :] = value[:, n * 128 : (n + 1) * 128]

    bias = bias_refs[0][...]
    for ref in bias_refs[1:]:
        bias = bias + ref[...]
    store_rows(along_ref, row, jnp.sum(bias, axis=0, keepdims=True))
    row = 8
    for ref in token_refs:
        value = jnp.sum(ref[...], axis=0, keepdims=True)
        store_rows(across_ref, row, value)
        row += value.shape[1] // 128


def join_kernel(matrices, across_ref, along_ref, o_ref):
    along_rows = along_ref.shape[0]
    token_rows = across_ref.shape[0] - 8
    o_ref[0:along_rows, :] = along_ref[...]
    o_ref[along_rows : along_rows + token_rows, :] = across_ref[8:, :]
    o_ref[along_rows + token_rows :, :] = jnp.broadcast_to(
        jnp.sum(across_ref[0:8, :], axis=1, keepdims=True), (8, 128)
    )


def step_kernel(cuts, grads_count, model, wide, *refs):
    grads = refs[:grads_count]
    across_ref, sums_ref, qkv_ref, out_ref, up_ref, down_ref = refs[grads_count : grads_count + 6]
    n_qkv, n_out, n_up, n_down, qkv_rows, qkv_cols = refs[grads_count + 6 : grads_count + 12]
    singles = refs[grads_count + 12 : grads_count + 18]
    copies = refs[grads_count + 18 :]
    totals_at = sums_ref.shape[0] - 8
    scales = []
    for matrix in range(len(cuts)):
        whole_mean = sums_ref[totals_at + matrix : totals_at + matrix + 1, :] / (
            model * wide[matrix]
        ) + EPS_FACTOR
        model_factor = (across_ref[matrix : matrix + 1, :] / wide[matrix] + EPS_FACTOR) / whole_mean
        if matrix < 3:
            qkv_rows[matrix : matrix + 1, :] = model_factor
        else:
            singles[matrix - 3][...] = model_factor
        scales.append((whole_mean, jnp.broadcast_to(model_factor, (128, 128)).T))
    row = 0
    for matrix, n, value in columns_of(grads, cuts):
        whole_mean, model_factor = scales[matrix]
        other_factor = (sums_ref[row : row + 1, :] / model + EPS_FACTOR) / whole_mean
        row += 1
        update = LEARN_RATE * (value * lax.rsqrt(model_factor * other_factor * whole_mean))
        at = slice(n * 128, (n + 1) * 128)
        if matrix < 3:
            n_qkv[matrix, :, at] = qkv_ref[matrix, :, at] - update
            qkv_cols[matrix : matrix + 1, at] = other_factor
            continue
        singles[matrix][n : n + 1, :] = other_factor
        if matrix == 3:
            n_out[at, :] = out_ref[at, :] - update.T
        elif matrix == 4:
            n_up[:, at] = up_ref[:, at] - update
        else:
            n_down[at, :] = down_ref[at, :] - update.T
    for ref in copies:
        count = ref.shape[0]
        ref[...] = sums_ref[row : row + count, :]
        row += count


def step_tail(dp_size, mp_size, attn_grads, ffn_grads, weights, token_sums, bias_sums, groups):
    w_qkv, w_out, w_up, w_down = weights
    shard, attn = w_qkv.shape[1:]
    hidden = w_up.shape[1]
    model = shard * dp_size
    per_group = attn // groups // 128
    attn_blocks, hidden_blocks = attn // 128, hidden // 128
    joined = jnp.concatenate([g[:, : 3 * attn // groups] for g in attn_grads], axis=1)
    grads = [joined, attn_grads[0], ffn_grads]
    cuts = [
        (
            0,
            tuple(
                (3 * g + c) * per_group + n for g in range(groups) for n in range(per_group)
            ),
            0,
        )
        for c in range(3)
    ]
    cuts += [
        (1, 3 * per_group, attn_blocks),
        (2, 0, hidden_blocks),
        (2, hidden_blocks, hidden_blocks),
    ]
    rows = 4 * attn_blocks + 2 * hidden_blocks
    bias_rows = hidden_blocks
    token_rows = len(token_sums) * model // 128

    def square(count):
        return jax.ShapeDtypeStruct((count, 128), F32)

    operands = (*grads, *token_sums, *bias_sums)
    across, along = call(
        functools.partial(sums_kernel, cuts, len(grads), len(token_sums)),
        (1,),
        [whole(a) for a in operands],
        [whole((8 + token_rows, 128)), whole((rows + bias_rows, 128))],
        [square(8 + token_rows), square(rows + bias_rows)],
        operands,
    )
    across = butterfly(across, "mp", mp_size)
    count = rows + bias_rows + token_rows + 8
    sums = call(
        functools.partial(join_kernel, len(cuts)),
        (1,),
        [whole(across), whole(along)],
        whole((count, 128)),
        square(count),
        (across, along),
    )
    sums = butterfly(sums, "dp", dp_size)
    wide = [attn * mp_size] * 4 + [hidden * mp_size] * 2
    operands = (*grads, across, sums, *weights)
    outs = [jax.ShapeDtypeStruct(w.shape, F32) for w in weights]
    outs += [jax.ShapeDtypeStruct((3, shard), F32), jax.ShapeDtypeStruct((3, attn), F32)]
    outs += [square(1)] * 3 + [square(attn_blocks), square(hidden_blocks), square(hidden_blocks)]
    outs += [square(bias_rows)] + [square(model // 128)] * len(token_sums)
    new_qkv, new_out, new_up, new_down, qkv_rows, qkv_cols, *rest = call(
        functools.partial(step_kernel, cuts, len(grads), model, wide),
        (1,),
        [whole(a) for a in operands],
        [whole(o.shape) for o in outs],
        outs,
        operands,
    )
    rest = [r.reshape(-1) for r in rest]
    return (
        (new_qkv, qkv_rows, qkv_cols),
        (new_out, rest[3], rest[0]),
        (new_up, rest[1], rest[4]),
        (new_down, rest[5], rest[2]),
        rest[7:],
        rest[6],
    )


def step_plain(dp_size, mp_size, attn_grads, ffn_grads, weights, token_sums, bias_sums, groups):
    w_qkv, w_out, w_up, w_down = weights
    shard, attn = w_qkv.shape[1:]
    hidden = w_up.shape[1]
    model = shard * dp_size
    width = attn // groups
    qkv = jnp.stack([g[:, : 3 * width].reshape(shard, 3, width) for g in attn_grads], axis=1)
    shards = [qkv[:, :, n].reshape(shard, attn) for n in range(3)] + [
        attn_grads[0][:, 3 * width :],
        ffn_grads[:, :hidden].astype(F32),
        ffn_grads[:, hidden:].astype(F32),
    ]
    squares = [g * g for g in shards]
    across = butterfly(
        jnp.concatenate(
            [jnp.sum(s, axis=1) for s in squares] + [jnp.sum(t, axis=0) for t in token_sums]
        ),
        "mp",
        mp_size,
    )
    model_sums = [across[n * shard : (n + 1) * shard] for n in range(6)]
    totals = jnp.stack([jnp.sum(s) for s in model_sums])
    sums = butterfly(
        jnp.concatenate(
            [jnp.sum(s, axis=0) for s in squares]
            + [across[6 * shard :], jnp.sum(sum(bias_sums), axis=0), totals]
        ),
        "dp",
        dp_size,
    )
    cuts = []
    start = 0
    for length in [attn] * 4 + [hidden] * 2 + [model] * len(token_sums) + [hidden, 6]:
        cuts.append(sums[start : start + length])
        start += length
    steps = []
    for n in range(6):
        wide = (attn if n < 4 else hidden) * mp_size
        whole_mean = cuts[-1][n] / (model * wide) + EPS_FACTOR
        model_factor = (model_sums[n] / wide + EPS_FACTOR) / whole_mean
        other_factor = (cuts[n] / model + EPS_FACTOR) / whole_mean
        update = shards[n] * lax.rsqrt(model_factor[:, None] * other_factor[None, :] * whole_mean)
        steps.append((LEARN_RATE * update, model_factor, other_factor))
    return (
        (
            w_qkv - jnp.stack([steps[n][0] for n in range(3)]),
            jnp.stack([steps[n][1] for n in range(3)]),
            jnp.stack([steps[n][2] for n in range(3)]),
        ),
        (w_out - steps[3][0].T, steps[3][2], steps[3][1]),
        (w_up - steps[4][0], steps[4][1], steps[4][2]),
        (w_down - steps[5][0].T, steps[5][2], steps[5][1]),
        cuts[6 : 6 + len(token_sums)],
        cuts[-2],
    )


def results(out_tokens, grad_tokens, step):
    qkv, out, up, down, token_sums, bias_sum = step
    return (
        out_tokens[None],
        grad_tokens[None],
        *qkv,
        *out,
        *up,
        *down,
        *token_sums[:4],
        bias_sum,
        token_sums[4],
    )


def body(
    dp_size,
    mp_size,
    tokens,
    cotangent,
    w_qkv,
    w_out,
    w_up,
    w_down,
    gain_attn,
    shift_attn,
    gain_ffn,
    shift_ffn,
    bias_up,
    bias_down,
    random_blocks,
):
    weights = (w_qkv, w_out, w_up, w_down)
    own_tokens, grad_top = tokens[0], cotangent[0]
    random_rows = random_blocks[0].reshape(random_blocks.shape[1], -1)
    index = lax.axis_index("mp").astype(jnp.int32).reshape(1)
    shard, attn = w_qkv.shape[1:]
    own_rows, model = own_tokens.shape
    width = min(128, attn)
    groups = attn // width
    low_attn, low_ffn = pack(weights, groups, width)
    if mp_size == 4 and dp_size == 8 and width == 128:
        arrange = paired_layer
    else:
        arrange = plain_layer
    out_tokens, grad_tokens, attn_grads, ffn_grads, token_sums, bias_sums = arrange(
        dp_size,
        mp_size,
        own_tokens,
        grad_top,
        random_rows,
        index,
        low_attn,
        low_ffn,
        (gain_attn, shift_attn, gain_ffn, shift_ffn),
        bias_up,
        bias_down,
        groups,
        width,
    )
    aligned = width == 128 and shard == 128 and w_up.shape[1] % 128 == 0
    step = (step_tail if aligned else step_plain)(
        dp_size, mp_size, attn_grads, ffn_grads, weights, token_sums, bias_sums, groups
    )
    return results(out_tokens, grad_tokens, step)


def paired_layer(
    dp_size,
    mp_size,
    tokens,
    grad_top,
    random_rows,
    index,
    low_attn,
    low_ffn,
    norms,
    bias_up,
    bias_down,
    groups,
    width,
):
    gain_attn, shift_attn, gain_ffn, shift_ffn = norms
    rows, model = tokens.shape
    attn = groups * width
    mine = lax.axis_index("dp")
    index_rows = gain_attn.reshape(8, -1)

    def other_core(value):
        return swap(value, 1, mp_size)

    def other_chip(value):
        return swap(value, 2, mp_size)

    places = [(mine + 2 * n) % dp_size for n in (0, 1, 3, 2)]
    places += [p ^ 1 for p in places]

    def levels_of(low):
        above = shifted(low, -2, dp_size)
        below = shifted(low, 2, dp_size)
        return [low, above, below, shifted(above, -2, dp_size)]

    def between_x(value):
        return swap(value, 1, dp_size, "dp")

    def fence(value, *others):
        return after(value, other_core(after(index_rows, *others)))

    normed = norm_call(tokens, gain_attn, shift_attn)
    normed = norm_call(tokens, gain_attn, shift_attn)
    normed_near = other_core(normed)
    far = other_chip(normed)
    attn_levels = levels_of(after(low_attn, normed))
    attn_swapped = [between_x(level) for level in attn_levels[:3]]
    attn_swapped.append(between_x(after(attn_levels[3], far)))
    ffn_low = lax.all_gather(
        after(low_ffn, far, attn_levels[3], *attn_swapped[:3]), "dp", axis=0, tiled=True
    )

    normed_pieces = [normed, normed_near, far, other_core(far)]
    top_far = other_chip(after(grad_top, far))
    top_near = other_core(grad_top)
    attn_low = assemble(attn_levels + attn_swapped, places)
    project = qkv_call(normed_pieces, after(attn_low, random_rows), 3 * attn)
    out_own = attn_low[:, 3 * attn :]
    out_far = other_chip(after(out_own, far))

    heads_out, heads_got = [], []
    for group in range(groups):
        if group == groups - 1:
            project = after(project, top_far)
        heads_out.append(
            attention_call(
                forward_kernel, 15, project, group, groups, (), random_rows, index, mp_size
            )
        )
        heads_got.append(other_chip(heads_out[-1][2 * rows :]))
    own, other = branch_call(
        tokens, heads_out, heads_got, attn_low, out_far
    )
    middle, second = residual_norm_call(own, other_core(other), gain_ffn, shift_ffn)

    second_far = other_chip(second)
    second_near = other_core(second)
    both_near, bias_near, back_own, back_near = ffn_call(
        [second, second_near], [grad_top, top_near], ffn_low, bias_up
    )
    second_far = after(second_far, back_own)
    second_last = other_core(second_far)
    top_last = other_core(top_far)
    both_far, bias_far, back_far, back_last = ffn_call(
        [second_far, second_last], [top_far, top_last], ffn_low, bias_up
    )
    crossing = (back_far.astype(F32) + other_core(back_last).astype(F32)).astype(BF16)
    crossed = other_chip(crossing)
    back_got = other_core(back_near)
    ffn_grads = double_outer_sum(
        [after(second, crossing), second_near, second_far, second_last],
        [grad_top, top_near, top_far, top_last],
        [(both_near, 0), (both_near, 1), (both_far, 0), (both_far, 1)],
    )
    down_far, down_last = down_call(after(both_far, ffn_grads), ffn_low, 2)
    crossed = after(crossed, ffn_grads, down_far)
    ffn_shard = lax.psum_scatter(
        after(ffn_grads, crossed), "dp", scatter_dimension=0, tiled=True
    )
    grad_middle, gain_two, shift_two, top_sum, grad_branch = norm_back_call(
        middle, grad_top, gain_ffn, [back_own, back_got, crossed], True
    )

    branch_pieces = [grad_branch, other_core(grad_branch)]
    away = head_grads_call(branch_pieces, out_far, 0, attn, groups)
    came = [other_chip(a) for a in away]
    stay = list(head_grads_call(branch_pieces, out_own, 0, attn, groups))
    out_away = other_chip(
        outer_sum([after(grad_branch, *away, *stay), branch_pieces[1]], heads_got)
    )
    out_stay = outer_sum(branch_pieces, [h[: 2 * rows] for h in heads_out])
    down_crossing = (
        down_far.astype(F32) + other_core(after(down_last, *away)).astype(F32)
    ).astype(BF16)
    down_crossed = other_chip(after(down_crossing, came[0]))

    grad_projects = []
    project = after(project, down_crossing, out_stay)
    for group in range(groups):
        grad_projects.append(
            attention_call(
                backward_kernel,
                6,
                project,
                group,
                groups,
                (stay[group], came[group]),
                random_rows,
                index,
                mp_size,
            )
        )
        if group == 0:
            first_sum = outer_sum(normed_pieces, grad_projects[:1], (out_stay, out_away))
            kept, sent = scatter_model_split(first_sum, dp_size)
            project, kept, sent = lax.optimization_barrier((project, kept, sent))
            sums = [(kept, between_x(sent))]
    grad_projects[-1] = after(grad_projects[-1], sums[0][1], down_crossed)

    [back_far] = back_project(grad_projects, attn_low, 2, 1, rows)
    came_far = other_core(back_far)
    [back_last] = back_project(
        [after(grad_projects[0], back_far)] + grad_projects[1:], attn_low, 3, 1, rows
    )
    crossing = (back_last.astype(F32) + came_far.astype(F32)).astype(BF16)
    crossed = other_chip(crossing)
    late = [after(g, crossing) for g in grad_projects]
    attn_parts = [scatter_model_end(after(sums[0][0], crossing), sums[0][1], dp_size)]
    for group in range(1, groups):
        kept, sent = scatter_model_split(
            outer_sum(normed_pieces, late[group : group + 1]), dp_size
        )
        attn_parts.append(scatter_model_end(kept, between_x(sent), dp_size))
        late = [after(g, sent) for g in late]
    back_own, back_near = back_project(late, attn_low, 0, 2, rows)
    back_got = other_core(back_near)
    down_own, down_near = down_call(after(both_near, back_own), ffn_low, 2)
    crossed = other_core(after(crossed, *(p for parts in attn_parts for p in parts)))
    out_tokens = (
        middle
        + down_own.astype(F32)
        + other_core(down_near).astype(F32)
        + down_crossed.astype(F32)
        + bias_down
    ).astype(BF16)
    grad_tokens, gain_one, shift_one = norm_back_call(
        tokens, grad_middle, gain_attn, [back_own, back_got, after(crossed, out_tokens)]
    )
    attn_grads = [sum(p.astype(F32) for p in parts) for parts in attn_parts]
    token_sums = [gain_one, shift_one, gain_two, shift_two, top_sum]
    return out_tokens, grad_tokens, attn_grads, ffn_shard, token_sums, [bias_near, bias_far]


def plain_layer(
    dp_size,
    mp_size,
    tokens,
    grad_top,
    random_rows,
    index,
    low_attn,
    low_ffn,
    norms,
    bias_up,
    bias_down,
    groups,
    width,
):
    gain_attn, shift_attn, gain_ffn, shift_ffn = norms
    rows, model = tokens.shape
    attn = groups * width
    lines = [[core + 2 * n for n in range(mp_size // 2)] for core in range(2)]
    core = lax.axis_index("mp") % 2

    def gather(value, axis, along=0):
        return lax.all_gather(value, axis, axis=along, tiled=True)

    def other_core(value):
        return swap(value, 1, mp_size)

    def scattered(value):
        return lax.psum_scatter(value, "mp", scatter_dimension=0, tiled=True)

    def own_first(value):
        half = value.shape[0] // 2
        return jnp.where(core == 0, value, jnp.roll(value, half, axis=0))

    attn_low = gather(low_attn, "dp")
    ffn_low = gather(low_ffn, "dp")
    normed = gather(norm_call(tokens, gain_attn, shift_attn), "mp")
    top_full = gather(grad_top, "mp")
    project = qkv_call([normed], attn_low[:, : 3 * attn], 3 * attn)
    out_low = lax.all_gather(
        attn_low[:, 3 * attn :], "mp", axis=1, axis_index_groups=lines, tiled=True
    )
    heads_out = [
        attention_call(forward_kernel, 15, project, g, groups, (), random_rows, index, 1)
        for g in range(groups)
    ]
    moved = own_first(
        lax.all_to_all(
            jnp.concatenate(heads_out, axis=1), "mp", 0, 1, axis_index_groups=lines, tiled=True
        )
    )
    branch = dot(moved, out_low, NT)
    middle, second = residual_norm_call(
        tokens.astype(F32) + branch[:rows],
        other_core(branch[rows:].astype(BF16)),
        gain_ffn,
        shift_ffn,
    )
    second_full = gather(second, "mp")
    both, bias_sum, back = ffn_call([second_full], [top_full], ffn_low, bias_up)
    ffn_grads = double_outer_sum([second_full], [top_full], [(both, 0)])
    ffn_shard = lax.psum_scatter(ffn_grads, "dp", scatter_dimension=0, tiled=True)
    grad_middle, gain_two, shift_two, top_sum, grad_branch = norm_back_call(
        middle, grad_top, gain_ffn, [scattered(back)], True
    )
    branch_pair = jnp.concatenate([grad_branch, other_core(grad_branch)], axis=0)
    away = own_first(dot(branch_pair, out_low, NN).astype(BF16))
    away = lax.all_to_all(away, "mp", 1, 0, axis_index_groups=lines, tiled=True)
    out_grad = lax.psum_scatter(
        dot(branch_pair, moved, TN).astype(BF16),
        "mp",
        scatter_dimension=1,
        axis_index_groups=lines,
        tiled=True,
    )
    grad_projects = [
        attention_call(
            backward_kernel,
            6,
            project,
            g,
            groups,
            (away[:, g * width : (g + 1) * width],),
            random_rows,
            index,
            1,
        )
        for g in range(groups)
    ]
    attn_grads = [
        scatter_model(
            outer_sum([normed], [g], (out_grad,) if n == 0 else ()), dp_size
        )
        for n, g in enumerate(grad_projects)
    ]
    back = sum(
        dot(g, attn_low[:, 3 * n * width : 3 * (n + 1) * width], NT)
        for n, g in enumerate(grad_projects)
    )
    grad_tokens, gain_one, shift_one = norm_back_call(
        tokens, grad_middle, gain_attn, [scattered(back.astype(BF16))]
    )
    down = scattered(down_call(both, ffn_low, 1)[0])
    out_tokens = (middle + down.astype(F32) + bias_down).astype(BF16)
    token_sums = [gain_one, shift_one, gain_two, shift_two, top_sum]
    return out_tokens, grad_tokens, attn_grads, ffn_shard, token_sums, [bias_sum]


def solution(mesh):
    placed = (
        P("dp", "mp", None),
        P("dp", "mp", None),
        P(None, "dp", "mp"),
        P("mp", "dp"),
        P("dp", "mp"),
        P("mp", "dp"),
        P(),
        P(),
        P(),
        P(),
        P("mp"),
        P(),
        P("dp", "mp", None, None),
    )
    return jax.shard_map(
        functools.partial(body, mesh.shape["dp"], mesh.shape["mp"]),
        mesh=mesh,
        in_specs=placed,
        out_specs=(
            P("dp", "mp", None),
            P("dp", "mp", None),
            P(None, "dp", "mp"),
            P(None, "dp"),
            P(None, "mp"),
            P("mp", "dp"),
            P("mp"),
            P("dp"),
            P("dp", "mp"),
            P("dp"),
            P("mp"),
            P("mp", "dp"),
            P("mp"),
            P("dp"),
            P(),
            P(),
            P(),
            P(),
            P("mp"),
            P(),
        ),
        check_vma=False,
    )
```

```python
import functools

import jax
import jax.numpy as jnp
from jax import lax
from jax.experimental import pallas as pl
from jax.experimental.pallas import tpu as pltpu
from jax.sharding import PartitionSpec as P

BLOCK = 64
EPS_NORM = 1e-05
EPS_FACTOR = 1e-30
LEARN_RATE = 0.1
GELU_SCALE = 0.7978845608028654
GELU_CUBE = 0.044715
F32 = jnp.float32
BF16 = jnp.bfloat16
NN = (((1,), (0,)), ((), ()))
NT = (((1,), (1,)), ((), ()))
TN = (((0,), (0,)), ((), ()))
VMEM_LIMIT = 24 << 20


def cost(microseconds):
    return pl.CostEstimate(flops=int(microseconds * 1.15e9), bytes_accessed=1 << 10, transcendentals=0)


CHEAP = cost(0.01)


def dot(left, right, form):
    return lax.dot_general(left, right, form, preferred_element_type=F32)


def swap(value, bit, size, axis="mp"):
    return lax.ppermute(value, axis, [(i, i ^ bit) for i in range(size)])


def after(value, *others):
    return lax.optimization_barrier((value, *others))[0]


def shifted(value, by, size):
    return lax.ppermute(value, "dp", [(i, (i + by) % size) for i in range(size)])


def scatter_model(partial, size):
    if size != 8:
        return lax.psum_scatter(partial, "dp", scatter_dimension=0, tiled=True).astype(F32)
    kept, sent = scatter_model_split(partial, size)
    return sum(p.astype(F32) for p in scatter_model_end(kept, swap(sent, 1, size, "dp"), size))


def scatter_model_split(partial, size):
    mine = lax.axis_index("dp")
    rows = partial.shape[0] // size
    columns = partial.shape[1]
    side = mine % 2
    split = partial.reshape(4, 2, rows, columns)

    def of_side(which):
        return lax.dynamic_slice(split, (0, which, 0, 0), (4, 1, rows, columns)).reshape(
            4, rows, columns
        )

    return of_side(side), of_side(1 - side)


def scatter_model_end(kept, got, size):
    level = lax.axis_index("dp") // 2
    rows, columns = kept.shape[1:]
    pair = (kept.astype(F32) + got.astype(F32)).astype(BF16)

    def of_level(which):
        return lax.dynamic_slice(pair, (which, 0, 0), (1, rows, columns))[0]

    parts = [shifted(of_level((level + n) % 4), 2 * n, size) for n in (1, 3, 2)]
    return [of_level(level)] + parts


def assemble_kernel(count, place_ref, *refs):
    rows = refs[0].shape[0]
    out_ref = refs[-1]
    if len(refs) > count + 1:
        out_ref[...] = refs[count][...]
    for n in range(count):
        at = pl.ds(pl.multiple_of(place_ref[n] * rows, rows), rows)
        out_ref[at, :] = refs[n][...]


def assemble(parts, places, total, base=None):
    count = len(parts)
    rows, columns = parts[0].shape
    tile = min(512, columns)
    whole_rows = pl.BlockSpec((total * rows, tile), lambda i: (0, i))
    return pl.pallas_call(
        functools.partial(assemble_kernel, count),
        grid=(columns // tile,),
        in_specs=[pl.BlockSpec(memory_space=pltpu.SMEM)]
        + [pl.BlockSpec((rows, tile), lambda i: (0, i))] * count
        + ([] if base is None else [whole_rows]),
        out_specs=whole_rows,
        out_shape=jax.ShapeDtypeStruct((total * rows, columns), parts[0].dtype),
        compiler_params=pltpu.CompilerParams(vmem_limit_bytes=16 << 20),
        cost_estimate=CHEAP,
    )(jnp.stack(places).astype(jnp.int32), *parts, *([] if base is None else [base]))


def butterfly(value, axis, size):
    bit = 1
    while bit < size:
        value = value + swap(value, bit, size, axis)
        bit *= 2
    return value


def stack_heads(block, heads, head_dim):
    if heads == 1:
        return block
    owner = lax.broadcasted_iota(jnp.int32, block.shape, 1) // head_dim
    zero = jnp.zeros_like(block)
    return jnp.concatenate([jnp.where(owner == h, block, zero) for h in range(heads)], axis=0)


def unstack_heads(stacked, heads, head_dim):
    if heads == 1:
        return stacked
    rows = stacked.shape[0] // heads
    owner = lax.broadcasted_iota(jnp.int32, (rows, stacked.shape[1]), 1) // head_dim
    result = stacked[:rows]
    for h in range(1, heads):
        result = jnp.where(owner >= h, stacked[h * rows : (h + 1) * rows], result)
    return result


def block_rows(place):
    return pl.ds(pl.multiple_of(place * BLOCK, BLOCK), BLOCK)


def near_rows(ref, fixed, drawn, heads, head_dim):
    parts = [ref[block_rows(place), :] for place in fixed]
    for places in drawn:
        block = ref[block_rows(places[0]), :]
        if heads > 1:
            owner = lax.broadcasted_iota(jnp.int32, block.shape, 1) // head_dim
            for h in range(1, heads):
                block = jnp.where(owner >= h, ref[block_rows(places[h]), :], block)
        parts.append(block)
    return jnp.concatenate(parts, axis=0)


def probabilities(keys, queries):
    scores = dot(keys, queries, NT)
    expanded = jnp.exp(scores - jnp.max(scores, axis=0, keepdims=True))
    return expanded * (1.0 / jnp.sum(expanded, axis=0, keepdims=True))


def scale_low(block, scaling):
    return (block.astype(F32) * scaling).astype(BF16)


def table_of(random_ref, place, step, first, heads, draws):
    fixed = [place(0), place(step), place(step + 1), place(step + 2), place(-1)]
    drawn = [
        [place(random_ref[first + h, step * draws + j]) for h in range(heads)]
        for j in range(draws)
    ]
    return fixed, drawn


def placer(index_ref, blocks_all, pieces):
    per_piece = blocks_all // pieces

    def place(block):
        if isinstance(block, int):
            block = jnp.int32(block % blocks_all)
        if pieces == 1:
            return block
        return ((block // per_piece) ^ index_ref[0]) * per_piece + block % per_piece

    return place


def forward_kernel(first, heads, head_dim, draws, pieces, unroll, random_ref, index_ref, q_ref, k_ref, v_ref, o_ref):
    blocks_all = q_ref.shape[0] // BLOCK
    scaling = head_dim**-0.5
    place = placer(index_ref, blocks_all, pieces)

    def attend(queries, keys, values):
        stacked = stack_heads(scale_low(queries, scaling), heads, head_dim)
        probs = probabilities(keys, stacked).astype(BF16)
        return unstack_heads(dot(probs, values, TN), heads, head_dim).astype(BF16)

    def middle(step, carry):
        fixed, drawn = table_of(random_ref, place, step, first, heads, draws)
        keys = near_rows(k_ref, fixed, drawn, heads, head_dim)
        values = near_rows(v_ref, fixed, drawn, heads, head_dim)
        at = block_rows(fixed[2])
        o_ref[at, :] = attend(q_ref[at, :], keys, values)
        return carry

    lax.fori_loop(0, blocks_all - 2, middle, 0, unroll=unroll)
    for end in (0, -1):
        at = block_rows(place(end))
        o_ref[at, :] = attend(q_ref[at, :], k_ref[...], v_ref[...])


def backward_kernel(
    first,
    heads,
    head_dim,
    draws,
    pieces,
    unroll,
    random_ref,
    index_ref,
    q_ref,
    k_ref,
    v_ref,
    *refs,
):
    parts = len(refs) - 8
    grad_refs, out_ref = refs[:parts], refs[parts]
    g_ref, k_near, v_near, k_drawn, v_drawn, k_ends, v_ends = refs[parts + 1 :]
    width = q_ref.shape[1]
    rows = g_ref.shape[0] // parts
    for n, ref in enumerate(grad_refs):
        g_ref[n * rows : (n + 1) * rows, :] = ref[...]
    blocks_all = q_ref.shape[0] // BLOCK
    scaling = head_dim**-0.5
    place = placer(index_ref, blocks_all, pieces)
    owner = lax.broadcasted_iota(jnp.int32, (BLOCK, q_ref.shape[1]), 1) // head_dim
    for ref in (k_drawn, v_drawn, k_ends, v_ends):
        ref[...] = jnp.zeros_like(ref)

    def back(queries, grads, keys, values):
        q_stack = stack_heads(scale_low(queries, scaling), heads, head_dim)
        g_stack = stack_heads(grads, heads, head_dim)
        probs = probabilities(keys, q_stack)
        grad_probs = dot(values, g_stack, NT)
        center = jnp.sum(probs * grad_probs, axis=0, keepdims=True)
        grad_scores = (probs * (grad_probs - center)).astype(BF16)
        grad_keys = dot(grad_scores, q_stack, NN)
        grad_values = dot(probs.astype(BF16), g_stack, NN)
        grad_queries = unstack_heads(dot(grad_scores, keys, TN), heads, head_dim) * scaling
        return grad_queries.astype(BF16), grad_keys, grad_values

    for number, end in enumerate((0, -1)):
        at = block_rows(place(end))
        dq, dk, dv = back(q_ref[at, :], g_ref[at, :], k_ref[...], v_ref[...])
        out_ref[at, 0:width] = dq
        if number == 0:
            k_near[...] = dk
            v_near[...] = dv
        else:
            k_near[...] += dk
            v_near[...] += dv

    def middle(step, carry):
        fixed, drawn = table_of(random_ref, place, step, first, heads, draws)
        keys = near_rows(k_ref, fixed, drawn, heads, head_dim)
        values = near_rows(v_ref, fixed, drawn, heads, head_dim)
        at = block_rows(fixed[2])
        dq, dk, dv = back(q_ref[at, :], g_ref[at, :], keys, values)
        out_ref[at, 0:width] = dq
        for part, near, far, ends in ((dk, k_near, k_drawn, k_ends), (dv, v_near, v_drawn, v_ends)):
            ends[0:BLOCK, :] += part[0:BLOCK]
            ends[BLOCK:, :] += part[4 * BLOCK : 5 * BLOCK]
            if pieces == 1:
                window = pl.ds(pl.multiple_of(step * BLOCK, BLOCK), 3 * BLOCK)
                near[window, :] += part[BLOCK : 4 * BLOCK]
            else:
                for n in range(1, 4):
                    near[block_rows(fixed[n]), :] += part[n * BLOCK : (n + 1) * BLOCK]
            for j in range(draws):
                block = part[(5 + j) * BLOCK : (6 + j) * BLOCK]
                for h in range(heads):
                    kept = block if heads == 1 else jnp.where(owner == h, block, 0.0)
                    far[block_rows(drawn[j][h]), :] += kept
        return carry

    lax.fori_loop(0, blocks_all - 2, middle, 0, unroll=unroll)
    for n, near, far, ends in ((1, k_near, k_drawn, k_ends), (2, v_near, v_drawn, v_ends)):
        near[block_rows(place(0)), :] += ends[0:BLOCK, :]
        near[block_rows(place(-1)), :] += ends[BLOCK:, :]
        out_ref[:, n * width : (n + 1) * width] = (near[...] + far[...]).astype(BF16)


def attention_call(kernel, unroll, project, group, groups, grads, table, index, pieces):
    seq_rows = project.shape[0]
    width = project.shape[1] // (3 * groups)
    heads = table.shape[0] // groups
    draws = table.shape[1] // (seq_rows // BLOCK - 2)
    head_dim = width // heads
    narrow = width % 128 != 0
    first = 3 * group * width
    if narrow:
        operands = [project[:, first + n * width : first + (n + 1) * width] for n in range(3)]
    else:
        operands = [project] * 3

    def spec(part):
        column = 0 if narrow else part
        return pl.BlockSpec((seq_rows, width), lambda g, *refs: (0, column))

    columns = width * (3 if grads else 1)
    total = pltpu.VMEM((seq_rows, width), F32)
    ends = pltpu.VMEM((2 * BLOCK, width), F32)
    return pl.pallas_call(
        functools.partial(kernel, group * heads, heads, head_dim, draws, pieces, unroll),
        grid_spec=pltpu.PrefetchScalarGridSpec(
            num_scalar_prefetch=2,
            grid=(1,),
            in_specs=[spec(3 * group), spec(3 * group + 1), spec(3 * group + 2)]
            + [pl.BlockSpec(g.shape, lambda g, *refs: (0, 0)) for g in grads],
            out_specs=pl.BlockSpec((seq_rows, columns), lambda g, *refs: (0, 0)),
            scratch_shapes=[pltpu.VMEM((seq_rows, width), BF16)] + [total] * 4 + [ends] * 2
            if grads
            else [],
        ),
        out_shape=jax.ShapeDtypeStruct((seq_rows, columns), BF16),
        compiler_params=pltpu.CompilerParams(vmem_limit_bytes=VMEM_LIMIT),
        cost_estimate=cost(5) if grads else CHEAP,
    )(
        table,
        index,
        *operands,
        *grads,
    )


def call(kernel, grid, in_specs, out_specs, out_shape, operands, estimate=CHEAP, limit=16):
    return pl.pallas_call(
        kernel,
        grid=grid,
        in_specs=in_specs,
        out_specs=out_specs,
        out_shape=out_shape,
        compiler_params=pltpu.CompilerParams(vmem_limit_bytes=limit << 20),
        cost_estimate=estimate,
    )(*operands)


def whole(array):
    shape = array if isinstance(array, tuple) else array.shape
    return pl.BlockSpec(shape, lambda i: (0,) * len(shape))


def row_tiles(tile, columns, column=0):
    return pl.BlockSpec((tile, columns), lambda i: (i, column))


def piece_tiles(number, tiles, tile, columns):
    return pl.BlockSpec((tile, columns), lambda i: (jnp.clip(i - number * tiles, 0, tiles - 1), 0))


def chosen(refs, tiles):
    which = pl.program_id(0) // tiles
    value = refs[0][...]
    for n in range(1, len(refs)):
        value = jnp.where(which == n, refs[n][...], value)
    return value


def store_chosen(refs, tiles, value):
    for n, ref in enumerate(refs):

        @pl.when(pl.program_id(0) // tiles == n)
        def _(ref=ref):
            ref[...] = value.astype(ref.dtype)


def folded(value):
    rows, columns = value.shape
    return jnp.sum(value.reshape(rows // 8, 8, columns), axis=0)


def normalize(values):
    center = jnp.mean(values, axis=1, keepdims=True)
    spread = values - center
    variance = jnp.mean(spread * spread, axis=1, keepdims=True)
    inverse = lax.rsqrt(variance + EPS_NORM)
    return spread * inverse, inverse


def norm_kernel(x_ref, gain_ref, shift_ref, h_ref):
    normal, _ = normalize(x_ref[...].astype(F32))
    h_ref[...] = (normal * gain_ref[...] + shift_ref[...]).astype(BF16)


def norm_call(values, gain, shift):
    rows, model = values.shape
    tile = min(128, rows)
    return call(
        norm_kernel,
        (rows // tile,),
        [row_tiles(tile, model), whole((1, model)), whole((1, model))],
        row_tiles(tile, model),
        jax.ShapeDtypeStruct((rows, model), BF16),
        (values, gain.reshape(1, model), shift.reshape(1, model)),
    )


def residual_norm_kernel(own_ref, got_ref, gain_ref, shift_ref, r_ref, h_ref):
    values = own_ref[...] + got_ref[...].astype(F32)
    r_ref[...] = values
    normal, _ = normalize(values)
    h_ref[...] = (normal * gain_ref[...] + shift_ref[...]).astype(BF16)


def residual_norm_call(own, got, gain, shift):
    rows, model = own.shape
    tile = min(128, rows)
    tiles = row_tiles(tile, model)
    return call(
        residual_norm_kernel,
        (rows // tile,),
        [tiles, tiles, whole((1, model)), whole((1, model))],
        [tiles, tiles],
        [jax.ShapeDtypeStruct((rows, model), F32), jax.ShapeDtypeStruct((rows, model), BF16)],
        (own, got, gain.reshape(1, model), shift.reshape(1, model)),
    )


def norm_back_kernel(count, x_ref, base_ref, gain_ref, *refs):
    grad_ref, gain_sum, shift_sum = refs[count : count + 3]
    more = refs[count + 3 :]

    @pl.when(pl.program_id(0) == 0)
    def _():
        for ref in (gain_sum, shift_sum, *more[:1]):
            ref[...] = jnp.zeros_like(ref)

    grad_norm = refs[0][...].astype(F32)
    for ref in refs[1:count]:
        grad_norm = grad_norm + ref[...].astype(F32)
    normal, inverse = normalize(x_ref[...].astype(F32))
    base = base_ref[...].astype(F32)
    scaled = grad_norm * gain_ref[...]
    mean_plain = jnp.mean(scaled, axis=1, keepdims=True)
    mean_normal = jnp.mean(scaled * normal, axis=1, keepdims=True)
    grad = base + inverse * (scaled - mean_plain - normal * mean_normal)
    grad_ref[...] = grad
    gain_sum[...] += folded(grad_norm * normal)
    shift_sum[...] += folded(grad_norm)
    if more:
        more[0][...] += folded(base)
        more[1][...] = grad.astype(BF16)


def norm_back_call(values, base, gain, grads, more=False):
    rows, model = values.shape
    tile = min(128, rows)
    tiles = row_tiles(tile, model)
    sums = jax.ShapeDtypeStruct((8, model), F32)
    result = jax.ShapeDtypeStruct((rows, model), F32)
    low = jax.ShapeDtypeStruct((rows, model), BF16)
    return call(
        functools.partial(norm_back_kernel, len(grads)),
        (rows // tile,),
        [tiles, tiles, whole((1, model))] + [tiles] * len(grads),
        [tiles] + [whole((8, model))] * 2 + ([whole((8, model)), tiles] if more else []),
        [result, sums, sums] + ([sums, low] if more else []),
        (values, base, gain.reshape(1, model), *grads),
    )


def pack_kernel(groups, width, qkv_ref, out_ref, up_ref, down_ref, attn_ref, ffn_ref):
    attn = groups * width
    for g in range(groups):
        for c in range(3):
            at = (3 * g + c) * width
            attn_ref[:, at : at + width] = qkv_ref[c, :, g * width : (g + 1) * width].astype(BF16)
    attn_ref[:, 3 * attn :] = out_ref[...].T.astype(BF16)
    hidden = up_ref.shape[1]
    ffn_ref[:, :hidden] = up_ref[...].astype(BF16)
    ffn_ref[:, hidden:] = down_ref[...].T.astype(BF16)


def pack(weights, groups, width):
    w_qkv, w_out, w_up, w_down = weights
    _, shard, attn = w_qkv.shape
    hidden = w_up.shape[1]
    if width % 128 or shard % 128 or hidden % 128:
        qkv = w_qkv.astype(BF16).reshape(3, shard, groups, width).transpose(1, 2, 0, 3)
        return (
            jnp.concatenate([qkv.reshape(shard, 3 * attn), w_out.astype(BF16).T], axis=1),
            jnp.concatenate([w_up.astype(BF16), w_down.astype(BF16).T], axis=1),
        )
    outs = [
        jax.ShapeDtypeStruct((shard, 4 * attn), BF16),
        jax.ShapeDtypeStruct((shard, 2 * hidden), BF16),
    ]
    return call(
        functools.partial(pack_kernel, groups, width),
        (1,),
        [whole(w) for w in weights],
        [whole(o.shape) for o in outs],
        outs,
        weights,
    )


def qkv_kernel(tiles, *refs):
    w_ref, o_ref = refs[-2:]
    o_ref[...] = dot(chosen(refs[:-2], tiles), w_ref[...], NN).astype(BF16)


def qkv_call(pieces, weights, columns):
    rows, model = pieces[0].shape
    tile = min(256, rows)
    tiles = rows // tile
    count = len(pieces)
    return call(
        functools.partial(qkv_kernel, tiles),
        (count * tiles,),
        [piece_tiles(n, tiles, tile, model) for n in range(count)] + [whole((model, columns))],
        row_tiles(tile, columns),
        jax.ShapeDtypeStruct((count * rows, columns), BF16),
        (*pieces, weights),
    )


def branch_kernel(tiles, groups, x_ref, *refs):
    outs, gots = refs[:groups], refs[groups : 2 * groups]
    near_ref, far_ref, own_ref, other_ref = refs[2 * groups :]

    def joined(parts):
        return jnp.concatenate([p[...] for p in parts], axis=1) if groups > 1 else parts[0][...]

    value = dot(joined(outs), near_ref[...], NT) + dot(joined(gots), far_ref[...], NT)
    step = pl.program_id(0)

    @pl.when(step < tiles)
    def _():
        own_ref[...] = value + x_ref[...].astype(F32)

    @pl.when(step >= tiles)
    def _():
        other_ref[...] = value.astype(BF16)


def branch_call(tokens, outs, gots, attn_low, out_far):
    rows, model = tokens.shape
    attn = out_far.shape[1]
    groups = len(outs)
    width = attn // groups
    tile = min(256, rows)
    tiles = rows // tile
    return call(
        functools.partial(branch_kernel, tiles, groups),
        (2 * tiles,),
        [piece_tiles(0, tiles, tile, model)]
        + [row_tiles(tile, width)] * (2 * groups)
        + [pl.BlockSpec((model, attn), lambda i: (0, 3)), whole(out_far)],
        [piece_tiles(0, tiles, tile, model), piece_tiles(1, tiles, tile, model)],
        [jax.ShapeDtypeStruct((rows, model), F32), jax.ShapeDtypeStruct((rows, model), BF16)],
        (tokens, *outs, *gots, attn_low, out_far),
    )


def gelu_parts(values):
    square = values * values
    curve = jnp.tanh(values * (GELU_SCALE + (GELU_SCALE * GELU_CUBE) * square))
    half = 0.5 + 0.5 * curve
    slope = half + (0.5 * values) * (1.0 - curve * curve) * (
        GELU_SCALE + (3.0 * GELU_SCALE * GELU_CUBE) * square
    )
    return values * half, slope


def ffn_kernel(tiles, count, *refs):
    h_refs, g_refs = refs[:count], refs[count : 2 * count]
    up_ref, down_ref, bias_ref, both_ref, sum_ref = refs[2 * count : 2 * count + 5]
    dh_refs = refs[2 * count + 5 :]
    hidden = up_ref.shape[1]

    @pl.when(pl.program_id(0) == 0)
    def _():
        sum_ref[...] = jnp.zeros_like(sum_ref)

    hidden_pre = dot(chosen(h_refs, tiles), up_ref[...], NN) + bias_ref[...]
    grad_active = dot(chosen(g_refs, tiles), down_ref[...], NN)
    active, slope = gelu_parts(hidden_pre)
    grad_hidden = (grad_active * slope).astype(BF16)
    both_ref[:, :hidden] = grad_hidden
    both_ref[:, hidden:] = active.astype(BF16)
    sum_ref[...] += folded(grad_hidden.astype(F32))
    store_chosen(dh_refs, tiles, dot(grad_hidden, up_ref[...], NT))


def ffn_call(normed, grads, ffn_low, bias):
    count = len(normed)
    rows, model = normed[0].shape
    hidden = ffn_low.shape[1] // 2
    tile = min(256, rows)
    tiles = rows // tile
    pieces = [piece_tiles(n, tiles, tile, model) for n in range(count)]
    both = jax.ShapeDtypeStruct((count * rows, 2 * hidden), BF16)
    return call(
        functools.partial(ffn_kernel, tiles, count),
        (count * tiles,),
        pieces
        + pieces
        + [
            pl.BlockSpec((model, hidden), lambda i: (0, 0)),
            pl.BlockSpec((model, hidden), lambda i: (0, 1)),
            whole((1, hidden)),
        ],
        [row_tiles(tile, 2 * hidden), whole((8, hidden))] + pieces,
        [both, jax.ShapeDtypeStruct((8, hidden), F32)]
        + [jax.ShapeDtypeStruct((rows, model), BF16)] * count,
        (*normed, *grads, ffn_low, ffn_low, bias.reshape(1, hidden)),
        limit=24,
    )


def row_piece(number, rows, columns):
    return pl.BlockSpec((rows, columns), lambda i: (number, 0))


def outer_kernel(count, rights_count, extras, *refs):
    lefts = refs[:count]
    at = count
    o_ref = refs[-1]
    column = 0
    for _ in range(rights_count):
        total = dot(lefts[0][...], refs[at][...], TN)
        for n in range(1, count):
            total = total + dot(lefts[n][...], refs[at + n][...], TN)
        at += count
        o_ref[:, column : column + total.shape[1]] = total.astype(BF16)
        column += total.shape[1]
    if extras:
        total = refs[at][...].astype(F32)
        for n in range(1, extras):
            total = total + refs[at + n][...].astype(F32)
        o_ref[:, column:] = total.astype(BF16)


def outer_sum(lefts, rights, extras=()):
    count = len(lefts)
    rows, model = lefts[0].shape
    tile = min(512, model)
    columns = sum(r.shape[1] for r in rights) + (extras[0].shape[1] if extras else 0)
    specs = [pl.BlockSpec((rows, tile), lambda i: (0, i))] * count
    operands = list(lefts)
    for right in rights:
        specs += [row_piece(n, rows, right.shape[1]) for n in range(count)]
        operands += [right] * count
    specs += [row_tiles(tile, e.shape[1]) for e in extras]
    return call(
        functools.partial(outer_kernel, count, len(rights), len(extras)),
        (model // tile,),
        specs,
        row_tiles(tile, columns),
        jax.ShapeDtypeStruct((model, columns), BF16),
        (*operands, *extras),
    )


def double_outer_kernel(count, steps, *refs):
    rights, o_ref = refs[2 * count : 3 * count], refs[3 * count]
    first = pl.program_id(0) < steps
    total = None
    for n in range(count):
        left = jnp.where(first, refs[n][...], refs[count + n][...])
        part = dot(left, rights[n][...], TN)
        total = part if total is None else total + part
    o_ref[...] = total.astype(BF16)


def double_outer_sum(lefts, other_lefts, rights):
    count = len(lefts)
    rows, model = lefts[0].shape
    columns = rights[0][0].shape[1] // 2
    tile = min(512, model)
    steps = model // tile

    def left_spec(which):
        return pl.BlockSpec(
            (rows, tile), lambda i: (0, jnp.clip(i - which * steps, 0, steps - 1))
        )

    def right_spec(block):
        return pl.BlockSpec((rows, columns), lambda i: (block, i // steps))

    return call(
        functools.partial(double_outer_kernel, count, steps),
        (2 * steps,),
        [left_spec(0)] * count + [left_spec(1)] * count + [right_spec(n) for _, n in rights],
        pl.BlockSpec((tile, columns), lambda i: (i % steps, i // steps)),
        jax.ShapeDtypeStruct((model, 2 * columns), BF16),
        (*lefts, *other_lefts, *(a for a, _ in rights)),
        limit=24,
    )


def head_grads_kernel(tiles, count, width, *refs):
    w_ref, outs = refs[count], refs[count + 1 :]
    value = dot(chosen(refs[:count], tiles), w_ref[...], NN).astype(BF16)
    for n, out in enumerate(outs):
        out[...] = value[:, n * width : (n + 1) * width]


def head_grads_call(pieces, weights, column, attn, groups):
    count = len(pieces)
    rows, model = pieces[0].shape
    width = attn // groups
    tile = min(256, rows)
    tiles = rows // tile
    return call(
        functools.partial(head_grads_kernel, tiles, count, width),
        (count * tiles,),
        [piece_tiles(n, tiles, tile, model) for n in range(count)]
        + [pl.BlockSpec((model, attn), lambda i: (0, column))],
        [row_tiles(tile, width)] * groups,
        [jax.ShapeDtypeStruct((count * rows, width), BF16)] * groups,
        (*pieces, weights),
    )


def back_project_kernel(groups, tiles, *refs):
    w_ref, outs = refs[groups], refs[groups + 1 :]
    parts = [refs[n][...] for n in range(groups)]
    grads = jnp.concatenate(parts, axis=1) if groups > 1 else parts[0]
    store_chosen(outs, tiles, dot(grads, w_ref[...], NT))


def back_project(grads, weights, first, count, rows):
    groups = len(grads)
    columns = grads[0].shape[1]
    model = weights.shape[0]
    tile = min(256, rows)
    tiles = rows // tile
    return call(
        functools.partial(back_project_kernel, groups, tiles),
        (count * tiles,),
        [pl.BlockSpec((tile, columns), lambda i: (first * tiles + i, 0))] * groups
        + [whole((model, groups * columns))],
        [piece_tiles(n, tiles, tile, model) for n in range(count)],
        [jax.ShapeDtypeStruct((rows, model), BF16)] * count,
        (*grads, weights),
    )


def down_kernel(tiles, z_ref, w_ref, *outs):
    store_chosen(outs, tiles, dot(z_ref[...], w_ref[...], NT))


def down_call(both, ffn_low, count):
    model = ffn_low.shape[0]
    hidden = ffn_low.shape[1] // 2
    rows = both.shape[0] // count
    tile = min(256, rows)
    tiles = rows // tile
    return call(
        functools.partial(down_kernel, tiles),
        (count * tiles,),
        [
            pl.BlockSpec((tile, hidden), lambda i: (i, 1)),
            pl.BlockSpec((model, hidden), lambda i: (0, 1)),
        ],
        [piece_tiles(n, tiles, tile, model) for n in range(count)],
        [jax.ShapeDtypeStruct((rows, model), BF16)] * count,
        (both, ffn_low),
    )


def columns_of(refs, cuts):
    for matrix, (which, first, blocks) in enumerate(cuts):
        for n, at in enumerate(first if isinstance(first, tuple) else range(first, first + blocks)):
            yield matrix, n, refs[which][:, at * 128 : (at + 1) * 128].astype(F32)


def sums_kernel(cuts, grads_count, token_count, *refs):
    grads = refs[:grads_count]
    token_refs = refs[grads_count : grads_count + token_count]
    bias_refs = refs[grads_count + token_count : -2]
    across_ref, along_ref = refs[-2:]
    across_ref[...] = jnp.zeros_like(across_ref)
    totals = [None] * len(cuts)
    row = 0
    for matrix, _, value in columns_of(grads, cuts):
        square = value * value
        totals[matrix] = square if totals[matrix] is None else totals[matrix] + square
        along_ref[row : row + 1, :] = jnp.sum(square, axis=0, keepdims=True)
        row += 1
    for matrix, total in enumerate(totals):
        across_ref[matrix : matrix + 1, :] = jnp.sum(total.T, axis=0, keepdims=True)

    def store_rows(ref, row, value):
        for n in range(value.shape[1] // 128):
            ref[row + n : row + n + 1, :] = value[:, n * 128 : (n + 1) * 128]

    bias = bias_refs[0][...]
    for ref in bias_refs[1:]:
        bias = bias + ref[...]
    store_rows(along_ref, row, jnp.sum(bias, axis=0, keepdims=True))
    row = 8
    for ref in token_refs:
        value = jnp.sum(ref[...], axis=0, keepdims=True)
        store_rows(across_ref, row, value)
        row += value.shape[1] // 128


def join_kernel(matrices, across_ref, along_ref, o_ref):
    along_rows = along_ref.shape[0]
    token_rows = across_ref.shape[0] - 8
    o_ref[0:along_rows, :] = along_ref[...]
    o_ref[along_rows : along_rows + token_rows, :] = across_ref[8:, :]
    o_ref[along_rows + token_rows :, :] = jnp.broadcast_to(
        jnp.sum(across_ref[0:8, :], axis=1, keepdims=True), (8, 128)
    )


def step_kernel(cuts, grads_count, model, wide, *refs):
    grads = refs[:grads_count]
    across_ref, sums_ref, qkv_ref, out_ref, up_ref, down_ref = refs[grads_count : grads_count + 6]
    n_qkv, n_out, n_up, n_down, qkv_rows, qkv_cols = refs[grads_count + 6 : grads_count + 12]
    singles = refs[grads_count + 12 : grads_count + 18]
    copies = refs[grads_count + 18 :]
    totals_at = sums_ref.shape[0] - 8
    scales = []
    for matrix in range(len(cuts)):
        whole_mean = sums_ref[totals_at + matrix : totals_at + matrix + 1, :] / (
            model * wide[matrix]
        ) + EPS_FACTOR
        model_factor = (across_ref[matrix : matrix + 1, :] / wide[matrix] + EPS_FACTOR) / whole_mean
        if matrix < 3:
            qkv_rows[matrix : matrix + 1, :] = model_factor
        else:
            singles[matrix - 3][...] = model_factor
        scales.append((whole_mean, jnp.broadcast_to(model_factor, (128, 128)).T))
    row = 0
    for matrix, n, value in columns_of(grads, cuts):
        whole_mean, model_factor = scales[matrix]
        other_factor = (sums_ref[row : row + 1, :] / model + EPS_FACTOR) / whole_mean
        row += 1
        update = LEARN_RATE * (value * lax.rsqrt(model_factor * other_factor * whole_mean))
        at = slice(n * 128, (n + 1) * 128)
        if matrix < 3:
            n_qkv[matrix, :, at] = qkv_ref[matrix, :, at] - update
            qkv_cols[matrix : matrix + 1, at] = other_factor
            continue
        singles[matrix][n : n + 1, :] = other_factor
        if matrix == 3:
            n_out[at, :] = out_ref[at, :] - update.T
        elif matrix == 4:
            n_up[:, at] = up_ref[:, at] - update
        else:
            n_down[at, :] = down_ref[at, :] - update.T
    for ref in copies:
        count = ref.shape[0]
        ref[...] = sums_ref[row : row + count, :]
        row += count


def step_tail(dp_size, mp_size, attn_grads, ffn_grads, weights, token_sums, bias_sums, groups):
    w_qkv, w_out, w_up, w_down = weights
    shard, attn = w_qkv.shape[1:]
    hidden = w_up.shape[1]
    model = shard * dp_size
    per_group = attn // groups // 128
    attn_blocks, hidden_blocks = attn // 128, hidden // 128
    joined = jnp.concatenate([g[:, : 3 * attn // groups] for g in attn_grads], axis=1)
    grads = [joined, attn_grads[0], ffn_grads]
    cuts = [
        (
            0,
            tuple(
                (3 * g + c) * per_group + n for g in range(groups) for n in range(per_group)
            ),
            0,
        )
        for c in range(3)
    ]
    cuts += [
        (1, 3 * per_group, attn_blocks),
        (2, 0, hidden_blocks),
        (2, hidden_blocks, hidden_blocks),
    ]
    rows = 4 * attn_blocks + 2 * hidden_blocks
    bias_rows = hidden_blocks
    token_rows = len(token_sums) * model // 128

    def square(count):
        return jax.ShapeDtypeStruct((count, 128), F32)

    operands = (*grads, *token_sums, *bias_sums)
    across, along = call(
        functools.partial(sums_kernel, cuts, len(grads), len(token_sums)),
        (1,),
        [whole(a) for a in operands],
        [whole((8 + token_rows, 128)), whole((rows + bias_rows, 128))],
        [square(8 + token_rows), square(rows + bias_rows)],
        operands,
    )
    across = butterfly(across, "mp", mp_size)
    count = rows + bias_rows + token_rows + 8
    sums = call(
        functools.partial(join_kernel, len(cuts)),
        (1,),
        [whole(across), whole(along)],
        whole((count, 128)),
        square(count),
        (across, along),
    )
    sums = butterfly(sums, "dp", dp_size)
    wide = [attn * mp_size] * 4 + [hidden * mp_size] * 2
    operands = (*grads, across, sums, *weights)
    outs = [jax.ShapeDtypeStruct(w.shape, F32) for w in weights]
    outs += [jax.ShapeDtypeStruct((3, shard), F32), jax.ShapeDtypeStruct((3, attn), F32)]
    outs += [square(1)] * 3 + [square(attn_blocks), square(hidden_blocks), square(hidden_blocks)]
    outs += [square(bias_rows)] + [square(model // 128)] * len(token_sums)
    new_qkv, new_out, new_up, new_down, qkv_rows, qkv_cols, *rest = call(
        functools.partial(step_kernel, cuts, len(grads), model, wide),
        (1,),
        [whole(a) for a in operands],
        [whole(o.shape) for o in outs],
        outs,
        operands,
    )
    rest = [r.reshape(-1) for r in rest]
    return (
        (new_qkv, qkv_rows, qkv_cols),
        (new_out, rest[3], rest[0]),
        (new_up, rest[1], rest[4]),
        (new_down, rest[5], rest[2]),
        rest[7:],
        rest[6],
    )


def step_plain(dp_size, mp_size, attn_grads, ffn_grads, weights, token_sums, bias_sums, groups):
    w_qkv, w_out, w_up, w_down = weights
    shard, attn = w_qkv.shape[1:]
    hidden = w_up.shape[1]
    model = shard * dp_size
    width = attn // groups
    qkv = jnp.stack([g[:, : 3 * width].reshape(shard, 3, width) for g in attn_grads], axis=1)
    shards = [qkv[:, :, n].reshape(shard, attn) for n in range(3)] + [
        attn_grads[0][:, 3 * width :],
        ffn_grads[:, :hidden].astype(F32),
        ffn_grads[:, hidden:].astype(F32),
    ]
    squares = [g * g for g in shards]
    across = butterfly(
        jnp.concatenate(
            [jnp.sum(s, axis=1) for s in squares] + [jnp.sum(t, axis=0) for t in token_sums]
        ),
        "mp",
        mp_size,
    )
    model_sums = [across[n * shard : (n + 1) * shard] for n in range(6)]
    totals = jnp.stack([jnp.sum(s) for s in model_sums])
    sums = butterfly(
        jnp.concatenate(
            [jnp.sum(s, axis=0) for s in squares]
            + [across[6 * shard :], jnp.sum(sum(bias_sums), axis=0), totals]
        ),
        "dp",
        dp_size,
    )
    cuts = []
    start = 0
    for length in [attn] * 4 + [hidden] * 2 + [model] * len(token_sums) + [hidden, 6]:
        cuts.append(sums[start : start + length])
        start += length
    steps = []
    for n in range(6):
        wide = (attn if n < 4 else hidden) * mp_size
        whole_mean = cuts[-1][n] / (model * wide) + EPS_FACTOR
        model_factor = (model_sums[n] / wide + EPS_FACTOR) / whole_mean
        other_factor = (cuts[n] / model + EPS_FACTOR) / whole_mean
        update = shards[n] * lax.rsqrt(model_factor[:, None] * other_factor[None, :] * whole_mean)
        steps.append((LEARN_RATE * update, model_factor, other_factor))
    return (
        (
            w_qkv - jnp.stack([steps[n][0] for n in range(3)]),
            jnp.stack([steps[n][1] for n in range(3)]),
            jnp.stack([steps[n][2] for n in range(3)]),
        ),
        (w_out - steps[3][0].T, steps[3][2], steps[3][1]),
        (w_up - steps[4][0], steps[4][1], steps[4][2]),
        (w_down - steps[5][0].T, steps[5][2], steps[5][1]),
        cuts[6 : 6 + len(token_sums)],
        cuts[-2],
    )


def results(out_tokens, grad_tokens, step):
    qkv, out, up, down, token_sums, bias_sum = step
    return (
        out_tokens[None],
        grad_tokens[None],
        *qkv,
        *out,
        *up,
        *down,
        *token_sums[:4],
        bias_sum,
        token_sums[4],
    )


def body(
    dp_size,
    mp_size,
    tokens,
    cotangent,
    w_qkv,
    w_out,
    w_up,
    w_down,
    gain_attn,
    shift_attn,
    gain_ffn,
    shift_ffn,
    bias_up,
    bias_down,
    random_blocks,
):
    weights = (w_qkv, w_out, w_up, w_down)
    own_tokens, grad_top = tokens[0], cotangent[0]
    random_rows = random_blocks[0].reshape(random_blocks.shape[1], -1)
    index = lax.axis_index("mp").astype(jnp.int32).reshape(1)
    shard, attn = w_qkv.shape[1:]
    own_rows, model = own_tokens.shape
    width = min(128, attn)
    groups = attn // width
    low_attn, low_ffn = pack(weights, groups, width)
    if mp_size == 4 and dp_size == 8 and width == 128:
        arrange = paired_layer
    else:
        arrange = plain_layer
    out_tokens, grad_tokens, attn_grads, ffn_grads, token_sums, bias_sums = arrange(
        dp_size,
        mp_size,
        own_tokens,
        grad_top,
        random_rows,
        index,
        low_attn,
        low_ffn,
        (gain_attn, shift_attn, gain_ffn, shift_ffn),
        bias_up,
        bias_down,
        groups,
        width,
    )
    aligned = width == 128 and shard == 128 and w_up.shape[1] % 128 == 0
    step = (step_tail if aligned else step_plain)(
        dp_size, mp_size, attn_grads, ffn_grads, weights, token_sums, bias_sums, groups
    )
    return results(out_tokens, grad_tokens, step)


def paired_layer(
    dp_size,
    mp_size,
    tokens,
    grad_top,
    random_rows,
    index,
    low_attn,
    low_ffn,
    norms,
    bias_up,
    bias_down,
    groups,
    width,
):
    gain_attn, shift_attn, gain_ffn, shift_ffn = norms
    rows, model = tokens.shape
    attn = groups * width
    mine = lax.axis_index("dp")
    index_rows = gain_attn.reshape(8, -1)

    def other_core(value):
        return swap(value, 1, mp_size)

    def other_chip(value):
        return swap(value, 2, mp_size)

    places = [(mine + 2 * n) % dp_size for n in (0, 1, 3, 2)]
    places += [p ^ 1 for p in places]

    def levels_of(low):
        above = shifted(low, -2, dp_size)
        below = shifted(low, 2, dp_size)
        return [low, above, below, shifted(above, -2, dp_size)]

    def between_x(value):
        return swap(value, 1, dp_size, "dp")

    def fence(value, *others):
        return after(value, other_core(after(index_rows, *others)))

    normed = norm_call(tokens, gain_attn, shift_attn)
    normed = norm_call(tokens, gain_attn, shift_attn)
    normed_near = other_core(normed)
    far = other_chip(normed)
    attn_levels = levels_of(after(low_attn, normed))
    attn_swapped = [between_x(level) for level in attn_levels[:3]]
    attn_swapped.append(between_x(after(attn_levels[3], far)))
    ffn_low = lax.all_gather(
        after(low_ffn, far, attn_levels[3], *attn_swapped[:3]), "dp", axis=0, tiled=True
    )

    normed_pieces = [normed, normed_near, far, other_core(far)]
    top_far = other_chip(after(grad_top, far))
    top_near = other_core(grad_top)
    early = assemble(
        attn_levels[:3] + attn_swapped[:3], places[:3] + places[4:7], dp_size
    )
    attn_low = assemble(
        [attn_levels[3], after(attn_swapped[3], early)], [places[3], places[7]], dp_size, early
    )
    project = qkv_call(normed_pieces, after(attn_low, random_rows), 3 * attn)
    out_own = attn_low[:, 3 * attn :]
    out_far = other_chip(after(out_own, far))

    heads_out, heads_got = [], []
    for group in range(groups):
        if group == groups - 1:
            project = after(project, top_far)
        heads_out.append(
            attention_call(
                forward_kernel, 15, project, group, groups, (), random_rows, index, mp_size
            )
        )
        heads_got.append(other_chip(heads_out[-1][2 * rows :]))
    own, other = branch_call(
        tokens, heads_out, heads_got, attn_low, out_far
    )
    middle, second = residual_norm_call(own, other_core(other), gain_ffn, shift_ffn)

    second_far = other_chip(second)
    second_near = other_core(second)
    both_near, bias_near, back_own, back_near = ffn_call(
        [second, second_near], [grad_top, top_near], ffn_low, bias_up
    )
    second_far = after(second_far, back_own)
    second_last = other_core(second_far)
    top_last = other_core(top_far)
    both_far, bias_far, back_far, back_last = ffn_call(
        [second_far, second_last], [top_far, top_last], ffn_low, bias_up
    )
    crossing = (back_far.astype(F32) + other_core(back_last).astype(F32)).astype(BF16)
    crossed = other_chip(crossing)
    back_got = other_core(back_near)
    ffn_grads = double_outer_sum(
        [after(second, crossing), second_near, second_far, second_last],
        [grad_top, top_near, top_far, top_last],
        [(both_near, 0), (both_near, 1), (both_far, 0), (both_far, 1)],
    )
    down_far, down_last = down_call(after(both_far, ffn_grads), ffn_low, 2)
    crossed = after(crossed, ffn_grads, down_far)
    ffn_shard = lax.psum_scatter(
        after(ffn_grads, crossed), "dp", scatter_dimension=0, tiled=True
    )
    grad_middle, gain_two, shift_two, top_sum, grad_branch = norm_back_call(
        middle, grad_top, gain_ffn, [back_own, back_got, crossed], True
    )

    branch_pieces = [grad_branch, other_core(grad_branch)]
    away = head_grads_call(branch_pieces, out_far, 0, attn, groups)
    came = [other_chip(a) for a in away]
    stay = list(head_grads_call(branch_pieces, out_own, 0, attn, groups))
    out_away = other_chip(
        outer_sum([after(grad_branch, *away, *stay), branch_pieces[1]], heads_got)
    )
    out_stay = outer_sum(branch_pieces, [h[: 2 * rows] for h in heads_out])
    down_crossing = (
        down_far.astype(F32) + other_core(after(down_last, *away)).astype(F32)
    ).astype(BF16)
    down_crossed = other_chip(after(down_crossing, came[0]))

    grad_projects = []
    project = after(project, down_crossing, out_stay)
    for group in range(groups):
        grad_projects.append(
            attention_call(
                backward_kernel,
                10,
                project,
                group,
                groups,
                (stay[group], came[group]),
                random_rows,
                index,
                mp_size,
            )
        )
        if group == 0:
            first_sum = outer_sum(normed_pieces, grad_projects[:1], (out_stay, out_away))
            kept, sent = scatter_model_split(first_sum, dp_size)
            project, kept, sent = lax.optimization_barrier((project, kept, sent))
            sums = [(kept, between_x(sent))]
    grad_projects[-1] = after(grad_projects[-1], sums[0][1], down_crossed)

    [back_far] = back_project(grad_projects, attn_low, 2, 1, rows)
    came_far = other_core(back_far)
    [back_last] = back_project(
        [after(grad_projects[0], back_far)] + grad_projects[1:], attn_low, 3, 1, rows
    )
    crossing = (back_last.astype(F32) + came_far.astype(F32)).astype(BF16)
    crossed = other_chip(crossing)
    late = [after(g, crossing) for g in grad_projects]
    attn_parts = [scatter_model_end(after(sums[0][0], crossing), sums[0][1], dp_size)]
    for group in range(1, groups):
        kept, sent = scatter_model_split(
            outer_sum(normed_pieces, late[group : group + 1]), dp_size
        )
        attn_parts.append(scatter_model_end(kept, between_x(sent), dp_size))
        late = [after(g, sent) for g in late]
    back_own, back_near = back_project(late, attn_low, 0, 2, rows)
    back_got = other_core(back_near)
    down_own, down_near = down_call(after(both_near, back_own), ffn_low, 2)
    crossed = other_core(after(crossed, *(p for parts in attn_parts for p in parts)))
    out_tokens = (
        middle
        + down_own.astype(F32)
        + other_core(down_near).astype(F32)
        + down_crossed.astype(F32)
        + bias_down
    ).astype(BF16)
    grad_tokens, gain_one, shift_one = norm_back_call(
        tokens, grad_middle, gain_attn, [back_own, back_got, after(crossed, out_tokens)]
    )
    attn_grads = [sum(p.astype(F32) for p in parts) for parts in attn_parts]
    token_sums = [gain_one, shift_one, gain_two, shift_two, top_sum]
    return out_tokens, grad_tokens, attn_grads, ffn_shard, token_sums, [bias_near, bias_far]


def plain_layer(
    dp_size,
    mp_size,
    tokens,
    grad_top,
    random_rows,
    index,
    low_attn,
    low_ffn,
    norms,
    bias_up,
    bias_down,
    groups,
    width,
):
    gain_attn, shift_attn, gain_ffn, shift_ffn = norms
    rows, model = tokens.shape
    attn = groups * width
    lines = [[core + 2 * n for n in range(mp_size // 2)] for core in range(2)]
    core = lax.axis_index("mp") % 2

    def gather(value, axis, along=0):
        return lax.all_gather(value, axis, axis=along, tiled=True)

    def other_core(value):
        return swap(value, 1, mp_size)

    def scattered(value):
        return lax.psum_scatter(value, "mp", scatter_dimension=0, tiled=True)

    def own_first(value):
        half = value.shape[0] // 2
        return jnp.where(core == 0, value, jnp.roll(value, half, axis=0))

    attn_low = gather(low_attn, "dp")
    ffn_low = gather(low_ffn, "dp")
    normed = gather(norm_call(tokens, gain_attn, shift_attn), "mp")
    top_full = gather(grad_top, "mp")
    project = qkv_call([normed], attn_low[:, : 3 * attn], 3 * attn)
    out_low = lax.all_gather(
        attn_low[:, 3 * attn :], "mp", axis=1, axis_index_groups=lines, tiled=True
    )
    heads_out = [
        attention_call(forward_kernel, 15, project, g, groups, (), random_rows, index, 1)
        for g in range(groups)
    ]
    moved = own_first(
        lax.all_to_all(
            jnp.concatenate(heads_out, axis=1), "mp", 0, 1, axis_index_groups=lines, tiled=True
        )
    )
    branch = dot(moved, out_low, NT)
    middle, second = residual_norm_call(
        tokens.astype(F32) + branch[:rows],
        other_core(branch[rows:].astype(BF16)),
        gain_ffn,
        shift_ffn,
    )
    second_full = gather(second, "mp")
    both, bias_sum, back = ffn_call([second_full], [top_full], ffn_low, bias_up)
    ffn_grads = double_outer_sum([second_full], [top_full], [(both, 0)])
    ffn_shard = lax.psum_scatter(ffn_grads, "dp", scatter_dimension=0, tiled=True)
    grad_middle, gain_two, shift_two, top_sum, grad_branch = norm_back_call(
        middle, grad_top, gain_ffn, [scattered(back)], True
    )
    branch_pair = jnp.concatenate([grad_branch, other_core(grad_branch)], axis=0)
    away = own_first(dot(branch_pair, out_low, NN).astype(BF16))
    away = lax.all_to_all(away, "mp", 1, 0, axis_index_groups=lines, tiled=True)
    out_grad = lax.psum_scatter(
        dot(branch_pair, moved, TN).astype(BF16),
        "mp",
        scatter_dimension=1,
        axis_index_groups=lines,
        tiled=True,
    )
    grad_projects = [
        attention_call(
            backward_kernel,
            6,
            project,
            g,
            groups,
            (away[:, g * width : (g + 1) * width],),
            random_rows,
            index,
            1,
        )
        for g in range(groups)
    ]
    attn_grads = [
        scatter_model(
            outer_sum([normed], [g], (out_grad,) if n == 0 else ()), dp_size
        )
        for n, g in enumerate(grad_projects)
    ]
    back = sum(
        dot(g, attn_low[:, 3 * n * width : 3 * (n + 1) * width], NT)
        for n, g in enumerate(grad_projects)
    )
    grad_tokens, gain_one, shift_one = norm_back_call(
        tokens, grad_middle, gain_attn, [scattered(back.astype(BF16))]
    )
    down = scattered(down_call(both, ffn_low, 1)[0])
    out_tokens = (middle + down.astype(F32) + bias_down).astype(BF16)
    token_sums = [gain_one, shift_one, gain_two, shift_two, top_sum]
    return out_tokens, grad_tokens, attn_grads, ffn_shard, token_sums, [bias_sum]


def solution(mesh):
    placed = (
        P("dp", "mp", None),
        P("dp", "mp", None),
        P(None, "dp", "mp"),
        P("mp", "dp"),
        P("dp", "mp"),
        P("mp", "dp"),
        P(),
        P(),
        P(),
        P(),
        P("mp"),
        P(),
        P("dp", "mp", None, None),
    )
    return jax.shard_map(
        functools.partial(body, mesh.shape["dp"], mesh.shape["mp"]),
        mesh=mesh,
        in_specs=placed,
        out_specs=(
            P("dp", "mp", None),
            P("dp", "mp", None),
            P(None, "dp", "mp"),
            P(None, "dp"),
            P(None, "mp"),
            P("mp", "dp"),
            P("mp"),
            P("dp"),
            P("dp", "mp"),
            P("dp"),
            P("mp"),
            P("mp", "dp"),
            P("mp"),
            P("dp"),
            P(),
            P(),
            P(),
            P(),
            P("mp"),
            P(),
        ),
        check_vma=False,
    )
```

```python
import functools

import jax
import jax.numpy as jnp
from jax import lax
from jax.experimental import pallas as pl
from jax.experimental.pallas import tpu as pltpu
from jax.sharding import PartitionSpec as P

BLOCK = 64
EPS_NORM = 1e-05
EPS_FACTOR = 1e-30
LEARN_RATE = 0.1
GELU_SCALE = 0.7978845608028654
GELU_CUBE = 0.044715
F32 = jnp.float32
BF16 = jnp.bfloat16
NN = (((1,), (0,)), ((), ()))
NT = (((1,), (1,)), ((), ()))
TN = (((0,), (0,)), ((), ()))
VMEM_LIMIT = 24 << 20


def cost(microseconds):
    return pl.CostEstimate(flops=int(microseconds * 1.15e9), bytes_accessed=1 << 10, transcendentals=0)


CHEAP = cost(0.01)


def dot(left, right, form):
    return lax.dot_general(left, right, form, preferred_element_type=F32)


def swap(value, bit, size, axis="mp"):
    return lax.ppermute(value, axis, [(i, i ^ bit) for i in range(size)])


def after(value, *others):
    return lax.optimization_barrier((value, *others))[0]


def shifted(value, by, size):
    return lax.ppermute(value, "dp", [(i, (i + by) % size) for i in range(size)])


def scatter_model(partial, size):
    if size != 8:
        return lax.psum_scatter(partial, "dp", scatter_dimension=0, tiled=True).astype(F32)
    kept, sent = scatter_model_split(partial, size)
    return sum(p.astype(F32) for p in scatter_model_end(kept, swap(sent, 1, size, "dp"), size))


def scatter_model_split(partial, size):
    mine = lax.axis_index("dp")
    rows = partial.shape[0] // size
    columns = partial.shape[1]
    side = mine % 2
    split = partial.reshape(4, 2, rows, columns)

    def of_side(which):
        return lax.dynamic_slice(split, (0, which, 0, 0), (4, 1, rows, columns)).reshape(
            4, rows, columns
        )

    return of_side(side), of_side(1 - side)


def scatter_model_end(kept, got, size):
    level = lax.axis_index("dp") // 2
    rows, columns = kept.shape[1:]
    pair = (kept.astype(F32) + got.astype(F32)).astype(BF16)

    def of_level(which):
        return lax.dynamic_slice(pair, (which, 0, 0), (1, rows, columns))[0]

    parts = [shifted(of_level((level + n) % 4), 2 * n, size) for n in (1, 3, 2)]
    return [of_level(level)] + parts


def assemble_kernel(count, place_ref, *refs):
    rows = refs[0].shape[0]
    out_ref = refs[-1]
    if len(refs) > count + 1:
        out_ref[...] = refs[count][...]
    for n in range(count):
        at = pl.ds(pl.multiple_of(place_ref[n] * rows, rows), rows)
        out_ref[at, :] = refs[n][...]


def assemble(parts, places, total, base=None):
    count = len(parts)
    rows, columns = parts[0].shape
    tile = min(512, columns)
    whole_rows = pl.BlockSpec((total * rows, tile), lambda i: (0, i))
    return pl.pallas_call(
        functools.partial(assemble_kernel, count),
        grid=(columns // tile,),
        in_specs=[pl.BlockSpec(memory_space=pltpu.SMEM)]
        + [pl.BlockSpec((rows, tile), lambda i: (0, i))] * count
        + ([] if base is None else [whole_rows]),
        out_specs=whole_rows,
        out_shape=jax.ShapeDtypeStruct((total * rows, columns), parts[0].dtype),
        compiler_params=pltpu.CompilerParams(vmem_limit_bytes=16 << 20),
        cost_estimate=CHEAP,
    )(jnp.stack(places).astype(jnp.int32), *parts, *([] if base is None else [base]))


def butterfly(value, axis, size):
    bit = 1
    while bit < size:
        value = value + swap(value, bit, size, axis)
        bit *= 2
    return value


def stack_heads(block, heads, head_dim):
    if heads == 1:
        return block
    owner = lax.broadcasted_iota(jnp.int32, block.shape, 1) // head_dim
    zero = jnp.zeros_like(block)
    return jnp.concatenate([jnp.where(owner == h, block, zero) for h in range(heads)], axis=0)


def unstack_heads(stacked, heads, head_dim):
    if heads == 1:
        return stacked
    rows = stacked.shape[0] // heads
    owner = lax.broadcasted_iota(jnp.int32, (rows, stacked.shape[1]), 1) // head_dim
    result = stacked[:rows]
    for h in range(1, heads):
        result = jnp.where(owner >= h, stacked[h * rows : (h + 1) * rows], result)
    return result


def block_rows(place):
    return pl.ds(pl.multiple_of(place * BLOCK, BLOCK), BLOCK)


def near_rows(ref, fixed, drawn, heads, head_dim):
    parts = [ref[block_rows(place), :] for place in fixed]
    for places in drawn:
        block = ref[block_rows(places[0]), :]
        if heads > 1:
            owner = lax.broadcasted_iota(jnp.int32, block.shape, 1) // head_dim
            for h in range(1, heads):
                block = jnp.where(owner >= h, ref[block_rows(places[h]), :], block)
        parts.append(block)
    return jnp.concatenate(parts, axis=0)


def probabilities(keys, queries):
    scores = dot(keys, queries, NT)
    expanded = jnp.exp(scores - jnp.max(scores, axis=0, keepdims=True))
    return expanded * (1.0 / jnp.sum(expanded, axis=0, keepdims=True))


def scale_low(block, scaling):
    return (block.astype(F32) * scaling).astype(BF16)


def table_of(random_ref, place, step, first, heads, draws):
    fixed = [place(0), place(step), place(step + 1), place(step + 2), place(-1)]
    drawn = [
        [place(random_ref[first + h, step * draws + j]) for h in range(heads)]
        for j in range(draws)
    ]
    return fixed, drawn


def placer(index_ref, blocks_all, pieces):
    per_piece = blocks_all // pieces

    def place(block):
        if isinstance(block, int):
            block = jnp.int32(block % blocks_all)
        if pieces == 1:
            return block
        return ((block // per_piece) ^ index_ref[0]) * per_piece + block % per_piece

    return place


def forward_kernel(first, heads, head_dim, draws, pieces, unroll, random_ref, index_ref, q_ref, k_ref, v_ref, o_ref):
    blocks_all = q_ref.shape[0] // BLOCK
    scaling = head_dim**-0.5
    place = placer(index_ref, blocks_all, pieces)

    def attend(queries, keys, values):
        stacked = stack_heads(scale_low(queries, scaling), heads, head_dim)
        probs = probabilities(keys, stacked).astype(BF16)
        return unstack_heads(dot(probs, values, TN), heads, head_dim).astype(BF16)

    def middle(step, carry):
        fixed, drawn = table_of(random_ref, place, step, first, heads, draws)
        keys = near_rows(k_ref, fixed, drawn, heads, head_dim)
        values = near_rows(v_ref, fixed, drawn, heads, head_dim)
        at = block_rows(fixed[2])
        o_ref[at, :] = attend(q_ref[at, :], keys, values)
        return carry

    lax.fori_loop(0, blocks_all - 2, middle, 0, unroll=unroll)
    for end in (0, -1):
        at = block_rows(place(end))
        o_ref[at, :] = attend(q_ref[at, :], k_ref[...], v_ref[...])


def backward_kernel(
    first,
    heads,
    head_dim,
    draws,
    pieces,
    unroll,
    random_ref,
    index_ref,
    q_ref,
    k_ref,
    v_ref,
    *refs,
):
    parts = len(refs) - 8
    grad_refs, out_ref = refs[:parts], refs[parts]
    g_ref, k_near, v_near, k_drawn, v_drawn, k_ends, v_ends = refs[parts + 1 :]
    width = q_ref.shape[1]
    rows = g_ref.shape[0] // parts
    for n, ref in enumerate(grad_refs):
        g_ref[n * rows : (n + 1) * rows, :] = ref[...]
    blocks_all = q_ref.shape[0] // BLOCK
    scaling = head_dim**-0.5
    place = placer(index_ref, blocks_all, pieces)
    owner = lax.broadcasted_iota(jnp.int32, (BLOCK, q_ref.shape[1]), 1) // head_dim
    for ref in (k_drawn, v_drawn, k_ends, v_ends):
        ref[...] = jnp.zeros_like(ref)

    def back(queries, grads, keys, values):
        q_stack = stack_heads(scale_low(queries, scaling), heads, head_dim)
        g_stack = stack_heads(grads, heads, head_dim)
        probs = probabilities(keys, q_stack)
        grad_probs = dot(values, g_stack, NT)
        center = jnp.sum(probs * grad_probs, axis=0, keepdims=True)
        grad_scores = (probs * (grad_probs - center)).astype(BF16)
        grad_keys = dot(grad_scores, q_stack, NN)
        grad_values = dot(probs.astype(BF16), g_stack, NN)
        grad_queries = unstack_heads(dot(grad_scores, keys, TN), heads, head_dim) * scaling
        return grad_queries.astype(BF16), grad_keys, grad_values

    for number, end in enumerate((0, -1)):
        at = block_rows(place(end))
        dq, dk, dv = back(q_ref[at, :], g_ref[at, :], k_ref[...], v_ref[...])
        out_ref[at, 0:width] = dq
        if number == 0:
            k_near[...] = dk
            v_near[...] = dv
        else:
            k_near[...] += dk
            v_near[...] += dv

    def middle(step, carry):
        fixed, drawn = table_of(random_ref, place, step, first, heads, draws)
        keys = near_rows(k_ref, fixed, drawn, heads, head_dim)
        values = near_rows(v_ref, fixed, drawn, heads, head_dim)
        at = block_rows(fixed[2])
        dq, dk, dv = back(q_ref[at, :], g_ref[at, :], keys, values)
        out_ref[at, 0:width] = dq
        for part, near, far, ends in ((dk, k_near, k_drawn, k_ends), (dv, v_near, v_drawn, v_ends)):
            ends[0:BLOCK, :] += part[0:BLOCK]
            ends[BLOCK:, :] += part[4 * BLOCK : 5 * BLOCK]
            if pieces == 1:
                window = pl.ds(pl.multiple_of(step * BLOCK, BLOCK), 3 * BLOCK)
                near[window, :] += part[BLOCK : 4 * BLOCK]
            else:
                for n in range(1, 4):
                    near[block_rows(fixed[n]), :] += part[n * BLOCK : (n + 1) * BLOCK]
            for j in range(draws):
                block = part[(5 + j) * BLOCK : (6 + j) * BLOCK]
                for h in range(heads):
                    kept = block if heads == 1 else jnp.where(owner == h, block, 0.0)
                    far[block_rows(drawn[j][h]), :] += kept
        return carry

    lax.fori_loop(0, blocks_all - 2, middle, 0, unroll=unroll)
    for n, near, far, ends in ((1, k_near, k_drawn, k_ends), (2, v_near, v_drawn, v_ends)):
        near[block_rows(place(0)), :] += ends[0:BLOCK, :]
        near[block_rows(place(-1)), :] += ends[BLOCK:, :]
        out_ref[:, n * width : (n + 1) * width] = (near[...] + far[...]).astype(BF16)


def attention_call(kernel, unroll, project, group, groups, grads, table, index, pieces):
    seq_rows = project.shape[0]
    width = project.shape[1] // (3 * groups)
    heads = table.shape[0] // groups
    draws = table.shape[1] // (seq_rows // BLOCK - 2)
    head_dim = width // heads
    narrow = width % 128 != 0
    first = 3 * group * width
    if narrow:
        operands = [project[:, first + n * width : first + (n + 1) * width] for n in range(3)]
    else:
        operands = [project] * 3

    def spec(part):
        column = 0 if narrow else part
        return pl.BlockSpec((seq_rows, width), lambda g, *refs: (0, column))

    columns = width * (3 if grads else 1)
    total = pltpu.VMEM((seq_rows, width), F32)
    ends = pltpu.VMEM((2 * BLOCK, width), F32)
    return pl.pallas_call(
        functools.partial(kernel, group * heads, heads, head_dim, draws, pieces, unroll),
        grid_spec=pltpu.PrefetchScalarGridSpec(
            num_scalar_prefetch=2,
            grid=(1,),
            in_specs=[spec(3 * group), spec(3 * group + 1), spec(3 * group + 2)]
            + [pl.BlockSpec(g.shape, lambda g, *refs: (0, 0)) for g in grads],
            out_specs=pl.BlockSpec((seq_rows, columns), lambda g, *refs: (0, 0)),
            scratch_shapes=[pltpu.VMEM((seq_rows, width), BF16)] + [total] * 4 + [ends] * 2
            if grads
            else [],
        ),
        out_shape=jax.ShapeDtypeStruct((seq_rows, columns), BF16),
        compiler_params=pltpu.CompilerParams(vmem_limit_bytes=VMEM_LIMIT),
        cost_estimate=cost(5) if grads else CHEAP,
    )(
        table,
        index,
        *operands,
        *grads,
    )


def call(kernel, grid, in_specs, out_specs, out_shape, operands, estimate=CHEAP, limit=16):
    return pl.pallas_call(
        kernel,
        grid=grid,
        in_specs=in_specs,
        out_specs=out_specs,
        out_shape=out_shape,
        compiler_params=pltpu.CompilerParams(vmem_limit_bytes=limit << 20),
        cost_estimate=estimate,
    )(*operands)


def whole(array):
    shape = array if isinstance(array, tuple) else array.shape
    return pl.BlockSpec(shape, lambda i: (0,) * len(shape))


def row_tiles(tile, columns, column=0):
    return pl.BlockSpec((tile, columns), lambda i: (i, column))


def piece_tiles(number, tiles, tile, columns):
    return pl.BlockSpec((tile, columns), lambda i: (jnp.clip(i - number * tiles, 0, tiles - 1), 0))


def chosen(refs, tiles):
    which = pl.program_id(0) // tiles
    value = refs[0][...]
    for n in range(1, len(refs)):
        value = jnp.where(which == n, refs[n][...], value)
    return value


def store_chosen(refs, tiles, value):
    for n, ref in enumerate(refs):

        @pl.when(pl.program_id(0) // tiles == n)
        def _(ref=ref):
            ref[...] = value.astype(ref.dtype)


def folded(value):
    rows, columns = value.shape
    return jnp.sum(value.reshape(rows // 8, 8, columns), axis=0)


def normalize(values):
    center = jnp.mean(values, axis=1, keepdims=True)
    spread = values - center
    variance = jnp.mean(spread * spread, axis=1, keepdims=True)
    inverse = lax.rsqrt(variance + EPS_NORM)
    return spread * inverse, inverse


def norm_kernel(x_ref, gain_ref, shift_ref, h_ref):
    normal, _ = normalize(x_ref[...].astype(F32))
    h_ref[...] = (normal * gain_ref[...] + shift_ref[...]).astype(BF16)


def norm_call(values, gain, shift):
    rows, model = values.shape
    tile = min(128, rows)
    return call(
        norm_kernel,
        (rows // tile,),
        [row_tiles(tile, model), whole((1, model)), whole((1, model))],
        row_tiles(tile, model),
        jax.ShapeDtypeStruct((rows, model), BF16),
        (values, gain.reshape(1, model), shift.reshape(1, model)),
    )


def residual_norm_kernel(own_ref, got_ref, gain_ref, shift_ref, r_ref, h_ref):
    values = own_ref[...] + got_ref[...].astype(F32)
    r_ref[...] = values
    normal, _ = normalize(values)
    h_ref[...] = (normal * gain_ref[...] + shift_ref[...]).astype(BF16)


def residual_norm_call(own, got, gain, shift):
    rows, model = own.shape
    tile = min(128, rows)
    tiles = row_tiles(tile, model)
    return call(
        residual_norm_kernel,
        (rows // tile,),
        [tiles, tiles, whole((1, model)), whole((1, model))],
        [tiles, tiles],
        [jax.ShapeDtypeStruct((rows, model), F32), jax.ShapeDtypeStruct((rows, model), BF16)],
        (own, got, gain.reshape(1, model), shift.reshape(1, model)),
    )


def norm_back_kernel(count, x_ref, base_ref, gain_ref, *refs):
    grad_ref, gain_sum, shift_sum = refs[count : count + 3]
    more = refs[count + 3 :]

    @pl.when(pl.program_id(0) == 0)
    def _():
        for ref in (gain_sum, shift_sum, *more[:1]):
            ref[...] = jnp.zeros_like(ref)

    grad_norm = refs[0][...].astype(F32)
    for ref in refs[1:count]:
        grad_norm = grad_norm + ref[...].astype(F32)
    normal, inverse = normalize(x_ref[...].astype(F32))
    base = base_ref[...].astype(F32)
    scaled = grad_norm * gain_ref[...]
    mean_plain = jnp.mean(scaled, axis=1, keepdims=True)
    mean_normal = jnp.mean(scaled * normal, axis=1, keepdims=True)
    grad = base + inverse * (scaled - mean_plain - normal * mean_normal)
    grad_ref[...] = grad
    gain_sum[...] += folded(grad_norm * normal)
    shift_sum[...] += folded(grad_norm)
    if more:
        more[0][...] += folded(base)
        more[1][...] = grad.astype(BF16)


def norm_back_call(values, base, gain, grads, more=False):
    rows, model = values.shape
    tile = min(128, rows)
    tiles = row_tiles(tile, model)
    sums = jax.ShapeDtypeStruct((8, model), F32)
    result = jax.ShapeDtypeStruct((rows, model), F32)
    low = jax.ShapeDtypeStruct((rows, model), BF16)
    return call(
        functools.partial(norm_back_kernel, len(grads)),
        (rows // tile,),
        [tiles, tiles, whole((1, model))] + [tiles] * len(grads),
        [tiles] + [whole((8, model))] * 2 + ([whole((8, model)), tiles] if more else []),
        [result, sums, sums] + ([sums, low] if more else []),
        (values, base, gain.reshape(1, model), *grads),
    )


def pack_kernel(groups, width, qkv_ref, out_ref, up_ref, down_ref, attn_ref, ffn_ref):
    attn = groups * width
    for g in range(groups):
        for c in range(3):
            at = (3 * g + c) * width
            attn_ref[:, at : at + width] = qkv_ref[c, :, g * width : (g + 1) * width].astype(BF16)
    attn_ref[:, 3 * attn :] = out_ref[...].T.astype(BF16)
    hidden = up_ref.shape[1]
    ffn_ref[:, :hidden] = up_ref[...].astype(BF16)
    ffn_ref[:, hidden:] = down_ref[...].T.astype(BF16)


def pack(weights, groups, width):
    w_qkv, w_out, w_up, w_down = weights
    _, shard, attn = w_qkv.shape
    hidden = w_up.shape[1]
    if width % 128 or shard % 128 or hidden % 128:
        qkv = w_qkv.astype(BF16).reshape(3, shard, groups, width).transpose(1, 2, 0, 3)
        return (
            jnp.concatenate([qkv.reshape(shard, 3 * attn), w_out.astype(BF16).T], axis=1),
            jnp.concatenate([w_up.astype(BF16), w_down.astype(BF16).T], axis=1),
        )
    outs = [
        jax.ShapeDtypeStruct((shard, 4 * attn), BF16),
        jax.ShapeDtypeStruct((shard, 2 * hidden), BF16),
    ]
    return call(
        functools.partial(pack_kernel, groups, width),
        (1,),
        [whole(w) for w in weights],
        [whole(o.shape) for o in outs],
        outs,
        weights,
    )


def qkv_kernel(tiles, *refs):
    w_ref, o_ref = refs[-2:]
    o_ref[...] = dot(chosen(refs[:-2], tiles), w_ref[...], NN).astype(BF16)


def qkv_call(pieces, weights, columns):
    rows, model = pieces[0].shape
    tile = min(256, rows)
    tiles = rows // tile
    count = len(pieces)
    return call(
        functools.partial(qkv_kernel, tiles),
        (count * tiles,),
        [piece_tiles(n, tiles, tile, model) for n in range(count)] + [whole((model, columns))],
        row_tiles(tile, columns),
        jax.ShapeDtypeStruct((count * rows, columns), BF16),
        (*pieces, weights),
    )


def branch_kernel(tiles, groups, x_ref, *refs):
    outs, gots = refs[:groups], refs[groups : 2 * groups]
    near_ref, far_ref, own_ref, other_ref = refs[2 * groups :]

    def joined(parts):
        return jnp.concatenate([p[...] for p in parts], axis=1) if groups > 1 else parts[0][...]

    value = dot(joined(outs), near_ref[...], NT) + dot(joined(gots), far_ref[...], NT)
    step = pl.program_id(0)

    @pl.when(step < tiles)
    def _():
        own_ref[...] = value + x_ref[...].astype(F32)

    @pl.when(step >= tiles)
    def _():
        other_ref[...] = value.astype(BF16)


def branch_call(tokens, outs, gots, attn_low, out_far):
    rows, model = tokens.shape
    attn = out_far.shape[1]
    groups = len(outs)
    width = attn // groups
    tile = min(256, rows)
    tiles = rows // tile
    return call(
        functools.partial(branch_kernel, tiles, groups),
        (2 * tiles,),
        [piece_tiles(0, tiles, tile, model)]
        + [row_tiles(tile, width)] * (2 * groups)
        + [pl.BlockSpec((model, attn), lambda i: (0, 3)), whole(out_far)],
        [piece_tiles(0, tiles, tile, model), piece_tiles(1, tiles, tile, model)],
        [jax.ShapeDtypeStruct((rows, model), F32), jax.ShapeDtypeStruct((rows, model), BF16)],
        (tokens, *outs, *gots, attn_low, out_far),
    )


def gelu_parts(values):
    square = values * values
    curve = jnp.tanh(values * (GELU_SCALE + (GELU_SCALE * GELU_CUBE) * square))
    half = 0.5 + 0.5 * curve
    slope = half + (0.5 * values) * (1.0 - curve * curve) * (
        GELU_SCALE + (3.0 * GELU_SCALE * GELU_CUBE) * square
    )
    return values * half, slope


def ffn_kernel(tiles, count, *refs):
    h_refs, g_refs = refs[:count], refs[count : 2 * count]
    up_ref, down_ref, bias_ref, both_ref, sum_ref = refs[2 * count : 2 * count + 5]
    dh_refs = refs[2 * count + 5 :]
    hidden = up_ref.shape[1]

    @pl.when(pl.program_id(0) == 0)
    def _():
        sum_ref[...] = jnp.zeros_like(sum_ref)

    hidden_pre = dot(chosen(h_refs, tiles), up_ref[...], NN) + bias_ref[...]
    grad_active = dot(chosen(g_refs, tiles), down_ref[...], NN)
    active, slope = gelu_parts(hidden_pre)
    grad_hidden = (grad_active * slope).astype(BF16)
    both_ref[:, :hidden] = grad_hidden
    both_ref[:, hidden:] = active.astype(BF16)
    sum_ref[...] += folded(grad_hidden.astype(F32))
    store_chosen(dh_refs, tiles, dot(grad_hidden, up_ref[...], NT))


def ffn_call(normed, grads, ffn_low, bias):
    count = len(normed)
    rows, model = normed[0].shape
    hidden = ffn_low.shape[1] // 2
    tile = min(256, rows)
    tiles = rows // tile
    pieces = [piece_tiles(n, tiles, tile, model) for n in range(count)]
    both = jax.ShapeDtypeStruct((count * rows, 2 * hidden), BF16)
    return call(
        functools.partial(ffn_kernel, tiles, count),
        (count * tiles,),
        pieces
        + pieces
        + [
            pl.BlockSpec((model, hidden), lambda i: (0, 0)),
            pl.BlockSpec((model, hidden), lambda i: (0, 1)),
            whole((1, hidden)),
        ],
        [row_tiles(tile, 2 * hidden), whole((8, hidden))] + pieces,
        [both, jax.ShapeDtypeStruct((8, hidden), F32)]
        + [jax.ShapeDtypeStruct((rows, model), BF16)] * count,
        (*normed, *grads, ffn_low, ffn_low, bias.reshape(1, hidden)),
        limit=24,
    )


def row_piece(number, rows, columns):
    return pl.BlockSpec((rows, columns), lambda i: (number, 0))


def outer_kernel(count, rights_count, extras, *refs):
    lefts = refs[:count]
    at = count
    o_ref = refs[-1]
    column = 0
    for _ in range(rights_count):
        total = dot(lefts[0][...], refs[at][...], TN)
        for n in range(1, count):
            total = total + dot(lefts[n][...], refs[at + n][...], TN)
        at += count
        o_ref[:, column : column + total.shape[1]] = total.astype(BF16)
        column += total.shape[1]
    if extras:
        total = refs[at][...].astype(F32)
        for n in range(1, extras):
            total = total + refs[at + n][...].astype(F32)
        o_ref[:, column:] = total.astype(BF16)


def outer_sum(lefts, rights, extras=()):
    count = len(lefts)
    rows, model = lefts[0].shape
    tile = min(512, model)
    columns = sum(r.shape[1] for r in rights) + (extras[0].shape[1] if extras else 0)
    specs = [pl.BlockSpec((rows, tile), lambda i: (0, i))] * count
    operands = list(lefts)
    for right in rights:
        specs += [row_piece(n, rows, right.shape[1]) for n in range(count)]
        operands += [right] * count
    specs += [row_tiles(tile, e.shape[1]) for e in extras]
    return call(
        functools.partial(outer_kernel, count, len(rights), len(extras)),
        (model // tile,),
        specs,
        row_tiles(tile, columns),
        jax.ShapeDtypeStruct((model, columns), BF16),
        (*operands, *extras),
    )


def double_outer_kernel(count, steps, *refs):
    rights, o_ref = refs[2 * count : 3 * count], refs[3 * count]
    first = pl.program_id(0) < steps
    total = None
    for n in range(count):
        left = jnp.where(first, refs[n][...], refs[count + n][...])
        part = dot(left, rights[n][...], TN)
        total = part if total is None else total + part
    o_ref[...] = total.astype(BF16)


def double_outer_sum(lefts, other_lefts, rights):
    count = len(lefts)
    rows, model = lefts[0].shape
    columns = rights[0][0].shape[1] // 2
    tile = min(512, model)
    steps = model // tile

    def left_spec(which):
        return pl.BlockSpec(
            (rows, tile), lambda i: (0, jnp.clip(i - which * steps, 0, steps - 1))
        )

    def right_spec(block):
        return pl.BlockSpec((rows, columns), lambda i: (block, i // steps))

    return call(
        functools.partial(double_outer_kernel, count, steps),
        (2 * steps,),
        [left_spec(0)] * count + [left_spec(1)] * count + [right_spec(n) for _, n in rights],
        pl.BlockSpec((tile, columns), lambda i: (i % steps, i // steps)),
        jax.ShapeDtypeStruct((model, 2 * columns), BF16),
        (*lefts, *other_lefts, *(a for a, _ in rights)),
        limit=24,
    )


def head_grads_kernel(tiles, count, width, *refs):
    w_ref, outs = refs[count], refs[count + 1 :]
    value = dot(chosen(refs[:count], tiles), w_ref[...], NN).astype(BF16)
    for n, out in enumerate(outs):
        out[...] = value[:, n * width : (n + 1) * width]


def head_grads_call(pieces, weights, column, attn, groups):
    count = len(pieces)
    rows, model = pieces[0].shape
    width = attn // groups
    tile = min(256, rows)
    tiles = rows // tile
    return call(
        functools.partial(head_grads_kernel, tiles, count, width),
        (count * tiles,),
        [piece_tiles(n, tiles, tile, model) for n in range(count)]
        + [pl.BlockSpec((model, attn), lambda i: (0, column))],
        [row_tiles(tile, width)] * groups,
        [jax.ShapeDtypeStruct((count * rows, width), BF16)] * groups,
        (*pieces, weights),
    )


def back_project_kernel(groups, tiles, *refs):
    w_ref, outs = refs[groups], refs[groups + 1 :]
    parts = [refs[n][...] for n in range(groups)]
    grads = jnp.concatenate(parts, axis=1) if groups > 1 else parts[0]
    store_chosen(outs, tiles, dot(grads, w_ref[...], NT))


def back_project(grads, weights, first, count, rows):
    groups = len(grads)
    columns = grads[0].shape[1]
    model = weights.shape[0]
    tile = min(256, rows)
    tiles = rows // tile
    return call(
        functools.partial(back_project_kernel, groups, tiles),
        (count * tiles,),
        [pl.BlockSpec((tile, columns), lambda i: (first * tiles + i, 0))] * groups
        + [whole((model, groups * columns))],
        [piece_tiles(n, tiles, tile, model) for n in range(count)],
        [jax.ShapeDtypeStruct((rows, model), BF16)] * count,
        (*grads, weights),
    )


def down_kernel(tiles, z_ref, w_ref, *outs):
    store_chosen(outs, tiles, dot(z_ref[...], w_ref[...], NT))


def down_call(both, ffn_low, count):
    model = ffn_low.shape[0]
    hidden = ffn_low.shape[1] // 2
    rows = both.shape[0] // count
    tile = min(256, rows)
    tiles = rows // tile
    return call(
        functools.partial(down_kernel, tiles),
        (count * tiles,),
        [
            pl.BlockSpec((tile, hidden), lambda i: (i, 1)),
            pl.BlockSpec((model, hidden), lambda i: (0, 1)),
        ],
        [piece_tiles(n, tiles, tile, model) for n in range(count)],
        [jax.ShapeDtypeStruct((rows, model), BF16)] * count,
        (both, ffn_low),
    )


def columns_of(refs, cuts):
    for matrix, (which, first, blocks) in enumerate(cuts):
        for n, at in enumerate(first if isinstance(first, tuple) else range(first, first + blocks)):
            yield matrix, n, refs[which][:, at * 128 : (at + 1) * 128].astype(F32)


def sums_kernel(cuts, grads_count, token_count, *refs):
    grads = refs[:grads_count]
    token_refs = refs[grads_count : grads_count + token_count]
    bias_refs = refs[grads_count + token_count : -2]
    across_ref, along_ref = refs[-2:]
    across_ref[...] = jnp.zeros_like(across_ref)
    totals = [None] * len(cuts)
    row = 0
    for matrix, _, value in columns_of(grads, cuts):
        square = value * value
        totals[matrix] = square if totals[matrix] is None else totals[matrix] + square
        along_ref[row : row + 1, :] = jnp.sum(square, axis=0, keepdims=True)
        row += 1
    for matrix, total in enumerate(totals):
        across_ref[matrix : matrix + 1, :] = jnp.sum(total.T, axis=0, keepdims=True)

    def store_rows(ref, row, value):
        for n in range(value.shape[1] // 128):
            ref[row + n : row + n + 1, :] = value[:, n * 128 : (n + 1) * 128]

    bias = bias_refs[0][...]
    for ref in bias_refs[1:]:
        bias = bias + ref[...]
    store_rows(along_ref, row, jnp.sum(bias, axis=0, keepdims=True))
    row = 8
    for ref in token_refs:
        value = jnp.sum(ref[...], axis=0, keepdims=True)
        store_rows(across_ref, row, value)
        row += value.shape[1] // 128


def join_kernel(matrices, across_ref, along_ref, o_ref):
    along_rows = along_ref.shape[0]
    token_rows = across_ref.shape[0] - 8
    o_ref[0:along_rows, :] = along_ref[...]
    o_ref[along_rows : along_rows + token_rows, :] = across_ref[8:, :]
    o_ref[along_rows + token_rows :, :] = jnp.broadcast_to(
        jnp.sum(across_ref[0:8, :], axis=1, keepdims=True), (8, 128)
    )


def step_kernel(cuts, grads_count, model, wide, *refs):
    grads = refs[:grads_count]
    across_ref, sums_ref, qkv_ref, out_ref, up_ref, down_ref = refs[grads_count : grads_count + 6]
    n_qkv, n_out, n_up, n_down, qkv_rows, qkv_cols = refs[grads_count + 6 : grads_count + 12]
    singles = refs[grads_count + 12 : grads_count + 18]
    copies = refs[grads_count + 18 :]
    totals_at = sums_ref.shape[0] - 8
    scales = []
    for matrix in range(len(cuts)):
        whole_mean = sums_ref[totals_at + matrix : totals_at + matrix + 1, :] / (
            model * wide[matrix]
        ) + EPS_FACTOR
        model_factor = (across_ref[matrix : matrix + 1, :] / wide[matrix] + EPS_FACTOR) / whole_mean
        if matrix < 3:
            qkv_rows[matrix : matrix + 1, :] = model_factor
        else:
            singles[matrix - 3][...] = model_factor
        scales.append((whole_mean, jnp.broadcast_to(model_factor, (128, 128)).T))
    row = 0
    for matrix, n, value in columns_of(grads, cuts):
        whole_mean, model_factor = scales[matrix]
        other_factor = (sums_ref[row : row + 1, :] / model + EPS_FACTOR) / whole_mean
        row += 1
        update = LEARN_RATE * (value * lax.rsqrt(model_factor * other_factor * whole_mean))
        at = slice(n * 128, (n + 1) * 128)
        if matrix < 3:
            n_qkv[matrix, :, at] = qkv_ref[matrix, :, at] - update
            qkv_cols[matrix : matrix + 1, at] = other_factor
            continue
        singles[matrix][n : n + 1, :] = other_factor
        if matrix == 3:
            n_out[at, :] = out_ref[at, :] - update.T
        elif matrix == 4:
            n_up[:, at] = up_ref[:, at] - update
        else:
            n_down[at, :] = down_ref[at, :] - update.T
    for ref in copies:
        count = ref.shape[0]
        ref[...] = sums_ref[row : row + count, :]
        row += count


def step_tail(dp_size, mp_size, attn_grads, ffn_grads, weights, token_sums, bias_sums, groups):
    w_qkv, w_out, w_up, w_down = weights
    shard, attn = w_qkv.shape[1:]
    hidden = w_up.shape[1]
    model = shard * dp_size
    per_group = attn // groups // 128
    attn_blocks, hidden_blocks = attn // 128, hidden // 128
    joined = jnp.concatenate([g[:, : 3 * attn // groups] for g in attn_grads], axis=1)
    grads = [joined, attn_grads[0], ffn_grads]
    cuts = [
        (
            0,
            tuple(
                (3 * g + c) * per_group + n for g in range(groups) for n in range(per_group)
            ),
            0,
        )
        for c in range(3)
    ]
    cuts += [
        (1, 3 * per_group, attn_blocks),
        (2, 0, hidden_blocks),
        (2, hidden_blocks, hidden_blocks),
    ]
    rows = 4 * attn_blocks + 2 * hidden_blocks
    bias_rows = hidden_blocks
    token_rows = len(token_sums) * model // 128

    def square(count):
        return jax.ShapeDtypeStruct((count, 128), F32)

    operands = (*grads, *token_sums, *bias_sums)
    across, along = call(
        functools.partial(sums_kernel, cuts, len(grads), len(token_sums)),
        (1,),
        [whole(a) for a in operands],
        [whole((8 + token_rows, 128)), whole((rows + bias_rows, 128))],
        [square(8 + token_rows), square(rows + bias_rows)],
        operands,
    )
    across = butterfly(across, "mp", mp_size)
    count = rows + bias_rows + token_rows + 8
    sums = call(
        functools.partial(join_kernel, len(cuts)),
        (1,),
        [whole(across), whole(along)],
        whole((count, 128)),
        square(count),
        (across, along),
    )
    sums = butterfly(sums, "dp", dp_size)
    wide = [attn * mp_size] * 4 + [hidden * mp_size] * 2
    operands = (*grads, across, sums, *weights)
    outs = [jax.ShapeDtypeStruct(w.shape, F32) for w in weights]
    outs += [jax.ShapeDtypeStruct((3, shard), F32), jax.ShapeDtypeStruct((3, attn), F32)]
    outs += [square(1)] * 3 + [square(attn_blocks), square(hidden_blocks), square(hidden_blocks)]
    outs += [square(bias_rows)] + [square(model // 128)] * len(token_sums)
    new_qkv, new_out, new_up, new_down, qkv_rows, qkv_cols, *rest = call(
        functools.partial(step_kernel, cuts, len(grads), model, wide),
        (1,),
        [whole(a) for a in operands],
        [whole(o.shape) for o in outs],
        outs,
        operands,
    )
    rest = [r.reshape(-1) for r in rest]
    return (
        (new_qkv, qkv_rows, qkv_cols),
        (new_out, rest[3], rest[0]),
        (new_up, rest[1], rest[4]),
        (new_down, rest[5], rest[2]),
        rest[7:],
        rest[6],
    )


def step_plain(dp_size, mp_size, attn_grads, ffn_grads, weights, token_sums, bias_sums, groups):
    w_qkv, w_out, w_up, w_down = weights
    shard, attn = w_qkv.shape[1:]
    hidden = w_up.shape[1]
    model = shard * dp_size
    width = attn // groups
    qkv = jnp.stack([g[:, : 3 * width].reshape(shard, 3, width) for g in attn_grads], axis=1)
    shards = [qkv[:, :, n].reshape(shard, attn) for n in range(3)] + [
        attn_grads[0][:, 3 * width :],
        ffn_grads[:, :hidden].astype(F32),
        ffn_grads[:, hidden:].astype(F32),
    ]
    squares = [g * g for g in shards]
    across = butterfly(
        jnp.concatenate(
            [jnp.sum(s, axis=1) for s in squares] + [jnp.sum(t, axis=0) for t in token_sums]
        ),
        "mp",
        mp_size,
    )
    model_sums = [across[n * shard : (n + 1) * shard] for n in range(6)]
    totals = jnp.stack([jnp.sum(s) for s in model_sums])
    sums = butterfly(
        jnp.concatenate(
            [jnp.sum(s, axis=0) for s in squares]
            + [across[6 * shard :], jnp.sum(sum(bias_sums), axis=0), totals]
        ),
        "dp",
        dp_size,
    )
    cuts = []
    start = 0
    for length in [attn] * 4 + [hidden] * 2 + [model] * len(token_sums) + [hidden, 6]:
        cuts.append(sums[start : start + length])
        start += length
    steps = []
    for n in range(6):
        wide = (attn if n < 4 else hidden) * mp_size
        whole_mean = cuts[-1][n] / (model * wide) + EPS_FACTOR
        model_factor = (model_sums[n] / wide + EPS_FACTOR) / whole_mean
        other_factor = (cuts[n] / model + EPS_FACTOR) / whole_mean
        update = shards[n] * lax.rsqrt(model_factor[:, None] * other_factor[None, :] * whole_mean)
        steps.append((LEARN_RATE * update, model_factor, other_factor))
    return (
        (
            w_qkv - jnp.stack([steps[n][0] for n in range(3)]),
            jnp.stack([steps[n][1] for n in range(3)]),
            jnp.stack([steps[n][2] for n in range(3)]),
        ),
        (w_out - steps[3][0].T, steps[3][2], steps[3][1]),
        (w_up - steps[4][0], steps[4][1], steps[4][2]),
        (w_down - steps[5][0].T, steps[5][2], steps[5][1]),
        cuts[6 : 6 + len(token_sums)],
        cuts[-2],
    )


def results(out_tokens, grad_tokens, step):
    qkv, out, up, down, token_sums, bias_sum = step
    return (
        out_tokens[None],
        grad_tokens[None],
        *qkv,
        *out,
        *up,
        *down,
        *token_sums[:4],
        bias_sum,
        token_sums[4],
    )


def body(
    dp_size,
    mp_size,
    tokens,
    cotangent,
    w_qkv,
    w_out,
    w_up,
    w_down,
    gain_attn,
    shift_attn,
    gain_ffn,
    shift_ffn,
    bias_up,
    bias_down,
    random_blocks,
):
    weights = (w_qkv, w_out, w_up, w_down)
    own_tokens, grad_top = tokens[0], cotangent[0]
    random_rows = random_blocks[0].reshape(random_blocks.shape[1], -1)
    index = lax.axis_index("mp").astype(jnp.int32).reshape(1)
    shard, attn = w_qkv.shape[1:]
    own_rows, model = own_tokens.shape
    width = min(128, attn)
    groups = attn // width
    low_attn, low_ffn = pack(weights, groups, width)
    if mp_size == 4 and dp_size == 8 and width == 128:
        arrange = paired_layer
    else:
        arrange = plain_layer
    out_tokens, grad_tokens, attn_grads, ffn_grads, token_sums, bias_sums = arrange(
        dp_size,
        mp_size,
        own_tokens,
        grad_top,
        random_rows,
        index,
        low_attn,
        low_ffn,
        (gain_attn, shift_attn, gain_ffn, shift_ffn),
        bias_up,
        bias_down,
        groups,
        width,
    )
    aligned = width == 128 and shard == 128 and w_up.shape[1] % 128 == 0
    step = (step_tail if aligned else step_plain)(
        dp_size, mp_size, attn_grads, ffn_grads, weights, token_sums, bias_sums, groups
    )
    return results(out_tokens, grad_tokens, step)


def paired_layer(
    dp_size,
    mp_size,
    tokens,
    grad_top,
    random_rows,
    index,
    low_attn,
    low_ffn,
    norms,
    bias_up,
    bias_down,
    groups,
    width,
):
    gain_attn, shift_attn, gain_ffn, shift_ffn = norms
    rows, model = tokens.shape
    attn = groups * width
    mine = lax.axis_index("dp")
    index_rows = gain_attn.reshape(8, -1)

    def other_core(value):
        return swap(value, 1, mp_size)

    def other_chip(value):
        return swap(value, 2, mp_size)

    places = [(mine + 2 * n) % dp_size for n in (0, 1, 3, 2)]
    places += [p ^ 1 for p in places]

    def levels_of(low):
        above = shifted(low, -2, dp_size)
        below = shifted(low, 2, dp_size)
        return [low, above, below, shifted(above, -2, dp_size)]

    def between_x(value):
        return swap(value, 1, dp_size, "dp")

    def fence(value, *others):
        return after(value, other_core(after(index_rows, *others)))

    normed = norm_call(tokens, gain_attn, shift_attn)
    normed = norm_call(tokens, gain_attn, shift_attn)
    normed_near = other_core(normed)
    far = other_chip(normed)
    attn_levels = levels_of(after(low_attn, normed))
    attn_swapped = [between_x(level) for level in attn_levels[:3]]
    attn_swapped.append(between_x(after(attn_levels[3], far)))
    ffn_low = lax.all_gather(
        after(low_ffn, far, *attn_levels[1:], *attn_swapped[:2]), "dp", axis=0, tiled=True
    )

    normed_pieces = [normed, normed_near, far, other_core(far)]
    top_far = other_chip(after(grad_top, far))
    top_near = other_core(grad_top)
    early = assemble(
        attn_levels[:3] + attn_swapped[:3], places[:3] + places[4:7], dp_size
    )
    attn_low = assemble(
        [attn_levels[3], after(attn_swapped[3], early)], [places[3], places[7]], dp_size, early
    )
    project = qkv_call(normed_pieces, after(attn_low, random_rows), 3 * attn)
    out_own = attn_low[:, 3 * attn :]
    out_far = other_chip(after(out_own, far))

    heads_out, heads_got = [], []
    for group in range(groups):
        if group == groups - 1:
            project = after(project, top_far)
        heads_out.append(
            attention_call(
                forward_kernel, 15, project, group, groups, (), random_rows, index, mp_size
            )
        )
        heads_got.append(other_chip(heads_out[-1][2 * rows :]))
    own, other = branch_call(
        tokens, heads_out, heads_got, attn_low, out_far
    )
    middle, second = residual_norm_call(own, other_core(other), gain_ffn, shift_ffn)

    second_far = other_chip(second)
    second_near = other_core(second)
    both_near, bias_near, back_own, back_near = ffn_call(
        [second, second_near], [grad_top, top_near], ffn_low, bias_up
    )
    second_far = after(second_far, back_own)
    second_last = other_core(second_far)
    top_last = other_core(top_far)
    both_far, bias_far, back_far, back_last = ffn_call(
        [second_far, second_last], [top_far, top_last], ffn_low, bias_up
    )
    crossing = (back_far.astype(F32) + other_core(back_last).astype(F32)).astype(BF16)
    crossed = other_chip(crossing)
    back_got = other_core(back_near)
    ffn_grads = double_outer_sum(
        [after(second, crossing), second_near, second_far, second_last],
        [grad_top, top_near, top_far, top_last],
        [(both_near, 0), (both_near, 1), (both_far, 0), (both_far, 1)],
    )
    down_far, down_last = down_call(after(both_far, ffn_grads), ffn_low, 2)
    crossed = after(crossed, ffn_grads, down_far)
    ffn_shard = lax.psum_scatter(
        after(ffn_grads, crossed), "dp", scatter_dimension=0, tiled=True
    )
    grad_middle, gain_two, shift_two, top_sum, grad_branch = norm_back_call(
        middle, grad_top, gain_ffn, [back_own, back_got, crossed], True
    )

    branch_pieces = [grad_branch, other_core(grad_branch)]
    away = head_grads_call(branch_pieces, out_far, 0, attn, groups)
    came = [other_chip(a) for a in away]
    stay = list(head_grads_call(branch_pieces, out_own, 0, attn, groups))
    out_away = other_chip(
        outer_sum([after(grad_branch, *away, *stay), branch_pieces[1]], heads_got)
    )
    out_stay = outer_sum(branch_pieces, [h[: 2 * rows] for h in heads_out])
    down_crossing = (
        down_far.astype(F32) + other_core(after(down_last, *away)).astype(F32)
    ).astype(BF16)
    down_crossed = other_chip(after(down_crossing, came[0]))

    grad_projects = []
    project = after(project, down_crossing, out_stay)
    for group in range(groups):
        grad_projects.append(
            attention_call(
                backward_kernel,
                10,
                project,
                group,
                groups,
                (stay[group], came[group]),
                random_rows,
                index,
                mp_size,
            )
        )
        if group == 0:
            first_sum = outer_sum(normed_pieces, grad_projects[:1], (out_stay, out_away))
            kept, sent = scatter_model_split(first_sum, dp_size)
            project, kept, sent = lax.optimization_barrier((project, kept, sent))
            sums = [(kept, between_x(sent))]
    grad_projects[-1] = after(grad_projects[-1], sums[0][1], down_crossed)

    [back_far] = back_project(grad_projects, attn_low, 2, 1, rows)
    came_far = other_core(back_far)
    [back_last] = back_project(
        [after(grad_projects[0], back_far)] + grad_projects[1:], attn_low, 3, 1, rows
    )
    crossing = (back_last.astype(F32) + came_far.astype(F32)).astype(BF16)
    crossed = other_chip(crossing)
    late = [after(g, crossing) for g in grad_projects]
    attn_parts = [scatter_model_end(after(sums[0][0], crossing), sums[0][1], dp_size)]
    for group in range(1, groups):
        kept, sent = scatter_model_split(
            outer_sum(normed_pieces, late[group : group + 1]), dp_size
        )
        attn_parts.append(scatter_model_end(kept, between_x(sent), dp_size))
        late = [after(g, sent) for g in late]
    back_own, back_near = back_project(late, attn_low, 0, 2, rows)
    back_got = other_core(back_near)
    down_own, down_near = down_call(after(both_near, back_own), ffn_low, 2)
    crossed = other_core(after(crossed, *(p for parts in attn_parts for p in parts)))
    out_tokens = (
        middle
        + down_own.astype(F32)
        + other_core(down_near).astype(F32)
        + down_crossed.astype(F32)
        + bias_down
    ).astype(BF16)
    grad_tokens, gain_one, shift_one = norm_back_call(
        tokens, grad_middle, gain_attn, [back_own, back_got, after(crossed, out_tokens)]
    )
    attn_grads = [sum(p.astype(F32) for p in parts) for parts in attn_parts]
    token_sums = [gain_one, shift_one, gain_two, shift_two, top_sum]
    return out_tokens, grad_tokens, attn_grads, ffn_shard, token_sums, [bias_near, bias_far]


def plain_layer(
    dp_size,
    mp_size,
    tokens,
    grad_top,
    random_rows,
    index,
    low_attn,
    low_ffn,
    norms,
    bias_up,
    bias_down,
    groups,
    width,
):
    gain_attn, shift_attn, gain_ffn, shift_ffn = norms
    rows, model = tokens.shape
    attn = groups * width
    lines = [[core + 2 * n for n in range(mp_size // 2)] for core in range(2)]
    core = lax.axis_index("mp") % 2

    def gather(value, axis, along=0):
        return lax.all_gather(value, axis, axis=along, tiled=True)

    def other_core(value):
        return swap(value, 1, mp_size)

    def scattered(value):
        return lax.psum_scatter(value, "mp", scatter_dimension=0, tiled=True)

    def own_first(value):
        half = value.shape[0] // 2
        return jnp.where(core == 0, value, jnp.roll(value, half, axis=0))

    attn_low = gather(low_attn, "dp")
    ffn_low = gather(low_ffn, "dp")
    normed = gather(norm_call(tokens, gain_attn, shift_attn), "mp")
    top_full = gather(grad_top, "mp")
    project = qkv_call([normed], attn_low[:, : 3 * attn], 3 * attn)
    out_low = lax.all_gather(
        attn_low[:, 3 * attn :], "mp", axis=1, axis_index_groups=lines, tiled=True
    )
    heads_out = [
        attention_call(forward_kernel, 15, project, g, groups, (), random_rows, index, 1)
        for g in range(groups)
    ]
    moved = own_first(
        lax.all_to_all(
            jnp.concatenate(heads_out, axis=1), "mp", 0, 1, axis_index_groups=lines, tiled=True
        )
    )
    branch = dot(moved, out_low, NT)
    middle, second = residual_norm_call(
        tokens.astype(F32) + branch[:rows],
        other_core(branch[rows:].astype(BF16)),
        gain_ffn,
        shift_ffn,
    )
    second_full = gather(second, "mp")
    both, bias_sum, back = ffn_call([second_full], [top_full], ffn_low, bias_up)
    ffn_grads = double_outer_sum([second_full], [top_full], [(both, 0)])
    ffn_shard = lax.psum_scatter(ffn_grads, "dp", scatter_dimension=0, tiled=True)
    grad_middle, gain_two, shift_two, top_sum, grad_branch = norm_back_call(
        middle, grad_top, gain_ffn, [scattered(back)], True
    )
    branch_pair = jnp.concatenate([grad_branch, other_core(grad_branch)], axis=0)
    away = own_first(dot(branch_pair, out_low, NN).astype(BF16))
    away = lax.all_to_all(away, "mp", 1, 0, axis_index_groups=lines, tiled=True)
    out_grad = lax.psum_scatter(
        dot(branch_pair, moved, TN).astype(BF16),
        "mp",
        scatter_dimension=1,
        axis_index_groups=lines,
        tiled=True,
    )
    grad_projects = [
        attention_call(
            backward_kernel,
            6,
            project,
            g,
            groups,
            (away[:, g * width : (g + 1) * width],),
            random_rows,
            index,
            1,
        )
        for g in range(groups)
    ]
    attn_grads = [
        scatter_model(
            outer_sum([normed], [g], (out_grad,) if n == 0 else ()), dp_size
        )
        for n, g in enumerate(grad_projects)
    ]
    back = sum(
        dot(g, attn_low[:, 3 * n * width : 3 * (n + 1) * width], NT)
        for n, g in enumerate(grad_projects)
    )
    grad_tokens, gain_one, shift_one = norm_back_call(
        tokens, grad_middle, gain_attn, [scattered(back.astype(BF16))]
    )
    down = scattered(down_call(both, ffn_low, 1)[0])
    out_tokens = (middle + down.astype(F32) + bias_down).astype(BF16)
    token_sums = [gain_one, shift_one, gain_two, shift_two, top_sum]
    return out_tokens, grad_tokens, attn_grads, ffn_shard, token_sums, [bias_sum]


def solution(mesh):
    placed = (
        P("dp", "mp", None),
        P("dp", "mp", None),
        P(None, "dp", "mp"),
        P("mp", "dp"),
        P("dp", "mp"),
        P("mp", "dp"),
        P(),
        P(),
        P(),
        P(),
        P("mp"),
        P(),
        P("dp", "mp", None, None),
    )
    return jax.shard_map(
        functools.partial(body, mesh.shape["dp"], mesh.shape["mp"]),
        mesh=mesh,
        in_specs=placed,
        out_specs=(
            P("dp", "mp", None),
            P("dp", "mp", None),
            P(None, "dp", "mp"),
            P(None, "dp"),
            P(None, "mp"),
            P("mp", "dp"),
            P("mp"),
            P("dp"),
            P("dp", "mp"),
            P("dp"),
            P("mp"),
            P("mp", "dp"),
            P("mp"),
            P("dp"),
            P(),
            P(),
            P(),
            P(),
            P("mp"),
            P(),
        ),
        check_vma=False,
    )
```
